32 devices in a mesh: dp: 16 (over z, x, core), tensor: 2 (over y).
Axes of the slice: x: 2, y: 2, z: 4, core: 2. Of those that a mesh axis runs over, the one named last changes fastest.
Arguments:
- hidden: bfloat16 [2048, 4096], P('dp', 'tensor'), may hold values from -6 to 6
- gain: bfloat16 [4096], P('tensor'), may hold values from 0.5 to 1.5
- w_query: bfloat16 [4096, 4096], P('dp', 'tensor'), may hold values from -0.09375 to 0.09375
- w_key: bfloat16 [4096, 1024], P('dp', 'tensor'), may hold values from -0.09375 to 0.09375
- w_value: bfloat16 [4096, 1024], P('dp', 'tensor'), may hold values from -0.09375 to 0.09375
- cotangent: bfloat16 [4096, 4096], P('dp', 'tensor'), may hold values from -6 to 6
- seq_length: int32 [16, 4], replicated, may hold values from 16 to 64, as said below
- home_offset: int32 [16, 4], replicated, may hold values from 0 to 112, as said below
- dest_shard: int32 [16, 4], replicated, may hold values from 0 to 15, as said below
- dest_offset: int32 [16, 4], replicated, may hold values from 0 to 192, as said below
Outputs:
- attention_output: bfloat16 [4096, 4096], P('dp', 'tensor')
- grad_hidden: bfloat16 [2048, 4096], P('dp', 'tensor')
- grad_value_weight: float32 [4096, 1024], P('dp', 'tensor')
The draws below stay inside these ranges and needn't reach their ends.
Inputs may be any that keep to these rules, and one draw needn't show every extreme that they name: `seq_length`: the 4 sequences of a shard fill its 128 rows exactly; every length is at least 16 and at most 64, and some sequence has length 64. `home_offset`: the sequences of a shard lie back to back from row 0 in the order of c. `dest_shard`: sequence c of shard h goes to shard (h + e) mod 16, e one of -1, 1, 8 and 9; every shard sends exactly one sequence to each of these 4 shards. `dest_offset`: the sequences that arrive at a shard lie back to back from row 0 of its 256 rows, in the order e = -1, 1, 8, 9; at some shard they fill all 256 rows.
All inputs are finite; a program needn't handle non-finite values.
Results may differ from the reference program's by a relative error of at most 0.02.
Values may be sent and summed in bfloat16 or wider, within the bound.
A program may use at most 128 MiB of HBM per device.

```python
import jax
import jax.numpy as jnp
from jax import lax

D = 4096
HEADS = 32
KV_HEADS = 8
HEAD = 128
TOK_DEV = 128
SEQS = 4
CAP = 256
TOKENS = 2048
DEST_ROWS = 4096
N_DP = 16
N_TENSOR = 2


def shuffle_four(subkey):
    return jax.random.permutation(subkey, 4).astype(jnp.int32)


def plan_arrays(key):
    shard_count = N_DP
    shortest = TOK_DEV // 8
    stride_values = [-1, 1, N_DP // 2, N_DP // 2 + 1]
    subkeys = jax.random.split(key, 7)
    len_one = jax.random.randint(subkeys[0], (shard_count,), shortest, 3 * shortest + 1)
    len_two = jax.random.randint(subkeys[1], (shard_count,), shortest, 3 * shortest + 1)
    remainder = TOK_DEV - len_one - len_two
    len_three = jax.random.randint(subkeys[2], (shard_count,), jnp.maximum(shortest, remainder - 4 * shortest), jnp.minimum(4 * shortest, remainder - shortest) + 1)
    len_four = remainder - len_three
    lengths = jnp.stack([len_one, len_two, len_three, len_four], 1).astype(jnp.int32)
    center = jax.random.randint(subkeys[3], (), 0, shard_count)
    stride_array = jnp.array(stride_values, jnp.int32)
    forced_home = (center - stride_array + shard_count) % shard_count
    home_index = jnp.arange(shard_count, dtype=jnp.int32)
    hits = (home_index[:, None] == forced_home[None, :]).astype(jnp.int32)
    forced = jnp.sum(hits, 1) > 0
    forced_slot = jnp.sum(hits * jnp.arange(4, dtype=jnp.int32)[None, :], 1)
    part_one = jax.random.randint(subkeys[4], (shard_count,), shortest, 2 * shortest + 1)
    part_two = jax.random.randint(subkeys[5], (shard_count,), shortest, 3 * shortest - part_one + 1)
    part_three = 4 * shortest - part_one - part_two
    forced_lengths = jnp.stack([jnp.full((shard_count,), 4 * shortest, jnp.int32), part_one, part_two, part_three], 1).astype(jnp.int32)
    lengths = jnp.where(forced[:, None], forced_lengths, lengths)
    orders = jax.vmap(shuffle_four)(jax.random.split(subkeys[6], shard_count))
    column = jnp.arange(4, dtype=jnp.int32)[None, :]
    swapped = jnp.where(orders == forced_slot[:, None], orders[:, :1], jnp.where(column == 0, forced_slot[:, None], orders))
    orders = jnp.where(forced[:, None], swapped, orders).astype(jnp.int32)
    moves_of = stride_array[orders]
    targets = (home_index[:, None] + moves_of + shard_count) % shard_count
    by_slot = [jnp.sum(lengths * (orders == number), 1) for number in range(4)]
    incoming = jnp.stack([jnp.roll(by_slot[number], stride_values[number]) for number in range(4)], 1)
    starts = jnp.cumsum(incoming, 1) - incoming
    start_home = jnp.stack([jnp.roll(starts[:, number], -stride_values[number]) for number in range(4)], 1)
    dest_off = jnp.sum(jnp.stack([(orders == number) * start_home[:, number:number + 1] for number in range(4)], 0), 0)
    home_off = jnp.cumsum(lengths, 1) - lengths
    return (lengths.astype(jnp.int32), home_off.astype(jnp.int32), targets.astype(jnp.int32), dest_off.astype(jnp.int32))


def draw_seq_length(key, part):
    shared = plan_arrays(key)
    return shared[0]


def draw_home_offset(key, part):
    shared = plan_arrays(key)
    return shared[1]


def draw_dest_shard(key, part):
    shared = plan_arrays(key)
    return shared[2]


def draw_dest_offset(key, part):
    shared = plan_arrays(key)
    return shared[3]


def steps_of(own_key, dims, shards, smallest, largest):
    def one(dim, blocks):
        draws = jax.random.uniform(jax.random.fold_in(jax.random.fold_in(own_key, 6), dim), (blocks,), jnp.float32, smallest / len(shards), largest / len(shards))
        return jnp.repeat(jnp.exp(draws), dims[dim] // blocks).reshape((-1,) + (1,) * (len(dims) - dim - 1))

    loudness = one(*shards[0])
    for cut in shards[1:]:
        loudness = loudness * one(*cut)
    return loudness


def gaussian(stream_key, dims, spread, most, cuts=(), kind=jnp.bfloat16):
    entries = jax.random.normal(stream_key, dims, jnp.float32) * spread
    if len(cuts) > 0:
        entries = steps_of(stream_key, dims, cuts, -0.22, 0.18) * entries
    return jnp.clip(entries, min=-most, max=most).astype(kind)


def setup_inputs(seed: int = 0) -> dict:
    streams_of = jax.random.split(jax.random.key(seed), 11)
    hidden = gaussian(streams_of[0], (TOKENS, D), 1.0, 6.0, ((0, 16), (1, 2)))
    gain = jnp.clip(1.0 + 0.1 * jax.random.normal(streams_of[1], (D,), jnp.float32), 0.5, 1.5).astype(jnp.bfloat16)
    w_query = gaussian(streams_of[2], (D, HEADS * HEAD), D ** -0.5, 0.09375, ((0, 16), (1, 2)))
    w_key = gaussian(streams_of[3], (D, KV_HEADS * HEAD), D ** -0.5, 0.09375, ((0, 16), (1, 2)))
    w_value = gaussian(streams_of[4], (D, KV_HEADS * HEAD), D ** -0.5, 0.09375, ((0, 16), (1, 2)))
    cotangent = gaussian(streams_of[5], (DEST_ROWS, HEADS * HEAD), 1.0, 6.0, ((0, 16), (1, 2)))
    seq_length = draw_seq_length(jax.random.fold_in(streams_of[10], 71), 0)
    home_offset = draw_home_offset(jax.random.fold_in(streams_of[10], 71), 0)
    dest_shard = draw_dest_shard(jax.random.fold_in(streams_of[10], 71), 0)
    dest_offset = draw_dest_offset(jax.random.fold_in(streams_of[10], 71), 0)
    return {"hidden": hidden, "gain": gain, "w_query": w_query, "w_key": w_key, "w_value": w_value, "cotangent": cotangent, "seq_length": seq_length, "home_offset": home_offset, "dest_shard": dest_shard, "dest_offset": dest_offset}


EPSILON = 1e-05
ROPE_BASE = 500000.0

def rope_tables(position):
    half_head = HEAD // 2
    exponent = jnp.arange(half_head, dtype=jnp.float32) * (2.0 / HEAD)
    inverse = jnp.power(jnp.float32(ROPE_BASE), -exponent)
    angles = position.astype(jnp.float32)[:, None] * inverse[None, :]
    return (jnp.cos(angles)[:, None, :], jnp.sin(angles)[:, None, :])

def rotate(values, cosine, sine_part):
    half_head = values.shape[-1] // 2
    lower_half = values[..., :half_head]
    upper_half = values[..., half_head:]
    return jnp.concatenate([lower_half * cosine - upper_half * sine_part, upper_half * cosine + lower_half * sine_part], -1)

def unrotate(values, cosine, sine_part):
    half_head = values.shape[-1] // 2
    lower_half = values[..., :half_head]
    upper_half = values[..., half_head:]
    return jnp.concatenate([lower_half * cosine + upper_half * sine_part, upper_half * cosine - lower_half * sine_part], -1)

def attention_block(normed, w_query, w_key, w_value, cotangent, segment, position, occupied):
    row_count = normed.shape[0]
    kv_heads = w_key.shape[1] // HEAD
    q_heads = w_query.shape[1] // HEAD
    group_size = q_heads // kv_heads
    cosine, sine_part = rope_tables(position)
    query_rows = jnp.dot(normed, w_query, preferred_element_type=jnp.float32).reshape(row_count, q_heads, HEAD)
    key_rows = jnp.dot(normed, w_key, preferred_element_type=jnp.float32).reshape(row_count, kv_heads, HEAD)
    value_rows = jnp.dot(normed, w_value, preferred_element_type=jnp.float32).astype(jnp.bfloat16).reshape(row_count, kv_heads, HEAD)
    query_rows = rotate(query_rows, cosine, sine_part).astype(jnp.bfloat16).reshape(row_count, kv_heads, group_size, HEAD)
    key_rows = rotate(key_rows, cosine, sine_part).astype(jnp.bfloat16)
    factor = HEAD ** (-0.5)
    scores = jnp.einsum('qhgd,khd->hgqk', query_rows.astype(jnp.float32), key_rows.astype(jnp.float32)) * factor
    allowed = (segment[:, None] == segment[None, :]) & (position[None, :] <= position[:, None])
    scores = jnp.where(allowed[None, None], scores, jnp.float32(-1e+30))
    row_max = lax.optimization_barrier(jnp.max(scores, -1, keepdims=True))
    exp_terms = jnp.exp(scores - row_max)
    attn_prob = exp_terms / lax.optimization_barrier(jnp.sum(exp_terms, -1, keepdims=True))
    prob_low = attn_prob.astype(jnp.bfloat16)
    mixed_rows = jnp.einsum('hgqk,khd->qhgd', prob_low.astype(jnp.float32), value_rows.astype(jnp.float32))
    attn_out = jnp.where(occupied[:, None], mixed_rows.reshape(row_count, q_heads * HEAD), jnp.float32(0.0)).astype(jnp.bfloat16)
    grad_out = jnp.where(occupied[:, None], cotangent, jnp.zeros((), jnp.bfloat16)).reshape(row_count, kv_heads, group_size, HEAD)
    grad_value = jnp.einsum('hgqk,qhgd->khd', prob_low.astype(jnp.float32), grad_out.astype(jnp.float32)).astype(jnp.bfloat16)
    grad_probs = jnp.einsum('qhgd,khd->hgqk', grad_out.astype(jnp.float32), value_rows.astype(jnp.float32))
    centre = lax.optimization_barrier(jnp.sum(grad_probs * attn_prob, -1, keepdims=True))
    grad_scores = (attn_prob * (grad_probs - centre) * factor).astype(jnp.bfloat16)
    grad_query = jnp.einsum('hgqk,khd->qhgd', grad_scores.astype(jnp.float32), key_rows.astype(jnp.float32)).reshape(row_count, q_heads, HEAD)
    grad_key = jnp.einsum('hgqk,qhgd->khd', grad_scores.astype(jnp.float32), query_rows.astype(jnp.float32))
    grad_query = unrotate(grad_query, cosine, sine_part).astype(jnp.bfloat16).reshape(row_count, q_heads * HEAD)
    grad_key = unrotate(grad_key, cosine, sine_part).astype(jnp.bfloat16).reshape(row_count, kv_heads * HEAD)
    return (attn_out, grad_query, grad_key, grad_value.reshape(row_count, kv_heads * HEAD))

def group_product(grads, weights):
    return jnp.einsum('rpc,dpc->prd', grads.reshape(CAP, N_TENSOR, -1).astype(jnp.float32), weights.reshape(D, N_TENSOR, -1).astype(jnp.float32))

def reference(hidden, gain, w_query, w_key, w_value, cotangent, seq_length, home_offset, dest_shard, dest_offset):
    within = jnp.arange(TOK_DEV, dtype=jnp.int32)
    lower_bound = home_offset[:, None, :]
    upper_bound = (home_offset + seq_length)[:, None, :]
    member = ((within[None, :, None] >= lower_bound) & (within[None, :, None] < upper_bound)).astype(jnp.int32)
    start_home = lax.optimization_barrier(jnp.sum(member * lower_bound, -1))
    start_dest = lax.optimization_barrier(jnp.sum(member * (dest_shard * CAP + dest_offset)[:, None, :], -1))
    seq_index = jnp.arange(N_DP * SEQS, dtype=jnp.int32).reshape(N_DP, SEQS)
    seq_of_row = lax.optimization_barrier(jnp.sum(member * seq_index[:, None, :], -1)).reshape(-1)
    position_home = (within[None, :] - start_home).reshape(-1)
    target = (start_dest + within[None, :] - start_home).reshape(-1)
    dest_total = N_DP * CAP
    placed = jnp.zeros((dest_total, D), jnp.bfloat16).at[target].set(hidden)
    segment = jnp.full((dest_total,), -1, jnp.int32).at[target].set(seq_of_row)
    position = jnp.zeros((dest_total,), jnp.int32).at[target].set(position_home)
    gain_wide = gain.astype(jnp.float32)

    def one_shard(carry, shard):
        start = shard * CAP
        dest_rows = lax.dynamic_slice_in_dim(placed, start, CAP, 0)
        seg_rows = lax.dynamic_slice_in_dim(segment, start, CAP, 0)
        pos_rows = lax.dynamic_slice_in_dim(position, start, CAP, 0)
        cot_rows = lax.dynamic_slice_in_dim(cotangent, start, CAP, 0)
        occupied = seg_rows >= 0
        values = dest_rows.astype(jnp.float32)
        inverse_rms = lax.rsqrt(lax.optimization_barrier(jnp.mean(values * values, 1, keepdims=True)) + EPSILON)
        normed = (values * inverse_rms * gain_wide).astype(jnp.bfloat16)
        attn_out, grad_query, grad_key, grad_value = attention_block(normed, w_query, w_key, w_value, cot_rows, seg_rows, pos_rows, occupied)
        group_terms = group_product(grad_query, w_query) + group_product(grad_key, w_key) + group_product(grad_value, w_value)
        summed = lax.optimization_barrier(jnp.sum(lax.optimization_barrier(group_terms.astype(jnp.bfloat16)).astype(jnp.float32), 0))
        weighted = summed * gain_wide
        row_dot = lax.optimization_barrier(jnp.sum(weighted * values, 1, keepdims=True))
        grad_rows = (inverse_rms * weighted - values * inverse_rms ** 3 * row_dot / D).astype(jnp.bfloat16)
        grad_weight = carry + jnp.einsum('rd,rc->dc', normed.astype(jnp.float32), grad_value.astype(jnp.float32))
        return (grad_weight, (attn_out, grad_rows))
    grad_weight, (attn_all, grad_all) = lax.scan(one_shard, jnp.zeros((D, KV_HEADS * HEAD), jnp.float32), jnp.arange(N_DP, dtype=jnp.int32))
    attention_output = attn_all.reshape(dest_total, HEADS * HEAD)
    grad_hidden = grad_all.reshape(dest_total, D)[target]
    return (attention_output, grad_hidden, grad_weight)
```

```python
import jax
import jax.numpy as jnp
from jax import lax
from jax.sharding import PartitionSpec as P

D = 4096
HEAD = 128
TOK_DEV = 128
MAXLEN = 64
CAP = 256


EPSILON = 1e-05
ROPE_BASE = 500000.0


def passed_along(value, axis, by):
    size = lax.axis_size(axis)
    return lax.ppermute(value, axis, [(i, (i + by) % size) for i in range(size)])


def rope_tables(position):
    half_head = HEAD // 2
    exponent = jnp.arange(half_head, dtype=jnp.float32) * (2.0 / HEAD)
    inverse = jnp.power(jnp.float32(ROPE_BASE), -exponent)
    angles = position.astype(jnp.float32)[:, None] * inverse[None, :]
    return (jnp.cos(angles)[:, None, :], jnp.sin(angles)[:, None, :])


def rotate(values, cosine, sine_part):
    half_head = values.shape[-1] // 2
    lower_half = values[..., :half_head]
    upper_half = values[..., half_head:]
    return jnp.concatenate(
        [
            lower_half * cosine - upper_half * sine_part,
            upper_half * cosine + lower_half * sine_part,
        ],
        -1,
    )


def attention_block(normed, w_query, w_key, w_value, cotangent, segment, position):
    row_count = normed.shape[0]
    kv_heads = w_key.shape[1] // HEAD
    q_heads = w_query.shape[1] // HEAD
    group_size = q_heads // kv_heads
    cosine, sine_part = rope_tables(position)
    query_rows = jnp.dot(normed, w_query, preferred_element_type=jnp.float32).reshape(
        row_count, q_heads, HEAD
    )
    key_rows = jnp.dot(normed, w_key, preferred_element_type=jnp.float32).reshape(
        row_count, kv_heads, HEAD
    )
    value_rows = (
        jnp.dot(normed, w_value, preferred_element_type=jnp.float32)
        .astype(jnp.bfloat16)
        .reshape(row_count, kv_heads, HEAD)
    )
    query_rows = (
        rotate(query_rows, cosine, sine_part)
        .astype(jnp.bfloat16)
        .reshape(row_count, kv_heads, group_size, HEAD)
    )
    key_rows = rotate(key_rows, cosine, sine_part).astype(jnp.bfloat16)
    factor = HEAD ** (-0.5)
    scores = (
        jnp.einsum("qhgd,khd->hgqk", query_rows, key_rows, preferred_element_type=jnp.float32)
        * factor
    )
    allowed = (segment[:, None] == segment[None, :]) & (position[None, :] <= position[:, None])
    scores = jnp.where(allowed[None, None], scores, jnp.float32(-1e30))
    row_max = jnp.max(scores, -1, keepdims=True)
    exp_terms = jnp.exp(scores - row_max)
    attn_prob = exp_terms / jnp.sum(exp_terms, -1, keepdims=True)
    prob_low = attn_prob.astype(jnp.bfloat16)
    attn_out = (
        jnp.einsum("hgqk,khd->qhgd", prob_low, value_rows, preferred_element_type=jnp.float32)
        .reshape(row_count, q_heads * HEAD)
        .astype(jnp.bfloat16)
    )
    grad_out = cotangent.reshape(row_count, kv_heads, group_size, HEAD)
    grad_value = jnp.einsum(
        "hgqk,qhgd->khd", prob_low, grad_out, preferred_element_type=jnp.float32
    ).astype(jnp.bfloat16)
    grad_probs = jnp.einsum(
        "qhgd,khd->hgqk", grad_out, value_rows, preferred_element_type=jnp.float32
    )
    centre = jnp.sum(grad_probs * attn_prob, -1, keepdims=True)
    grad_scores = (attn_prob * (grad_probs - centre) * factor).astype(jnp.bfloat16)
    grad_query = jnp.einsum(
        "hgqk,khd->qhgd", grad_scores, key_rows, preferred_element_type=jnp.float32
    ).reshape(row_count, q_heads, HEAD)
    grad_key = jnp.einsum(
        "hgqk,qhgd->khd", grad_scores, query_rows, preferred_element_type=jnp.float32
    )
    grad_query = (
        rotate(grad_query, cosine, -sine_part)
        .astype(jnp.bfloat16)
        .reshape(row_count, q_heads * HEAD)
    )
    grad_key = (
        rotate(grad_key, cosine, -sine_part)
        .astype(jnp.bfloat16)
        .reshape(row_count, kv_heads * HEAD)
    )
    return (attn_out, grad_query, grad_key, grad_value.reshape(row_count, kv_heads * HEAD))


def pick_rows(selection, matrix):
    return jnp.dot(
        selection.astype(jnp.bfloat16), matrix, preferred_element_type=jnp.float32
    ).astype(jnp.bfloat16)


def on_device(
    hidden,
    gain,
    w_query,
    w_key,
    w_value,
    cotangent,
    seq_length,
    home_offset,
    dest_shard,
    dest_offset,
):
    shards = lax.axis_size("dp")
    my_shard = lax.axis_index("dp")
    width_here = hidden.shape[1]
    shift_list = [-1, 1, shards // 2, shards // 2 + 1]
    stride_array = jnp.array(shift_list, dtype=jnp.int32)
    stride_mod = jnp.array([stride % shards for stride in shift_list], dtype=jnp.int32)
    wq_full, wk_full, wv_full = (
        lax.all_gather(w_query, "dp", axis=0, tiled=True),
        lax.all_gather(w_key, "dp", axis=0, tiled=True),
        lax.all_gather(w_value, "dp", axis=0, tiled=True),
    )
    own_len = seq_length[my_shard]
    own_off = home_offset[my_shard]
    own_move = (dest_shard[my_shard] - my_shard + shards) % shards
    chosen = (own_move[None, :] == stride_mod[:, None]).astype(jnp.int32)
    slot_len = jnp.sum(chosen * own_len[None, :], 1)
    slot_off = jnp.sum(chosen * own_off[None, :], 1)
    sources = (my_shard - stride_array + shards) % shards
    source_move = (dest_shard[sources] - sources[:, None] + shards) % shards
    matches = (source_move == stride_mod[:, None]).astype(jnp.int32)
    in_len = jnp.sum(matches * seq_length[sources], 1)
    in_start = jnp.sum(matches * dest_offset[sources], 1)
    within = jnp.arange(MAXLEN, dtype=jnp.int32)[None, :, None]

    def cuts(starts, lengths, rows):
        row = jnp.arange(rows, dtype=jnp.int32)[None, None, :]
        return (within < lengths[:, None, None]) & (row == starts[:, None, None] + within)

    home_cut = cuts(slot_off, slot_len, TOK_DEV).reshape(-1, TOK_DEV)
    dest_cut = cuts(in_start, in_len, CAP).reshape(-1, CAP)
    cot_blocks = pick_rows(dest_cut, cotangent).reshape(-1, MAXLEN, width_here)
    cot_home = jnp.concatenate(
        [passed_along(cot_blocks[i], "dp", -stride) for i, stride in enumerate(shift_list)], 0
    )
    cot_home = pick_rows(home_cut.T, cot_home)
    home_slot = jnp.arange(TOK_DEV, dtype=jnp.int32)
    belong = (
        (home_slot[None, :] >= own_off[:, None])
        & (home_slot[None, :] < (own_off + own_len)[:, None])
    ).astype(jnp.int32)
    start_of = jnp.sum(belong * own_off[:, None], 0)
    position = home_slot - start_of

    rows_full, gain_full = (
        lax.all_gather(hidden, "tensor", axis=1, tiled=True),
        lax.all_gather(gain, "tensor", axis=0, tiled=True),
    )
    values = rows_full.astype(jnp.float32)
    inverse_rms = lax.rsqrt(jnp.mean(values * values, 1, keepdims=True) + EPSILON)
    normed = (values * inverse_rms * gain_full.astype(jnp.float32)).astype(jnp.bfloat16)
    normed_columns = lax.all_to_all(normed, "dp", split_axis=1, concat_axis=0, tiled=True)
    attn_out, grad_query, grad_key, grad_value = attention_block(
        normed, wq_full, wk_full, wv_full, cot_home, start_of, position
    )
    out_blocks = pick_rows(home_cut, attn_out).reshape(-1, MAXLEN, width_here)
    out_dest = jnp.concatenate(
        [passed_along(out_blocks[i], "dp", stride) for i, stride in enumerate(shift_list)], 0
    )
    attention_output = pick_rows(dest_cut.T, out_dest)
    value_all = lax.all_gather(grad_value, "dp", axis=0, tiled=True)
    grad_value_weight = jnp.einsum(
        "rd,rc->dc", normed_columns, value_all, preferred_element_type=jnp.float32
    )
    partial_value = jnp.einsum("rc,dc->rd", grad_query, wq_full, preferred_element_type=jnp.float32)
    partial_value = partial_value + jnp.einsum(
        "rc,dc->rd", grad_key, wk_full, preferred_element_type=jnp.float32
    )
    partial_value = partial_value + jnp.einsum(
        "rc,dc->rd", grad_value, wv_full, preferred_element_type=jnp.float32
    )
    gain_here = gain.astype(jnp.float32)
    summed = lax.psum_scatter(
        partial_value.astype(jnp.bfloat16), "tensor", scatter_dimension=1, tiled=True
    ).astype(jnp.float32)
    weighted = summed * gain_here
    local_vals = hidden.astype(jnp.float32)
    row_dot = lax.psum(jnp.sum(weighted * local_vals, 1), "tensor")
    grad_hidden = (
        inverse_rms * weighted - local_vals * inverse_rms**3 * row_dot[:, None] / D
    ).astype(jnp.bfloat16)
    return (attention_output, grad_hidden, grad_value_weight)


def solution(mesh):
    return jax.shard_map(
        on_device,
        mesh=mesh,
        in_specs=(
            P("dp", "tensor"),
            P("tensor"),
            P("dp", "tensor"),
            P("dp", "tensor"),
            P("dp", "tensor"),
            P("dp", "tensor"),
            P(),
            P(),
            P(),
            P(),
        ),
        out_specs=(P("dp", "tensor"), P("dp", "tensor"), P("dp", "tensor")),
        check_vma=False,
    )
```

```python
import functools
import math

import jax
import jax.numpy as jnp
from jax import lax
from jax.experimental import pallas as pl
from jax.experimental.pallas import tpu as pltpu
from jax.sharding import PartitionSpec as P

D = 4096
HEAD = 128
GROUP = 4
TOK_DEV = 128
MAXLEN = 64
CAP = 256
TILE = 512
TILES = D // TILE
HEAD_COLS = (GROUP + 2) * HEAD
EPSILON = 1e-05
ROPE_BASE = 500000.0
BF16 = jnp.bfloat16
F32 = jnp.float32
NN = (((1,), (0,)), ((), ()))
NT = (((1,), (1,)), ((), ()))
TN = (((0,), (0,)), ((), ()))


def mm(a, b, dims=NN):
    return lax.dot_general(a, b, dims, preferred_element_type=F32)


def kernel(
    n,
    nt,
    seq_length,
    home_offset,
    dest_shard,
    dest_offset,
    hidden,
    gain,
    freq,
    cotangent,
    w_query,
    w_key,
    w_value,
    out_ref,
    gh_ref,
    gvw_ref,
    wbuf,
    hid,
    gbuf,
    nrm,
    nblk,
    ncol,
    cot_send,
    cot_recv,
    cot_home,
    acc,
    pacc,
    psend,
    precv,
    rsend,
    rrecv,
    gvbuf,
    out_send,
    out_recv,
    gvw_acc,
    load_sem,
    wsend,
    wrecv,
    ssend,
    srecv,
    gsend,
    grecv,
    gssend,
    gsrecv,
    hsend,
    hrecv,
    bsend,
    brecv,
    csend,
    crecv,
    asend,
    arecv,
    osend,
    orecv,
    psems,
    prems,
    rsems,
    rrems,
):
    me = lax.axis_index("dp")
    t = lax.axis_index("tensor")
    kh = wbuf.shape[0]
    blk = D // n
    tp = TILES // nt
    chips = n // 2
    hops = chips // 2
    zs = chips // 2
    core = lax.rem(me, 2)
    chip = lax.div(me, 2)
    z, x = lax.div(chip, 2), lax.rem(chip, 2)
    place = (1 - x) * z + x * (2 * zs - 1 - z)
    sibling = me + 1 - 2 * core
    strides = [n - 1, 1, n // 2, n // 2 + 1]

    def chip_at(position):
        position = lax.rem(position + 2 * chips, chips)
        side = lax.div(position, zs)
        return (1 - side) * (2 * position) + side * (2 * (2 * zs - 1 - position) + 1)

    sides = [chip_at(place + 1) * 2 + core, chip_at(place - 1) * 2 + core]

    barrier = pltpu.get_barrier_semaphore()

    def greet(j, carry):
        pl.semaphore_signal(
            barrier,
            inc=1,
            device_id={"dp": lax.rem(me + j, n)},
            device_id_type=pl.DeviceIdType.MESH,
        )
        return carry

    lax.fori_loop(1, n, greet, 0)
    for j in range(1, nt):
        pl.semaphore_signal(
            barrier,
            inc=1,
            device_id={"tensor": lax.rem(t + j, nt)},
            device_id_type=pl.DeviceIdType.MESH,
        )

    def remote(src, dst, ssem, rsem, where):
        return pltpu.make_async_remote_copy(
            src_ref=src,
            dst_ref=dst,
            send_sem=ssem,
            recv_sem=rsem,
            device_id=where,
            device_id_type=pl.DeviceIdType.MESH,
        )

    loads = []
    own_rows = pl.ds(pl.multiple_of(me * blk, blk), blk)
    for h in range(kh):
        for part, (src, first, width) in enumerate(
            (
                (w_query, 0, GROUP * HEAD),
                (w_key, GROUP * HEAD, HEAD),
                (w_value, (GROUP + 1) * HEAD, HEAD),
            )
        ):
            loads.append(
                pltpu.make_async_copy(
                    src.at[:, pl.ds(h * width, width)],
                    wbuf.at[h, own_rows, pl.ds(first, width)],
                    load_sem.at[h, part],
                )
            )
    for load in loads:
        load.start()

    for i in range(tp):
        hid[t * tp + i] = hidden[:, i * TILE : (i + 1) * TILE]
        gbuf[t * tp + i] = jnp.broadcast_to(gain[:, i * TILE : (i + 1) * TILE], (8, TILE))

    pl.semaphore_wait(barrier, n - 1 + nt - 1)

    own_tiles = pl.ds(t * tp, tp)
    tensor_copies = []
    for j in range(1, nt):
        peer = {"tensor": lax.rem(t + j, nt)}
        tensor_copies.append(
            remote(hid.at[own_tiles], hid.at[own_tiles], hsend.at[j, 0], hrecv.at[j, 0], peer)
        )
        tensor_copies.append(
            remote(gbuf.at[own_tiles], gbuf.at[own_tiles], hsend.at[j, 1], hrecv.at[j, 1], peer)
        )
    for copy in tensor_copies:
        copy.start()

    def w_view(h, which, q, part):
        rows = (2 * q + which) * blk
        if part is None:
            return wbuf.at[h, pl.ds(pl.multiple_of(rows, blk), blk)]
        half = blk // 2
        return wbuf.at[h, pl.ds(pl.multiple_of(rows + part * half, half), half)]

    def g_view(h, which, q, part):
        rows = (2 * q + which) * TOK_DEV
        half = TOK_DEV if part is None else TOK_DEV // 2
        rows = rows if part is None else rows + part * half
        return gvbuf.at[:, pl.ds(pl.multiple_of(rows, half), half)]

    def part_of(way, k):
        return way if k == hops else None

    def distant(way, k):
        return chip_at(place - k) if way == 0 else chip_at(place + k)

    def ring_copy(view, sems, h, way, k, q):
        block = view(h, core, q, part_of(way, k))
        return remote(
            block, block, sems[0].at[h, way, k], sems[1].at[h, way, k], {"dp": sides[way]}
        )

    def sibling_copy(view, sems, h, way, k, q, which):
        block = view(h, which, q, part_of(way, k))
        return remote(
            block, block, sems[2].at[h, way, k], sems[3].at[h, way, k], {"dp": sibling}
        )

    def ring_begin(view, sems, h):
        for way in range(2):
            ring_copy(view, sems, h, way, 1, chip).start()
        sibling_copy(view, sems, h, 0, 0, chip, core).start()

    def ring_steps(view, sems, h):
        for k in range(1, hops + 1):
            for way in range(2):
                q = distant(way, k)
                ring_copy(view, sems, h, way, k, q).wait_recv()
                if k < hops:
                    ring_copy(view, sems, h, way, k + 1, q).start()
                sibling_copy(view, sems, h, way, k, q, core).start()
        sibling_copy(view, sems, h, 0, 0, chip, 1 - core).wait_recv()
        for k in range(1, hops + 1):
            for way in range(2):
                sibling_copy(view, sems, h, way, k, distant(way, k), 1 - core).wait_recv()

    def ring_end(view, sems, h):
        sibling_copy(view, sems, h, 0, 0, chip, core).wait_send()
        for k in range(1, hops + 1):
            for way in range(2):
                q = distant(way, k)
                sibling_copy(view, sems, h, way, k, q, core).wait_send()
                ring_copy(view, sems, h, way, k, distant(way, k - 1)).wait_send()

    w_sems = (wsend, wrecv, ssend, srecv)
    g_sems = (gsend, grecv, gssend, gsrecv)
    for load in loads:
        load.wait()
    ring_begin(w_view, w_sems, 0)
    if kh > 1:
        ring_begin(w_view, w_sems, 1)

    def picked(table, row, target, slot):
        total = jnp.int32(0)
        for c in range(4):
            total = total + jnp.where(dest_shard[row, c] == target, table[row, c], 0)
        return total

    home_plan, dest_plan = [], []
    for stride in strides:
        target = lax.rem(me + stride, n)
        source = lax.rem(me - stride + n, n)
        home_plan.append(
            (picked(home_offset, me, target, 0), picked(seq_length, me, target, 0))
        )
        dest_plan.append(
            (picked(dest_offset, source, me, 0), picked(seq_length, source, me, 0))
        )

    def cut(plan, rows):
        start, length = plan
        w = lax.broadcasted_iota(jnp.int32, (MAXLEN, rows), 0)
        r = lax.broadcasted_iota(jnp.int32, (MAXLEN, rows), 1)
        return jnp.where((w < length) & (r == start + w), 1.0, 0.0).astype(BF16)

    def uncut(plan, rows):
        start, length = plan
        w = lax.broadcasted_iota(jnp.int32, (rows, MAXLEN), 1)
        r = lax.broadcasted_iota(jnp.int32, (rows, MAXLEN), 0)
        return jnp.where((w < length) & (r == start + w), 1.0, 0.0).astype(BF16)

    for e in range(4):
        cot_send[e] = mm(cut(dest_plan[e], CAP), cotangent[...]).astype(BF16)
    cot_copies = [
        remote(
            cot_send.at[e],
            cot_recv.at[e],
            csend.at[e],
            crecv.at[e],
            {"dp": lax.rem(me - strides[e] + n, n)},
        )
        for e in range(4)
    ]
    for copy in cot_copies:
        copy.start()

    for copy in tensor_copies:
        copy.wait_send()
    for j in range(1, nt):
        theirs = pl.ds(lax.rem(t - j + nt, nt) * tp, tp)
        peer = {"tensor": lax.rem(t + j, nt)}
        remote(hid.at[theirs], hid.at[theirs], hsend.at[j, 0], hrecv.at[j, 0], peer).wait_recv()
        remote(gbuf.at[theirs], gbuf.at[theirs], hsend.at[j, 1], hrecv.at[j, 1], peer).wait_recv()
    squares = jnp.zeros((TOK_DEV, 1), F32)
    for j in range(TILES):
        values = hid[j].astype(F32)
        squares = squares + jnp.sum(values * values, 1, keepdims=True)
    inverse_rms = lax.rsqrt(squares * (1.0 / D) + EPSILON)
    for j in range(TILES):
        rows = (hid[j].astype(F32) * inverse_rms * gbuf[j, 0:1, :]).astype(BF16)
        nrm[j] = rows
        for i in range(TILE // blk):
            nblk[j * (TILE // blk) + i] = rows[:, i * blk : (i + 1) * blk]
    my_tokens = pl.ds(pl.multiple_of(me * TOK_DEV, TOK_DEV), TOK_DEV)

    def norm_copy(j):
        peer = lax.rem(me + j, n)
        return remote(
            nblk.at[peer], ncol.at[my_tokens], bsend.at[j], brecv.at[j], {"dp": peer}
        )

    def norm_start(j, carry):
        norm_copy(j).start()
        return carry

    lax.fori_loop(1, n, norm_start, 0)
    ncol[my_tokens, :] = nblk[me]

    row = lax.broadcasted_iota(jnp.int32, (TOK_DEV, TOK_DEV), 0)
    col = lax.broadcasted_iota(jnp.int32, (TOK_DEV, TOK_DEV), 1)
    row_start = jnp.zeros((TOK_DEV, TOK_DEV), jnp.int32)
    col_start = jnp.zeros((TOK_DEV, TOK_DEV), jnp.int32)
    for start, length in home_plan:
        row_start = jnp.where((row >= start) & (row < start + length), start, row_start)
        col_start = jnp.where((col >= start) & (col < start + length), start, col_start)
    bias = jnp.where((row_start == col_start) & (col <= row), 0.0, -1e30).astype(F32)
    bias = jnp.concatenate([bias] * GROUP, 0)
    angles = (row - row_start).astype(F32) * freq[0:1, :]
    cosine = jnp.cos(angles)
    sine = jnp.sin(angles) * jnp.where(col < HEAD // 2, -1.0, 1.0)

    def rotate(values, sine_part):
        return values * cosine + pltpu.roll(values, HEAD // 2, 1) * sine_part

    for copy in cot_copies:
        copy.wait()
    for h in range(kh):
        total = jnp.zeros((TOK_DEV, TILE), F32)
        for e in range(4):
            total = total + mm(
                uncut(home_plan[e], TOK_DEV), cot_recv[e, :, h * TILE : (h + 1) * TILE]
            )
        cot_home[h] = total.astype(BF16)

    for j in range(TILES):
        pacc[j] = jnp.zeros((TOK_DEV, TILE), F32)

    def out_copy(h, e):
        return remote(
            out_send.at[h, e],
            out_recv.at[h, e],
            osend.at[h, e],
            orecv.at[h, e],
            {"dp": lax.rem(me + strides[e], n)},
        )

    def one_head(h, carry):
        ring_steps(w_view, w_sems, h)

        @pl.when(h + 2 < kh)
        def _():
            ring_begin(w_view, w_sems, h + 2)

        acc[...] = jnp.zeros_like(acc)

        def project(j, carry):
            rows = pl.ds(pl.multiple_of(j * TILE, TILE), TILE)
            acc[...] += mm(nrm[j], wbuf[h, rows, :])
            return carry

        lax.fori_loop(0, TILES, project, 0)
        query = jnp.concatenate(
            [rotate(acc[:, g * HEAD : (g + 1) * HEAD], sine) for g in range(GROUP)], 0
        ).astype(BF16)
        key = rotate(acc[:, GROUP * HEAD : (GROUP + 1) * HEAD], sine).astype(BF16)
        value = acc[:, (GROUP + 1) * HEAD :].astype(BF16)
        factor = HEAD**-0.5
        scores = mm(query, key, NT) * factor + bias
        exp_terms = jnp.exp(scores - jnp.max(scores, -1, keepdims=True))
        probs = exp_terms / jnp.sum(exp_terms, -1, keepdims=True)
        probs_low = probs.astype(BF16)
        mixed = mm(probs_low, value).astype(BF16)
        cot = cot_home[h]
        grad_out = jnp.concatenate(
            [cot[:, g * HEAD : (g + 1) * HEAD] for g in range(GROUP)], 0
        )
        grad_value = mm(probs_low, grad_out, TN).astype(BF16)
        grad_probs = mm(grad_out, value, NT)
        centre = jnp.sum(grad_probs * probs, -1, keepdims=True)
        grad_scores = (probs * (grad_probs - centre) * factor).astype(BF16)
        grad_query = mm(grad_scores, key)
        grad_key = rotate(mm(grad_scores, query, TN), -sine).astype(BF16)
        attn = jnp.concatenate(
            [mixed[g * TOK_DEV : (g + 1) * TOK_DEV] for g in range(GROUP)], 1
        )
        for e in range(4):
            out_send[h, e] = mm(cut(home_plan[e], TOK_DEV), attn).astype(BF16)
            out_copy(h, e).start()
        gvbuf[h, my_tokens, :] = grad_value
        grads = jnp.concatenate(
            [
                rotate(grad_query[g * TOK_DEV : (g + 1) * TOK_DEV], -sine).astype(BF16)
                for g in range(GROUP)
            ]
            + [grad_key, grad_value],
            1,
        )

        def back(j, carry):
            rows = pl.ds(pl.multiple_of(j * TILE, TILE), TILE)
            pacc[j] += mm(grads, wbuf[h, rows, :], NT)
            return carry

        lax.fori_loop(0, TILES, back, 0)
        return carry

    lax.fori_loop(0, kh, one_head, 0)

    ring_begin(g_view, g_sems, 0)
    dots = jnp.zeros((TOK_DEV, 1), F32)
    for j in range(TILES):
        low = pacc[j].astype(BF16)
        psend[j] = low
        dots = dots + jnp.sum(
            low.astype(F32) * gbuf[j, 0:1, :] * hid[j].astype(F32), 1, keepdims=True
        )
    rsend[...] = jnp.broadcast_to(dots, (TOK_DEV, HEAD))
    term_copies = []
    for j in range(1, nt):
        to = lax.rem(t + j, nt)
        peer = {"tensor": to}
        term_copies.append(
            remote(
                psend.at[pl.ds(to * tp, tp)], precv.at[j - 1], psems.at[j], prems.at[j], peer
            )
        )
        term_copies.append(remote(rsend, rrecv.at[j - 1], rsems.at[j], rrems.at[j], peer))
    for copy in term_copies:
        copy.start()
    ring_steps(g_view, g_sems, 0)
    for copy in term_copies:
        copy.wait()
    row_dot = rsend[:, 0:1]
    for j in range(1, nt):
        row_dot = row_dot + rrecv[j - 1, :, 0:1]
    for i in range(tp):
        summed = psend[t * tp + i].astype(F32)
        for j in range(1, nt):
            summed = summed + precv[j - 1, i].astype(F32)
        weighted = summed * gbuf[t * tp + i, 0:1, :]
        gh_ref[:, i * TILE : (i + 1) * TILE] = (
            inverse_rms * weighted
            - hid[t * tp + i].astype(F32) * inverse_rms**3 * row_dot * (1.0 / D)
        ).astype(BF16)

    for h in range(kh):
        for e in range(4):
            out_copy(h, e).wait()
        total = jnp.zeros((CAP, TILE), F32)
        for e in range(4):
            total = total + mm(uncut(dest_plan[e], CAP), out_recv[h, e])
        out_ref[:, h * TILE : (h + 1) * TILE] = total.astype(BF16)

    def norm_wait(j, carry):
        peer = lax.rem(me - j + n, n)
        theirs = pl.ds(pl.multiple_of(peer * TOK_DEV, TOK_DEV), TOK_DEV)
        remote(
            nblk.at[peer], ncol.at[theirs], bsend.at[j], brecv.at[j], {"dp": peer}
        ).wait_recv()
        norm_copy(j).wait_send()
        return carry

    lax.fori_loop(1, n, norm_wait, 0)
    gvw_acc[...] = jnp.zeros_like(gvw_acc)

    def weigh(c, carry):
        rows = pl.ds(pl.multiple_of(c * TILE, TILE), TILE)
        for h in range(kh):
            gvw_acc[:, h * HEAD : (h + 1) * HEAD] += mm(ncol[rows, :], gvbuf[h, rows, :], TN)
        return carry

    lax.fori_loop(0, n * TOK_DEV // TILE, weigh, 0)
    gvw_ref[...] = gvw_acc[...]

    def finish(h, carry):
        ring_end(w_view, w_sems, h)
        return carry

    lax.fori_loop(0, kh, finish, 0)
    ring_end(g_view, g_sems, 0)


def on_device(
    hidden,
    gain,
    w_query,
    w_key,
    w_value,
    cotangent,
    seq_length,
    home_offset,
    dest_shard,
    dest_offset,
):
    n = lax.axis_size("dp")
    nt = lax.axis_size("tensor")
    kh = w_key.shape[1] // HEAD
    width = hidden.shape[1]
    blk = D // n
    tp = TILES // nt
    hops = n // 4
    half = HEAD // 2
    exponent = jnp.arange(half, dtype=F32) * (2.0 / HEAD)
    inverse = jnp.power(jnp.float32(ROPE_BASE), -exponent)
    freq = jnp.broadcast_to(jnp.concatenate([inverse, inverse])[None, :], (8, HEAD))
    dma = pltpu.SemaphoreType.DMA
    vmem = pl.BlockSpec(memory_space=pltpu.VMEM)
    smem = pl.BlockSpec(memory_space=pltpu.SMEM)
    anywhere = pl.BlockSpec(memory_space=pl.ANY)
    return pl.pallas_call(
        functools.partial(kernel, n, nt),
        out_shape=(
            jax.ShapeDtypeStruct((CAP, width), BF16),
            jax.ShapeDtypeStruct((TOK_DEV, width), BF16),
            jax.ShapeDtypeStruct((blk, kh * HEAD), F32),
        ),
        in_specs=[smem] * 4 + [vmem] * 4 + [anywhere] * 3,
        out_specs=(vmem, vmem, vmem),
        scratch_shapes=[
            pltpu.VMEM((kh, D, HEAD_COLS), BF16),
            pltpu.VMEM((TILES, TOK_DEV, TILE), BF16),
            pltpu.VMEM((TILES, 8, TILE), F32),
            pltpu.VMEM((TILES, TOK_DEV, TILE), BF16),
            pltpu.VMEM((n, TOK_DEV, blk), BF16),
            pltpu.VMEM((n * TOK_DEV, blk), BF16),
            pltpu.VMEM((4, MAXLEN, width), BF16),
            pltpu.VMEM((4, MAXLEN, width), BF16),
            pltpu.VMEM((kh, TOK_DEV, TILE), BF16),
            pltpu.VMEM((TOK_DEV, HEAD_COLS), F32),
            pltpu.VMEM((TILES, TOK_DEV, TILE), F32),
            pltpu.VMEM((TILES, TOK_DEV, TILE), BF16),
            pltpu.VMEM((nt - 1, tp, TOK_DEV, TILE), BF16),
            pltpu.VMEM((TOK_DEV, HEAD), F32),
            pltpu.VMEM((nt - 1, TOK_DEV, HEAD), F32),
            pltpu.VMEM((kh, n * TOK_DEV, HEAD), BF16),
            pltpu.VMEM((kh, 4, MAXLEN, TILE), BF16),
            pltpu.VMEM((kh, 4, MAXLEN, TILE), BF16),
            pltpu.VMEM((blk, kh * HEAD), F32),
            dma((kh, 3)),
            dma((kh, 2, hops + 1)),
            dma((kh, 2, hops + 1)),
            dma((kh, 2, hops + 1)),
            dma((kh, 2, hops + 1)),
            dma((1, 2, hops + 1)),
            dma((1, 2, hops + 1)),
            dma((1, 2, hops + 1)),
            dma((1, 2, hops + 1)),
            dma((nt, 2)),
            dma((nt, 2)),
            dma((n,)),
            dma((n,)),
            dma((4,)),
            dma((4,)),
            dma((4,)),
            dma((4,)),
            dma((kh, 4)),
            dma((kh, 4)),
            dma((nt,)),
            dma((nt,)),
            dma((nt,)),
            dma((nt,)),
        ],
        compiler_params=pltpu.CompilerParams(
            collective_id=0, has_side_effects=True, vmem_limit_bytes=56 * 1024 * 1024
        ),
        cost_estimate=pl.CostEstimate(
            flops=8 * 10**9, bytes_accessed=8 * 10**6, transcendentals=10**6
        ),
    )(
        seq_length,
        home_offset,
        dest_shard,
        dest_offset,
        hidden,
        gain.astype(F32)[None, :],
        freq,
        cotangent,
        w_query,
        w_key,
        w_value,
    )


def solution(mesh):
    return jax.shard_map(
        on_device,
        mesh=mesh,
        in_specs=(
            P("dp", "tensor"),
            P("tensor"),
            P("dp", "tensor"),
            P("dp", "tensor"),
            P("dp", "tensor"),
            P("dp", "tensor"),
            P(),
            P(),
            P(),
            P(),
        ),
        out_specs=(P("dp", "tensor"), P("dp", "tensor"), P("dp", "tensor")),
        check_vma=False,
    )
```

```python
import functools
import math

import jax
import jax.numpy as jnp
from jax import lax
from jax.experimental import pallas as pl
from jax.experimental.pallas import tpu as pltpu
from jax.sharding import PartitionSpec as P

D = 4096
HEAD = 128
GROUP = 4
TOK_DEV = 128
MAXLEN = 64
CAP = 256
TILE = 512
TILES = D // TILE
HEAD_COLS = (GROUP + 2) * HEAD
EPSILON = 1e-05
ROPE_BASE = 500000.0
BF16 = jnp.bfloat16
F32 = jnp.float32
NN = (((1,), (0,)), ((), ()))
NT = (((1,), (1,)), ((), ()))
TN = (((0,), (0,)), ((), ()))


def mm(a, b, dims=NN):
    return lax.dot_general(a, b, dims, preferred_element_type=F32)


def kernel(
    n,
    nt,
    seq_length,
    home_offset,
    dest_shard,
    dest_offset,
    hidden,
    gain,
    freq,
    cotangent,
    w_query,
    w_key,
    w_value,
    out_ref,
    gh_ref,
    gvw_ref,
    wbuf,
    hid,
    gbuf,
    nrm,
    nblk,
    ncol,
    cot_send,
    cot_recv,
    cot_home,
    acc,
    pacc,
    psend,
    precv,
    rsend,
    rrecv,
    gvbuf,
    out_send,
    out_recv,
    gvw_acc,
    load_sem,
    wzs,
    wzr,
    wxs,
    wxr,
    wss,
    wsr,
    gzs,
    gzr,
    gxs,
    gxr,
    gss,
    gsr,
    ysend,
    yrecv,
    hsend,
    hrecv,
    bsend,
    brecv,
    csend,
    crecv,
    asend,
    arecv,
    osend,
    orecv,
    psems,
    prems,
    rsems,
    rrems,
):
    me = lax.axis_index("dp")
    t = lax.axis_index("tensor")
    kh = wbuf.shape[0]
    blk = D // n
    tp = TILES // nt
    zs = n // 4
    core = lax.rem(me, 2)
    chip = lax.div(me, 2)
    z, x = lax.div(chip, 2), lax.rem(chip, 2)
    sibling = me + 1 - 2 * core
    strides = [n - 1, 1, n // 2, n // 2 + 1]

    barrier = pltpu.get_barrier_semaphore()

    def greet(j, carry):
        pl.semaphore_signal(
            barrier,
            inc=1,
            device_id={"dp": lax.rem(me + j, n)},
            device_id_type=pl.DeviceIdType.MESH,
        )
        return carry

    lax.fori_loop(1, n, greet, 0)
    for j in range(1, nt):
        pl.semaphore_signal(
            barrier,
            inc=1,
            device_id={"tensor": lax.rem(t + j, nt)},
            device_id_type=pl.DeviceIdType.MESH,
        )

    def remote(src, dst, ssem, rsem, where):
        return pltpu.make_async_remote_copy(
            src_ref=src,
            dst_ref=dst,
            send_sem=ssem,
            recv_sem=rsem,
            device_id=where,
            device_id_type=pl.DeviceIdType.MESH,
        )

    loads = []
    own_rows = pl.ds(pl.multiple_of(me * blk, blk), blk)
    for h in range(kh):
        for part, (src, first, width) in enumerate(
            (
                (w_query, 0, GROUP * HEAD),
                (w_key, GROUP * HEAD, HEAD),
                (w_value, (GROUP + 1) * HEAD, HEAD),
            )
        ):
            loads.append(
                pltpu.make_async_copy(
                    src.at[:, pl.ds(h * width, width)],
                    wbuf.at[h, own_rows, pl.ds(first, width)],
                    load_sem.at[h, part],
                )
            )
    for load in loads:
        load.start()

    for i in range(tp):
        hid[t * tp + i] = hidden[:, i * TILE : (i + 1) * TILE]
        gbuf[t * tp + i] = jnp.broadcast_to(gain[:, i * TILE : (i + 1) * TILE], (8, TILE))

    pl.semaphore_wait(barrier, n - 1 + nt - 1)

    own_tiles = pl.ds(t * tp, tp)
    tensor_copies = []
    for j in range(1, nt):
        peer = {"tensor": lax.rem(t + j, nt)}
        tensor_copies.append(
            remote(hid.at[own_tiles], hid.at[own_tiles], hsend.at[j, 0], hrecv.at[j, 0], peer)
        )
        tensor_copies.append(
            remote(gbuf.at[own_tiles], gbuf.at[own_tiles], hsend.at[j, 1], hrecv.at[j, 1], peer)
        )
    for copy in tensor_copies:
        copy.start()

    def w_view(h, zz, xx, which):
        rows = pl.multiple_of((4 * zz + 2 * xx + which) * blk, blk)
        return wbuf.at[h, pl.ds(rows, blk)]

    def g_view(h, zz, xx, which):
        rows = pl.multiple_of((4 * zz + 2 * xx + which) * TOK_DEV, TOK_DEV)
        return gvbuf.at[h, pl.ds(rows, TOK_DEV)]

    up, down = lax.rem(me + 4, n), lax.rem(me - 4 + n, n)
    across = me + 2 - 4 * x

    def z_copy(view, sems, h, way, zz):
        block = view(h, zz, x, core)
        return remote(
            block,
            block,
            sems[0].at[h, way, zz],
            sems[1].at[h, zz],
            {"dp": up if way == 0 else down},
        )

    def x_copy(view, sems, h, zz, xx):
        block = view(h, zz, xx, core)
        return remote(block, block, sems[2].at[h, zz], sems[3].at[h, zz], {"dp": across})

    def s_copy(view, sems, h, zz, xx, which):
        block = view(h, zz, xx, which)
        return remote(
            block, block, sems[4].at[h, xx, zz], sems[5].at[h, xx, zz], {"dp": sibling}
        )

    def begin(view, sems, h):
        @pl.when(z < zs - 1)
        def _():
            z_copy(view, sems, h, 0, z).start()

        @pl.when(z > 0)
        def _():
            z_copy(view, sems, h, 1, z).start()

        x_copy(view, sems, h, z, x).start()
        s_copy(view, sems, h, z, x, core).start()

    def step(view, sems, h, k):
        if k < zs:

            @pl.when(z >= k)
            def _():
                zz = z - k
                z_copy(view, sems, h, 0, zz).wait_recv()

                @pl.when(z < zs - 1)
                def _():
                    z_copy(view, sems, h, 0, zz).start()

                x_copy(view, sems, h, zz, x).start()
                s_copy(view, sems, h, zz, x, core).start()

            @pl.when(z + k < zs)
            def _():
                zz = z + k
                z_copy(view, sems, h, 1, zz).wait_recv()

                @pl.when(z > 0)
                def _():
                    z_copy(view, sems, h, 1, zz).start()

                x_copy(view, sems, h, zz, x).start()
                s_copy(view, sems, h, zz, x, core).start()

        def from_across(zz):
            x_copy(view, sems, h, zz, 1 - x).wait_recv()
            s_copy(view, sems, h, zz, 1 - x, core).start()

        if k == 1:
            from_across(z)
        else:

            @pl.when(z >= k - 1)
            def _():
                from_across(z - k + 1)

            @pl.when(z + k - 1 < zs)
            def _():
                from_across(z + k - 1)

    def gathered(view, sems, h):
        def one(zz, carry):
            s_copy(view, sems, h, zz, x, 1 - core).wait_recv()
            s_copy(view, sems, h, zz, 1 - x, 1 - core).wait_recv()
            return carry

        lax.fori_loop(0, zs, one, 0)

    def drained(view, sems, h):
        def one(zz, carry):
            s_copy(view, sems, h, zz, x, core).wait_send()
            s_copy(view, sems, h, zz, 1 - x, core).wait_send()
            x_copy(view, sems, h, zz, x).wait_send()

            @pl.when((zz <= z) & (z < zs - 1))
            def _():
                z_copy(view, sems, h, 0, zz).wait_send()

            @pl.when((zz >= z) & (z > 0))
            def _():
                z_copy(view, sems, h, 1, zz).wait_send()

            return carry

        lax.fori_loop(0, zs, one, 0)

    w_sems = (wzs, wzr, wxs, wxr, wss, wsr)
    g_sems = (gzs, gzr, gxs, gxr, gss, gsr)
    early = zs // 2
    for load in loads:
        load.wait()
    begin(w_view, w_sems, 0)
    if kh > 1:
        begin(w_view, w_sems, 1)

    def picked(table, row, target, slot):
        total = jnp.int32(0)
        for c in range(4):
            total = total + jnp.where(dest_shard[row, c] == target, table[row, c], 0)
        return total

    home_plan, dest_plan = [], []
    for stride in strides:
        target = lax.rem(me + stride, n)
        source = lax.rem(me - stride + n, n)
        home_plan.append(
            (picked(home_offset, me, target, 0), picked(seq_length, me, target, 0))
        )
        dest_plan.append(
            (picked(dest_offset, source, me, 0), picked(seq_length, source, me, 0))
        )

    def cut(plan, rows):
        start, length = plan
        w = lax.broadcasted_iota(jnp.int32, (MAXLEN, rows), 0)
        r = lax.broadcasted_iota(jnp.int32, (MAXLEN, rows), 1)
        return jnp.where((w < length) & (r == start + w), 1.0, 0.0).astype(BF16)

    def uncut(plan, rows):
        start, length = plan
        w = lax.broadcasted_iota(jnp.int32, (rows, MAXLEN), 1)
        r = lax.broadcasted_iota(jnp.int32, (rows, MAXLEN), 0)
        return jnp.where((w < length) & (r == start + w), 1.0, 0.0).astype(BF16)

    for e in range(4):
        cot_send[e] = mm(cut(dest_plan[e], CAP), cotangent[...]).astype(BF16)
    cot_copies = [
        remote(
            cot_send.at[e],
            cot_recv.at[e],
            csend.at[e],
            crecv.at[e],
            {"dp": lax.rem(me - strides[e] + n, n)},
        )
        for e in range(4)
    ]
    for copy in cot_copies:
        copy.start()
    for k in range(1, early):
        step(w_view, w_sems, 0, k)

    for copy in tensor_copies:
        copy.wait_send()
    for j in range(1, nt):
        theirs = pl.ds(lax.rem(t - j + nt, nt) * tp, tp)
        peer = {"tensor": lax.rem(t + j, nt)}
        remote(hid.at[theirs], hid.at[theirs], hsend.at[j, 0], hrecv.at[j, 0], peer).wait_recv()
        remote(gbuf.at[theirs], gbuf.at[theirs], hsend.at[j, 1], hrecv.at[j, 1], peer).wait_recv()
    squares = jnp.zeros((TOK_DEV, 1), F32)
    for j in range(TILES):
        values = hid[j].astype(F32)
        squares = squares + jnp.sum(values * values, 1, keepdims=True)
    inverse_rms = lax.rsqrt(squares * (1.0 / D) + EPSILON)
    for j in range(TILES):
        rows = (hid[j].astype(F32) * inverse_rms * gbuf[j, 0:1, :]).astype(BF16)
        nrm[j] = rows
        for i in range(TILE // blk):
            nblk[j * (TILE // blk) + i] = rows[:, i * blk : (i + 1) * blk]
    my_tokens = pl.ds(pl.multiple_of(me * TOK_DEV, TOK_DEV), TOK_DEV)
    share = TOK_DEV // nt
    my_share = pl.ds(pl.multiple_of(t * share, share), share)

    def norm_copy(j, src, dst):
        return remote(
            nblk.at[src, my_share],
            ncol.at[dst, my_share],
            bsend.at[j],
            brecv.at[j],
            {"dp": lax.rem(me + j, n)},
        )

    def norm_start(j, carry):
        norm_copy(j, lax.rem(me + j, n), me).start()
        return carry

    lax.fori_loop(1, n, norm_start, 0)
    ncol[me, my_share, :] = nblk[me, my_share, :]

    def share_copy(j, shard):
        rows = pl.ds(pl.multiple_of(shard * share, share), share)
        block = ncol.at[:, rows]
        return remote(
            block, block, ysend.at[j], yrecv.at[j], {"tensor": lax.rem(t + j, nt)}
        )

    def share_rows():
        def norm_wait(j, carry):
            norm_copy(j, lax.rem(me + j, n), lax.rem(me - j + n, n)).wait_recv()
            norm_copy(j, lax.rem(me + j, n), me).wait_send()
            return carry

        lax.fori_loop(1, n, norm_wait, 0)
        for j in range(1, nt):
            share_copy(j, t).start()

    step(w_view, w_sems, 0, early)

    row = lax.broadcasted_iota(jnp.int32, (TOK_DEV, TOK_DEV), 0)
    col = lax.broadcasted_iota(jnp.int32, (TOK_DEV, TOK_DEV), 1)
    row_start = jnp.zeros((TOK_DEV, TOK_DEV), jnp.int32)
    col_start = jnp.zeros((TOK_DEV, TOK_DEV), jnp.int32)
    for start, length in home_plan:
        row_start = jnp.where((row >= start) & (row < start + length), start, row_start)
        col_start = jnp.where((col >= start) & (col < start + length), start, col_start)
    bias = jnp.where((row_start == col_start) & (col <= row), 0.0, -1e30).astype(F32)
    bias = jnp.concatenate([bias] * GROUP, 0)
    angles = (row - row_start).astype(F32) * freq[0:1, :]
    cosine = jnp.cos(angles)
    sine = jnp.sin(angles) * jnp.where(col < HEAD // 2, -1.0, 1.0)

    def rotate(values, sine_part):
        return values * cosine + pltpu.roll(values, HEAD // 2, 1) * sine_part

    for copy in cot_copies:
        copy.wait()
    for h in range(kh):
        total = jnp.zeros((TOK_DEV, TILE), F32)
        for e in range(4):
            total = total + mm(
                uncut(home_plan[e], TOK_DEV), cot_recv[e, :, h * TILE : (h + 1) * TILE]
            )
        cot_home[h] = total.astype(BF16)

    for j in range(TILES):
        pacc[j] = jnp.zeros((TOK_DEV, TILE), F32)

    def out_copy(h, e):
        return remote(
            out_send.at[h, e],
            out_recv.at[h, e],
            osend.at[h, e],
            orecv.at[h, e],
            {"dp": lax.rem(me + strides[e], n)},
        )

    def project_head(h):
        gathered(w_view, w_sems, h)
        acc[...] = jnp.zeros_like(acc)

        def project(j, carry):
            rows = pl.ds(pl.multiple_of(j * TILE, TILE), TILE)
            acc[...] += mm(nrm[j], wbuf[h, rows, :])
            return carry

        lax.fori_loop(0, TILES, project, 0)
    def attend_head(h):
        query = jnp.concatenate(
            [rotate(acc[:, g * HEAD : (g + 1) * HEAD], sine) for g in range(GROUP)], 0
        ).astype(BF16)
        key = rotate(acc[:, GROUP * HEAD : (GROUP + 1) * HEAD], sine).astype(BF16)
        value = acc[:, (GROUP + 1) * HEAD :].astype(BF16)
        factor = HEAD**-0.5
        scores = mm(query, key, NT) * factor + bias
        exp_terms = jnp.exp(scores - jnp.max(scores, -1, keepdims=True))
        probs = exp_terms / jnp.sum(exp_terms, -1, keepdims=True)
        probs_low = probs.astype(BF16)
        mixed = mm(probs_low, value).astype(BF16)
        cot = cot_home[h]
        grad_out = jnp.concatenate(
            [cot[:, g * HEAD : (g + 1) * HEAD] for g in range(GROUP)], 0
        )
        grad_value = mm(probs_low, grad_out, TN).astype(BF16)
        grad_probs = mm(grad_out, value, NT)
        centre = jnp.sum(grad_probs * probs, -1, keepdims=True)
        grad_scores = (probs * (grad_probs - centre) * factor).astype(BF16)
        grad_query = mm(grad_scores, key)
        grad_key = rotate(mm(grad_scores, query, TN), -sine).astype(BF16)
        attn = jnp.concatenate(
            [mixed[g * TOK_DEV : (g + 1) * TOK_DEV] for g in range(GROUP)], 1
        )
        for e in range(4):
            out_send[h, e] = mm(cut(home_plan[e], TOK_DEV), attn).astype(BF16)
            out_copy(h, e).start()
        gvbuf[h, my_tokens, :] = grad_value
        grads = jnp.concatenate(
            [
                rotate(grad_query[g * TOK_DEV : (g + 1) * TOK_DEV], -sine).astype(BF16)
                for g in range(GROUP)
            ]
            + [grad_key, grad_value],
            1,
        )

        def back(j, carry):
            rows = pl.ds(pl.multiple_of(j * TILE, TILE), TILE)
            pacc[j] += mm(grads, wbuf[h, rows, :], NT)
            return carry

        lax.fori_loop(0, TILES, back, 0)
        begin(g_view, g_sems, h)

    def round_of(h, carry):
        for k in range(1, early + 1):

            @pl.when(h < kh)
            def _():
                step(w_view, w_sems, h, early + k)

            @pl.when(h + 1 < kh)
            def _():
                step(w_view, w_sems, h + 1, k)

            @pl.when((h >= 2) & (h < kh))
            def _():
                step(g_view, g_sems, h - 2, 2 * k - 1)
                step(g_view, g_sems, h - 2, 2 * k)

            if k == 1:

                @pl.when(h + 2 < kh)
                def _():
                    begin(w_view, w_sems, h + 2)

                @pl.when(h >= 1)
                def _():
                    project_head(h - 1)

        @pl.when(h >= 1)
        def _():
            attend_head(h - 1)

        @pl.when(h == 1)
        def _():
            share_rows()

        return carry

    lax.fori_loop(0, kh + 1, round_of, 0)

    last = range(max(kh - 2, 0), kh)
    dots = jnp.zeros((TOK_DEV, 1), F32)
    for j in range(TILES):
        low = pacc[j].astype(BF16)
        psend[j] = low
        dots = dots + jnp.sum(
            low.astype(F32) * gbuf[j, 0:1, :] * hid[j].astype(F32), 1, keepdims=True
        )
    rsend[...] = jnp.broadcast_to(dots, (TOK_DEV, HEAD))
    term_copies = []
    for j in range(1, nt):
        to = lax.rem(t + j, nt)
        peer = {"tensor": to}
        term_copies.append(
            remote(
                psend.at[pl.ds(to * tp, tp)], precv.at[j - 1], psems.at[j], prems.at[j], peer
            )
        )
        term_copies.append(remote(rsend, rrecv.at[j - 1], rsems.at[j], rrems.at[j], peer))
    for copy in term_copies:
        copy.start()
    def place_out(h):
        for e in range(4):
            out_copy(h, e).wait()
        total = jnp.zeros((CAP, TILE), F32)
        for e in range(4):
            total = total + mm(uncut(dest_plan[e], CAP), out_recv[h, e])
        out_ref[:, h * TILE : (h + 1) * TILE] = total.astype(BF16)

    for k in range(1, zs + 1):
        for h in last:
            step(g_view, g_sems, h, k)
        if k <= kh:
            place_out(k - 1)
    for copy in term_copies:
        copy.wait()
    row_dot = rsend[:, 0:1]
    for j in range(1, nt):
        row_dot = row_dot + rrecv[j - 1, :, 0:1]
    for i in range(tp):
        summed = psend[t * tp + i].astype(F32)
        for j in range(1, nt):
            summed = summed + precv[j - 1, i].astype(F32)
        weighted = summed * gbuf[t * tp + i, 0:1, :]
        gh_ref[:, i * TILE : (i + 1) * TILE] = (
            inverse_rms * weighted
            - hid[t * tp + i].astype(F32) * inverse_rms**3 * row_dot * (1.0 / D)
        ).astype(BF16)

    for j in range(1, nt):
        share_copy(j, t).wait_send()
        share_copy(j, lax.rem(t - j + nt, nt)).wait_recv()
    for h in range(kh):
        gathered(g_view, g_sems, h)
    gvw_acc[...] = jnp.zeros_like(gvw_acc)

    def weigh(c, carry):
        rows = pl.ds(pl.multiple_of(c * TILE, TILE), TILE)
        owners = pl.ds(c * (TILE // TOK_DEV), TILE // TOK_DEV)
        columns = ncol[owners].reshape(TILE, blk)
        values = jnp.concatenate([gvbuf[h, rows, :] for h in range(kh)], 1)
        gvw_acc[...] += mm(columns, values, TN)
        return carry

    lax.fori_loop(0, n * TOK_DEV // TILE, weigh, 0)
    gvw_ref[...] = gvw_acc[...]

    def finish(h, carry):
        drained(w_view, w_sems, h)
        drained(g_view, g_sems, h)
        return carry

    lax.fori_loop(0, kh, finish, 0)


def on_device(
    hidden,
    gain,
    w_query,
    w_key,
    w_value,
    cotangent,
    seq_length,
    home_offset,
    dest_shard,
    dest_offset,
):
    n = lax.axis_size("dp")
    nt = lax.axis_size("tensor")
    kh = w_key.shape[1] // HEAD
    width = hidden.shape[1]
    blk = D // n
    tp = TILES // nt
    zs = n // 4
    half = HEAD // 2
    exponent = jnp.arange(half, dtype=F32) * (2.0 / HEAD)
    inverse = jnp.power(jnp.float32(ROPE_BASE), -exponent)
    freq = jnp.broadcast_to(jnp.concatenate([inverse, inverse])[None, :], (8, HEAD))
    dma = pltpu.SemaphoreType.DMA
    vmem = pl.BlockSpec(memory_space=pltpu.VMEM)
    smem = pl.BlockSpec(memory_space=pltpu.SMEM)
    anywhere = pl.BlockSpec(memory_space=pl.ANY)
    return pl.pallas_call(
        functools.partial(kernel, n, nt),
        out_shape=(
            jax.ShapeDtypeStruct((CAP, width), BF16),
            jax.ShapeDtypeStruct((TOK_DEV, width), BF16),
            jax.ShapeDtypeStruct((blk, kh * HEAD), F32),
        ),
        in_specs=[smem] * 4 + [vmem] * 4 + [anywhere] * 3,
        out_specs=(vmem, vmem, vmem),
        scratch_shapes=[
            pltpu.VMEM((kh, D, HEAD_COLS), BF16),
            pltpu.VMEM((TILES, TOK_DEV, TILE), BF16),
            pltpu.VMEM((TILES, 8, TILE), F32),
            pltpu.VMEM((TILES, TOK_DEV, TILE), BF16),
            pltpu.VMEM((n, TOK_DEV, blk), BF16),
            pltpu.VMEM((n, TOK_DEV, blk), BF16),
            pltpu.VMEM((4, MAXLEN, width), BF16),
            pltpu.VMEM((4, MAXLEN, width), BF16),
            pltpu.VMEM((kh, TOK_DEV, TILE), BF16),
            pltpu.VMEM((TOK_DEV, HEAD_COLS), F32),
            pltpu.VMEM((TILES, TOK_DEV, TILE), F32),
            pltpu.VMEM((TILES, TOK_DEV, TILE), BF16),
            pltpu.VMEM((nt - 1, tp, TOK_DEV, TILE), BF16),
            pltpu.VMEM((TOK_DEV, HEAD), F32),
            pltpu.VMEM((nt - 1, TOK_DEV, HEAD), F32),
            pltpu.VMEM((kh, n * TOK_DEV, HEAD), BF16),
            pltpu.VMEM((kh, 4, MAXLEN, TILE), BF16),
            pltpu.VMEM((kh, 4, MAXLEN, TILE), BF16),
            pltpu.VMEM((blk, kh * HEAD), F32),
            dma((kh, 3)),
            dma((kh, 2, zs)),
            dma((kh, zs)),
            dma((kh, zs)),
            dma((kh, zs)),
            dma((kh, 2, zs)),
            dma((kh, 2, zs)),
            dma((kh, 2, zs)),
            dma((kh, zs)),
            dma((kh, zs)),
            dma((kh, zs)),
            dma((kh, 2, zs)),
            dma((kh, 2, zs)),
            dma((nt,)),
            dma((nt,)),
            dma((nt, 2)),
            dma((nt, 2)),
            dma((n,)),
            dma((n,)),
            dma((4,)),
            dma((4,)),
            dma((4,)),
            dma((4,)),
            dma((kh, 4)),
            dma((kh, 4)),
            dma((nt,)),
            dma((nt,)),
            dma((nt,)),
            dma((nt,)),
        ],
        compiler_params=pltpu.CompilerParams(
            collective_id=0, has_side_effects=True, vmem_limit_bytes=56 * 1024 * 1024
        ),
        cost_estimate=pl.CostEstimate(
            flops=8 * 10**9, bytes_accessed=8 * 10**6, transcendentals=10**6
        ),
    )(
        seq_length,
        home_offset,
        dest_shard,
        dest_offset,
        hidden,
        gain.astype(F32)[None, :],
        freq,
        cotangent,
        w_query,
        w_key,
        w_value,
    )


def solution(mesh):
    return jax.shard_map(
        on_device,
        mesh=mesh,
        in_specs=(
            P("dp", "tensor"),
            P("tensor"),
            P("dp", "tensor"),
            P("dp", "tensor"),
            P("dp", "tensor"),
            P("dp", "tensor"),
            P(),
            P(),
            P(),
            P(),
        ),
        out_specs=(P("dp", "tensor"), P("dp", "tensor"), P("dp", "tensor")),
        check_vma=False,
    )
```

```python
import functools
import math

import jax
import jax.numpy as jnp
from jax import lax
from jax.experimental import pallas as pl
from jax.experimental.pallas import tpu as pltpu
from jax.sharding import PartitionSpec as P

D = 4096
HEAD = 128
GROUP = 4
TOK_DEV = 128
MAXLEN = 64
CAP = 256
TILE = 512
TILES = D // TILE
HEAD_COLS = (GROUP + 2) * HEAD
EPSILON = 1e-05
ROPE_BASE = 500000.0
BF16 = jnp.bfloat16
F32 = jnp.float32
NN = (((1,), (0,)), ((), ()))
NT = (((1,), (1,)), ((), ()))
TN = (((0,), (0,)), ((), ()))


def mm(a, b, dims=NN):
    return lax.dot_general(a, b, dims, preferred_element_type=F32)


def kernel(
    n,
    nt,
    seq_length,
    home_offset,
    dest_shard,
    dest_offset,
    hidden,
    gain,
    freq,
    cotangent,
    w_query,
    w_key,
    w_value,
    out_ref,
    gh_ref,
    gvw_ref,
    wbuf,
    hid,
    gbuf,
    nrm,
    nblk,
    ncol,
    cot_send,
    cot_recv,
    cot_home,
    acc,
    grads_t,
    pacc,
    psend,
    precv,
    rsend,
    rrecv,
    gvbuf,
    out_send,
    out_recv,
    gvw_acc,
    load_sem,
    wzs,
    wzr,
    wxs,
    wxr,
    wss,
    wsr,
    gzs,
    gzr,
    gxs,
    gxr,
    gss,
    gsr,
    ysend,
    yrecv,
    hsend,
    hrecv,
    bsend,
    brecv,
    csend,
    crecv,
    asend,
    arecv,
    osend,
    orecv,
    psems,
    prems,
    rsems,
    rrems,
):
    me = lax.axis_index("dp")
    t = lax.axis_index("tensor")
    kh = wbuf.shape[0]
    blk = D // n
    tp = TILES // nt
    zs = n // 4
    core = lax.rem(me, 2)
    chip = lax.div(me, 2)
    z, x = lax.div(chip, 2), lax.rem(chip, 2)
    sibling = me + 1 - 2 * core
    strides = [n - 1, 1, n // 2, n // 2 + 1]

    barrier = pltpu.get_barrier_semaphore()

    def greet(j, carry):
        pl.semaphore_signal(
            barrier,
            inc=1,
            device_id={"dp": lax.rem(me + j, n)},
            device_id_type=pl.DeviceIdType.MESH,
        )
        return carry

    lax.fori_loop(1, n, greet, 0)
    for j in range(1, nt):
        pl.semaphore_signal(
            barrier,
            inc=1,
            device_id={"tensor": lax.rem(t + j, nt)},
            device_id_type=pl.DeviceIdType.MESH,
        )

    def remote(src, dst, ssem, rsem, where):
        return pltpu.make_async_remote_copy(
            src_ref=src,
            dst_ref=dst,
            send_sem=ssem,
            recv_sem=rsem,
            device_id=where,
            device_id_type=pl.DeviceIdType.MESH,
        )

    loads = []
    own_rows = pl.ds(pl.multiple_of(me * blk, blk), blk)
    for h in range(kh):
        for part, (src, first, width) in enumerate(
            (
                (w_query, 0, GROUP * HEAD),
                (w_key, GROUP * HEAD, HEAD),
                (w_value, (GROUP + 1) * HEAD, HEAD),
            )
        ):
            loads.append(
                pltpu.make_async_copy(
                    src.at[:, pl.ds(h * width, width)],
                    wbuf.at[h, own_rows, pl.ds(first, width)],
                    load_sem.at[h, part],
                )
            )
    for load in loads:
        load.start()

    for i in range(tp):
        hid[t * tp + i] = hidden[:, i * TILE : (i + 1) * TILE]
        gbuf[t * tp + i] = jnp.broadcast_to(gain[:, i * TILE : (i + 1) * TILE], (8, TILE))

    pl.semaphore_wait(barrier, n - 1 + nt - 1)

    own_tiles = pl.ds(t * tp, tp)
    tensor_copies = []
    for j in range(1, nt):
        peer = {"tensor": lax.rem(t + j, nt)}
        tensor_copies.append(
            remote(hid.at[own_tiles], hid.at[own_tiles], hsend.at[j, 0], hrecv.at[j, 0], peer)
        )
        tensor_copies.append(
            remote(gbuf.at[own_tiles], gbuf.at[own_tiles], hsend.at[j, 1], hrecv.at[j, 1], peer)
        )
    for copy in tensor_copies:
        copy.start()

    def w_view(h, zz, xx, which):
        rows = pl.multiple_of((4 * zz + 2 * xx + which) * blk, blk)
        return wbuf.at[h, pl.ds(rows, blk)]

    def g_view(h, zz, xx, which):
        rows = pl.multiple_of((4 * zz + 2 * xx + which) * TOK_DEV, TOK_DEV)
        return gvbuf.at[h, pl.ds(rows, TOK_DEV)]

    up, down = lax.rem(me + 4, n), lax.rem(me - 4 + n, n)
    across = me + 2 - 4 * x

    def z_copy(view, sems, h, way, zz):
        block = view(h, zz, x, core)
        return remote(
            block,
            block,
            sems[0].at[h, way, zz],
            sems[1].at[h, zz],
            {"dp": up if way == 0 else down},
        )

    def x_copy(view, sems, h, zz, xx):
        block = view(h, zz, xx, core)
        return remote(block, block, sems[2].at[h, zz], sems[3].at[h, zz], {"dp": across})

    def s_copy(view, sems, h, zz, xx, which):
        block = view(h, zz, xx, which)
        return remote(
            block, block, sems[4].at[h, xx, zz], sems[5].at[h, xx, zz], {"dp": sibling}
        )

    def begin(view, sems, h):
        @pl.when(z < zs - 1)
        def _():
            z_copy(view, sems, h, 0, z).start()

        @pl.when(z > 0)
        def _():
            z_copy(view, sems, h, 1, z).start()

        x_copy(view, sems, h, z, x).start()
        s_copy(view, sems, h, z, x, core).start()

    def step(view, sems, h, k):
        if k < zs:

            @pl.when(z >= k)
            def _():
                zz = z - k
                z_copy(view, sems, h, 0, zz).wait_recv()

                @pl.when(z < zs - 1)
                def _():
                    z_copy(view, sems, h, 0, zz).start()

                x_copy(view, sems, h, zz, x).start()
                s_copy(view, sems, h, zz, x, core).start()

            @pl.when(z + k < zs)
            def _():
                zz = z + k
                z_copy(view, sems, h, 1, zz).wait_recv()

                @pl.when(z > 0)
                def _():
                    z_copy(view, sems, h, 1, zz).start()

                x_copy(view, sems, h, zz, x).start()
                s_copy(view, sems, h, zz, x, core).start()

        def from_across(zz):
            x_copy(view, sems, h, zz, 1 - x).wait_recv()
            s_copy(view, sems, h, zz, 1 - x, core).start()

        if k == 1:
            from_across(z)
        else:

            @pl.when(z >= k - 1)
            def _():
                from_across(z - k + 1)

            @pl.when(z + k - 1 < zs)
            def _():
                from_across(z + k - 1)

    def gathered(view, sems, h):
        def one(zz, carry):
            s_copy(view, sems, h, zz, x, 1 - core).wait_recv()
            s_copy(view, sems, h, zz, 1 - x, 1 - core).wait_recv()
            return carry

        lax.fori_loop(0, zs, one, 0)

    def drained(view, sems, h):
        def one(zz, carry):
            s_copy(view, sems, h, zz, x, core).wait_send()
            s_copy(view, sems, h, zz, 1 - x, core).wait_send()
            x_copy(view, sems, h, zz, x).wait_send()

            @pl.when((zz <= z) & (z < zs - 1))
            def _():
                z_copy(view, sems, h, 0, zz).wait_send()

            @pl.when((zz >= z) & (z > 0))
            def _():
                z_copy(view, sems, h, 1, zz).wait_send()

            return carry

        lax.fori_loop(0, zs, one, 0)

    w_sems = (wzs, wzr, wxs, wxr, wss, wsr)
    g_sems = (gzs, gzr, gxs, gxr, gss, gsr)
    early = zs // 2
    for load in loads:
        load.wait()
    for h in range(kh):
        begin(w_view, w_sems, h)

    def picked(table, row, target, slot):
        total = jnp.int32(0)
        for c in range(4):
            total = total + jnp.where(dest_shard[row, c] == target, table[row, c], 0)
        return total

    home_plan, dest_plan = [], []
    for stride in strides:
        target = lax.rem(me + stride, n)
        source = lax.rem(me - stride + n, n)
        home_plan.append(
            (picked(home_offset, me, target, 0), picked(seq_length, me, target, 0))
        )
        dest_plan.append(
            (picked(dest_offset, source, me, 0), picked(seq_length, source, me, 0))
        )

    def cut(plan, rows):
        w = lax.broadcasted_iota(jnp.int32, (MAXLEN, rows), 0)
        r = lax.broadcasted_iota(jnp.int32, (MAXLEN, rows), 1)
        return jnp.concatenate(
            [
                jnp.where((w < length) & (r == start + w), 1.0, 0.0)
                for start, length in plan
            ],
            0,
        ).astype(BF16)

    def uncut(plan, rows):
        place = lax.broadcasted_iota(jnp.int32, (rows, 4 * MAXLEN), 1)
        r = lax.broadcasted_iota(jnp.int32, (rows, 4 * MAXLEN), 0)
        total = jnp.zeros((rows, 4 * MAXLEN), F32)
        for e, (start, length) in enumerate(plan):
            w = place - e * MAXLEN
            total = jnp.where((w >= 0) & (w < length) & (r == start + w), 1.0, total)
        return total.astype(BF16)

    picks = cut(dest_plan, CAP)
    for i in range(tp):
        columns = slice(i * TILE, (i + 1) * TILE)
        cot_send[:, :, columns] = (
            mm(picks, cotangent[:, columns]).astype(BF16).reshape(4, MAXLEN, TILE)
        )
    cot_copies = [
        remote(
            cot_send.at[e],
            cot_recv.at[e],
            csend.at[e],
            crecv.at[e],
            {"dp": lax.rem(me - strides[e] + n, n)},
        )
        for e in range(4)
    ]
    for copy in cot_copies:
        copy.start()
    for k in range(1, early):
        step(w_view, w_sems, 0, k)

    for copy in tensor_copies:
        copy.wait_send()
    for j in range(1, nt):
        theirs = pl.ds(lax.rem(t - j + nt, nt) * tp, tp)
        peer = {"tensor": lax.rem(t + j, nt)}
        remote(hid.at[theirs], hid.at[theirs], hsend.at[j, 0], hrecv.at[j, 0], peer).wait_recv()
        remote(gbuf.at[theirs], gbuf.at[theirs], hsend.at[j, 1], hrecv.at[j, 1], peer).wait_recv()
    squares = jnp.zeros((TOK_DEV, 1), F32)
    for j in range(TILES):
        values = hid[j].astype(F32)
        squares = squares + jnp.sum(values * values, 1, keepdims=True)
    inverse_rms = lax.rsqrt(squares * (1.0 / D) + EPSILON)
    for j in range(TILES):
        rows = (hid[j].astype(F32) * inverse_rms * gbuf[j, 0:1, :]).astype(BF16)
        nrm[j] = rows
        for i in range(TILE // blk):
            nblk[j * (TILE // blk) + i] = rows[:, i * blk : (i + 1) * blk]
    my_tokens = pl.ds(pl.multiple_of(me * TOK_DEV, TOK_DEV), TOK_DEV)
    share = TOK_DEV // nt
    my_share = pl.ds(pl.multiple_of(t * share, share), share)

    def norm_copy(j, src, dst):
        return remote(
            nblk.at[src, my_share],
            ncol.at[dst, my_share],
            bsend.at[j],
            brecv.at[j],
            {"dp": lax.rem(me + j, n)},
        )

    def norm_start(j, carry):
        norm_copy(j, lax.rem(me + j, n), me).start()
        return carry

    lax.fori_loop(1, n, norm_start, 0)
    ncol[me, my_share, :] = nblk[me, my_share, :]

    def share_copy(j, shard):
        rows = pl.ds(pl.multiple_of(shard * share, share), share)
        block = ncol.at[:, rows]
        return remote(
            block, block, ysend.at[j], yrecv.at[j], {"tensor": lax.rem(t + j, nt)}
        )

    def share_rows():
        def norm_wait(j, carry):
            norm_copy(j, lax.rem(me + j, n), lax.rem(me - j + n, n)).wait_recv()
            norm_copy(j, lax.rem(me + j, n), me).wait_send()
            return carry

        lax.fori_loop(1, n, norm_wait, 0)
        for j in range(1, nt):
            share_copy(j, t).start()

    step(w_view, w_sems, 0, early)

    row = lax.broadcasted_iota(jnp.int32, (TOK_DEV, TOK_DEV), 0)
    col = lax.broadcasted_iota(jnp.int32, (TOK_DEV, TOK_DEV), 1)
    row_start = jnp.zeros((TOK_DEV, TOK_DEV), jnp.int32)
    col_start = jnp.zeros((TOK_DEV, TOK_DEV), jnp.int32)
    for start, length in home_plan:
        row_start = jnp.where((row >= start) & (row < start + length), start, row_start)
        col_start = jnp.where((col >= start) & (col < start + length), start, col_start)
    bias = jnp.where((row_start == col_start) & (col <= row), 0.0, -1e30).astype(F32)
    bias = jnp.concatenate([bias] * GROUP, 0)
    angles = (row - row_start).astype(F32) * freq[0:1, :]
    cosine = jnp.cos(angles)
    sine = jnp.sin(angles) * jnp.where(col < HEAD // 2, -1.0, 1.0)

    def rotate(values, sine_part):
        return values * cosine + pltpu.roll(values, HEAD // 2, 1) * sine_part

    for copy in cot_copies:
        copy.wait()
    picks = uncut(home_plan, TOK_DEV)
    for h in range(kh):
        arrived = cot_recv[:, :, h * TILE : (h + 1) * TILE].reshape(4 * MAXLEN, TILE)
        cot_home[h] = mm(picks, arrived).astype(BF16)

    for j in range(TILES):
        pacc[j] = jnp.zeros((TILE, TOK_DEV), F32)

    def out_copy(h, e):
        return remote(
            out_send.at[h, e],
            out_recv.at[h, e],
            osend.at[h, e],
            orecv.at[h, e],
            {"dp": lax.rem(me + strides[e], n)},
        )

    def project_head(h, first, last):
        def project(j, carry):
            rows = pl.ds(pl.multiple_of(j * TILE, TILE), TILE)
            acc[...] += mm(nrm[j], wbuf[h, rows, :])
            return carry

        lax.fori_loop(first, last, project, 0)

    def attend_head(h):
        query = jnp.concatenate(
            [rotate(acc[:, g * HEAD : (g + 1) * HEAD], sine) for g in range(GROUP)], 0
        ).astype(BF16)
        key = rotate(acc[:, GROUP * HEAD : (GROUP + 1) * HEAD], sine).astype(BF16)
        value = acc[:, (GROUP + 1) * HEAD :].astype(BF16)
        factor = HEAD**-0.5
        scores = mm(query, key, NT) * factor + bias
        exp_terms = jnp.exp(scores - jnp.max(scores, -1, keepdims=True))
        probs = exp_terms / jnp.sum(exp_terms, -1, keepdims=True)
        probs_low = probs.astype(BF16)
        mixed = mm(probs_low, value).astype(BF16)
        cot = cot_home[h]
        grad_out = jnp.concatenate(
            [cot[:, g * HEAD : (g + 1) * HEAD] for g in range(GROUP)], 0
        )
        grad_value = mm(probs_low, grad_out, TN)
        grad_probs = mm(grad_out, value, NT)
        centre = jnp.sum(grad_probs * probs, -1, keepdims=True)
        grad_scores = (probs * (grad_probs - centre) * factor).astype(BF16)
        grad_query = mm(grad_scores, key)
        grad_key = rotate(mm(grad_scores, query, TN), -sine)
        attn = jnp.concatenate(
            [mixed[g * TOK_DEV : (g + 1) * TOK_DEV] for g in range(GROUP)], 1
        )
        out_send[h] = (
            mm(cut(home_plan, TOK_DEV), attn).astype(BF16).reshape(4, MAXLEN, TILE)
        )
        for e in range(4):
            out_copy(h, e).start()
        gvbuf[h, my_tokens, :] = grad_value.astype(BF16)
        grads = jnp.concatenate(
            [
                rotate(grad_query[g * TOK_DEV : (g + 1) * TOK_DEV], -sine).T
                for g in range(GROUP)
            ]
            + [grad_key.T, grad_value.T],
            0,
        )
        grads_t[...] = grads.astype(BF16)
        begin(g_view, g_sems, h)

    def back_head(h):
        def back(j, carry):
            rows = pl.ds(pl.multiple_of(j * TILE, TILE), TILE)
            pacc[j] += mm(wbuf[h, rows, :], grads_t[...])
            return carry

        lax.fori_loop(0, TILES, back, 0)

    def round_of(h, carry):
        for k in range(1, early + 1):

            @pl.when(h < kh)
            def _():
                step(w_view, w_sems, h, early + k)

            @pl.when((h >= 2) & (h < kh))
            def _():
                step(g_view, g_sems, h - 2, 2 * k - 1)
                step(g_view, g_sems, h - 2, 2 * k)

            if k == 1:

                @pl.when(h >= 1)
                def _():
                    gathered(w_view, w_sems, h - 1)
                    acc[...] = jnp.zeros_like(acc)
                    project_head(h - 1, 0, TILES // 2)

            if k == 2:

                @pl.when(h >= 1)
                def _():
                    attend_head(h - 1)

            @pl.when(h + 1 < kh)
            def _():
                step(w_view, w_sems, h + 1, k)

            if k == 1:

                @pl.when(h >= 1)
                def _():
                    project_head(h - 1, TILES // 2, TILES)

            if k == 2:

                @pl.when(h >= 1)
                def _():
                    back_head(h - 1)

        @pl.when(h == 1)
        def _():
            share_rows()

        return carry

    lax.fori_loop(0, kh + 1, round_of, 0)

    last = range(max(kh - 2, 0), kh)
    dots = jnp.zeros((TOK_DEV, 1), F32)
    for j in range(TILES):
        low = pacc[j].T.astype(BF16)
        psend[j] = low
        dots = dots + jnp.sum(
            low.astype(F32) * gbuf[j, 0:1, :] * hid[j].astype(F32), 1, keepdims=True
        )
    rsend[...] = jnp.broadcast_to(dots, (TOK_DEV, HEAD))
    term_copies = []
    for j in range(1, nt):
        to = lax.rem(t + j, nt)
        peer = {"tensor": to}
        term_copies.append(
            remote(
                psend.at[pl.ds(to * tp, tp)], precv.at[j - 1], psems.at[j], prems.at[j], peer
            )
        )
        term_copies.append(remote(rsend, rrecv.at[j - 1], rsems.at[j], rrems.at[j], peer))
    for copy in term_copies:
        copy.start()
    def place_out(h):
        for e in range(4):
            out_copy(h, e).wait()
        arrived = out_recv[h].reshape(4 * MAXLEN, TILE)
        out_ref[:, h * TILE : (h + 1) * TILE] = mm(uncut(dest_plan, CAP), arrived).astype(BF16)

    for k in range(1, zs + 1):
        for h in last:
            step(g_view, g_sems, h, k)
        if k <= kh:
            place_out(k - 1)
    for copy in term_copies:
        copy.wait()
    row_dot = rsend[:, 0:1]
    for j in range(1, nt):
        row_dot = row_dot + rrecv[j - 1, :, 0:1]
    for i in range(tp):
        summed = psend[t * tp + i].astype(F32)
        for j in range(1, nt):
            summed = summed + precv[j - 1, i].astype(F32)
        weighted = summed * gbuf[t * tp + i, 0:1, :]
        gh_ref[:, i * TILE : (i + 1) * TILE] = (
            inverse_rms * weighted
            - hid[t * tp + i].astype(F32) * inverse_rms**3 * row_dot * (1.0 / D)
        ).astype(BF16)

    for j in range(1, nt):
        share_copy(j, t).wait_send()
        share_copy(j, lax.rem(t - j + nt, nt)).wait_recv()
    for h in range(kh):
        gathered(g_view, g_sems, h)
    gvw_acc[...] = jnp.zeros_like(gvw_acc)

    def weigh(c, carry):
        rows = pl.ds(pl.multiple_of(c * TILE, TILE), TILE)
        owners = pl.ds(c * (TILE // TOK_DEV), TILE // TOK_DEV)
        columns = ncol[owners].reshape(TILE, blk)
        values = jnp.concatenate([gvbuf[h, rows, :] for h in range(kh)], 1)
        gvw_acc[...] += mm(columns, values, TN)
        return carry

    lax.fori_loop(0, n * TOK_DEV // TILE, weigh, 0)
    gvw_ref[...] = gvw_acc[...]

    def finish(h, carry):
        drained(w_view, w_sems, h)
        drained(g_view, g_sems, h)
        return carry

    lax.fori_loop(0, kh, finish, 0)


def on_device(
    hidden,
    gain,
    w_query,
    w_key,
    w_value,
    cotangent,
    seq_length,
    home_offset,
    dest_shard,
    dest_offset,
):
    n = lax.axis_size("dp")
    nt = lax.axis_size("tensor")
    kh = w_key.shape[1] // HEAD
    width = hidden.shape[1]
    blk = D // n
    tp = TILES // nt
    zs = n // 4
    half = HEAD // 2
    exponent = jnp.arange(half, dtype=F32) * (2.0 / HEAD)
    inverse = jnp.power(jnp.float32(ROPE_BASE), -exponent)
    freq = jnp.broadcast_to(jnp.concatenate([inverse, inverse])[None, :], (8, HEAD))
    dma = pltpu.SemaphoreType.DMA
    vmem = pl.BlockSpec(memory_space=pltpu.VMEM)
    smem = pl.BlockSpec(memory_space=pltpu.SMEM)
    anywhere = pl.BlockSpec(memory_space=pl.ANY)
    return pl.pallas_call(
        functools.partial(kernel, n, nt),
        out_shape=(
            jax.ShapeDtypeStruct((CAP, width), BF16),
            jax.ShapeDtypeStruct((TOK_DEV, width), BF16),
            jax.ShapeDtypeStruct((blk, kh * HEAD), F32),
        ),
        in_specs=[smem] * 4 + [vmem] * 4 + [anywhere] * 3,
        out_specs=(vmem, vmem, vmem),
        scratch_shapes=[
            pltpu.VMEM((kh, D, HEAD_COLS), BF16),
            pltpu.VMEM((TILES, TOK_DEV, TILE), BF16),
            pltpu.VMEM((TILES, 8, TILE), F32),
            pltpu.VMEM((TILES, TOK_DEV, TILE), BF16),
            pltpu.VMEM((n, TOK_DEV, blk), BF16),
            pltpu.VMEM((n, TOK_DEV, blk), BF16),
            pltpu.VMEM((4, MAXLEN, width), BF16),
            pltpu.VMEM((4, MAXLEN, width), BF16),
            pltpu.VMEM((kh, TOK_DEV, TILE), BF16),
            pltpu.VMEM((TOK_DEV, HEAD_COLS), F32),
            pltpu.VMEM((HEAD_COLS, TOK_DEV), BF16),
            pltpu.VMEM((TILES, TILE, TOK_DEV), F32),
            pltpu.VMEM((TILES, TOK_DEV, TILE), BF16),
            pltpu.VMEM((nt - 1, tp, TOK_DEV, TILE), BF16),
            pltpu.VMEM((TOK_DEV, HEAD), F32),
            pltpu.VMEM((nt - 1, TOK_DEV, HEAD), F32),
            pltpu.VMEM((kh, n * TOK_DEV, HEAD), BF16),
            pltpu.VMEM((kh, 4, MAXLEN, TILE), BF16),
            pltpu.VMEM((kh, 4, MAXLEN, TILE), BF16),
            pltpu.VMEM((blk, kh * HEAD), F32),
            dma((kh, 3)),
            dma((kh, 2, zs)),
            dma((kh, zs)),
            dma((kh, zs)),
            dma((kh, zs)),
            dma((kh, 2, zs)),
            dma((kh, 2, zs)),
            dma((kh, 2, zs)),
            dma((kh, zs)),
            dma((kh, zs)),
            dma((kh, zs)),
            dma((kh, 2, zs)),
            dma((kh, 2, zs)),
            dma((nt,)),
            dma((nt,)),
            dma((nt, 2)),
            dma((nt, 2)),
            dma((n,)),
            dma((n,)),
            dma((4,)),
            dma((4,)),
            dma((4,)),
            dma((4,)),
            dma((kh, 4)),
            dma((kh, 4)),
            dma((nt,)),
            dma((nt,)),
            dma((nt,)),
            dma((nt,)),
        ],
        compiler_params=pltpu.CompilerParams(
            collective_id=0, has_side_effects=True, vmem_limit_bytes=56 * 1024 * 1024
        ),
        cost_estimate=pl.CostEstimate(
            flops=8 * 10**9, bytes_accessed=8 * 10**6, transcendentals=10**6
        ),
    )(
        seq_length,
        home_offset,
        dest_shard,
        dest_offset,
        hidden,
        gain.astype(F32)[None, :],
        freq,
        cotangent,
        w_query,
        w_key,
        w_value,
    )


def solution(mesh):
    return jax.shard_map(
        on_device,
        mesh=mesh,
        in_specs=(
            P("dp", "tensor"),
            P("tensor"),
            P("dp", "tensor"),
            P("dp", "tensor"),
            P("dp", "tensor"),
            P("dp", "tensor"),
            P(),
            P(),
            P(),
            P(),
        ),
        out_specs=(P("dp", "tensor"), P("dp", "tensor"), P("dp", "tensor")),
        check_vma=False,
    )
```

```python
import functools
import math

import jax
import jax.numpy as jnp
from jax import lax
from jax.experimental import pallas as pl
from jax.experimental.pallas import tpu as pltpu
from jax.sharding import PartitionSpec as P

D = 4096
HEAD = 128
GROUP = 4
TOK_DEV = 128
MAXLEN = 64
CAP = 256
TILE = 512
TILES = D // TILE
HEAD_COLS = (GROUP + 2) * HEAD
EPSILON = 1e-05
ROPE_BASE = 500000.0
BF16 = jnp.bfloat16
F32 = jnp.float32
NN = (((1,), (0,)), ((), ()))
NT = (((1,), (1,)), ((), ()))
TN = (((0,), (0,)), ((), ()))


def mm(a, b, dims=NN):
    return lax.dot_general(a, b, dims, preferred_element_type=F32)


def kernel(
    n,
    nt,
    seq_length,
    home_offset,
    dest_shard,
    dest_offset,
    hidden,
    gain,
    freq,
    cotangent,
    w_query,
    w_key,
    w_value,
    out_ref,
    gh_ref,
    gvw_ref,
    wbuf,
    hid,
    gbuf,
    nrm,
    nblk,
    ncol,
    cot_send,
    cot_recv,
    cot_home,
    acc,
    grads_t,
    pacc,
    psend,
    precv,
    rsend,
    rrecv,
    gvbuf,
    out_send,
    out_recv,
    gvw_acc,
    load_sem,
    wzs,
    wzr,
    wxs,
    wxr,
    wss,
    wsr,
    gzs,
    gzr,
    gxs,
    gxr,
    gss,
    gsr,
    ysend,
    yrecv,
    hsend,
    hrecv,
    bsend,
    brecv,
    csend,
    crecv,
    asend,
    arecv,
    osend,
    orecv,
    psems,
    prems,
    rsems,
    rrems,
):
    me = lax.axis_index("dp")
    t = lax.axis_index("tensor")
    kh = wbuf.shape[0]
    blk = D // n
    tp = TILES // nt
    zs = n // 4
    core = lax.rem(me, 2)
    chip = lax.div(me, 2)
    z, x = lax.div(chip, 2), lax.rem(chip, 2)
    sibling = me + 1 - 2 * core
    strides = [n - 1, 1, n // 2, n // 2 + 1]

    barrier = pltpu.get_barrier_semaphore()

    def greet(j, carry):
        pl.semaphore_signal(
            barrier,
            inc=1,
            device_id={"dp": lax.rem(me + j, n)},
            device_id_type=pl.DeviceIdType.MESH,
        )
        return carry

    lax.fori_loop(1, n, greet, 0)
    for j in range(1, nt):
        pl.semaphore_signal(
            barrier,
            inc=1,
            device_id={"tensor": lax.rem(t + j, nt)},
            device_id_type=pl.DeviceIdType.MESH,
        )

    def remote(src, dst, ssem, rsem, where):
        return pltpu.make_async_remote_copy(
            src_ref=src,
            dst_ref=dst,
            send_sem=ssem,
            recv_sem=rsem,
            device_id=where,
            device_id_type=pl.DeviceIdType.MESH,
        )

    loads = []
    own_rows = pl.ds(pl.multiple_of(me * blk, blk), blk)
    for h in range(kh):
        for part, (src, first, width) in enumerate(
            (
                (w_query, 0, GROUP * HEAD),
                (w_key, GROUP * HEAD, HEAD),
                (w_value, (GROUP + 1) * HEAD, HEAD),
            )
        ):
            loads.append(
                pltpu.make_async_copy(
                    src.at[:, pl.ds(h * width, width)],
                    wbuf.at[h, own_rows, pl.ds(first, width)],
                    load_sem.at[h, part],
                )
            )
    for load in loads:
        load.start()

    for i in range(tp):
        hid[t * tp + i] = hidden[:, i * TILE : (i + 1) * TILE]
        gbuf[t * tp + i] = jnp.broadcast_to(gain[:, i * TILE : (i + 1) * TILE], (8, TILE))

    pl.semaphore_wait(barrier, n - 1 + nt - 1)

    own_tiles = pl.ds(t * tp, tp)
    tensor_copies = []
    for j in range(1, nt):
        peer = {"tensor": lax.rem(t + j, nt)}
        tensor_copies.append(
            remote(hid.at[own_tiles], hid.at[own_tiles], hsend.at[j, 0], hrecv.at[j, 0], peer)
        )
        tensor_copies.append(
            remote(gbuf.at[own_tiles], gbuf.at[own_tiles], hsend.at[j, 1], hrecv.at[j, 1], peer)
        )
    for copy in tensor_copies:
        copy.start()

    def w_view(h, zz, xx, which):
        rows = pl.multiple_of((4 * zz + 2 * xx + which) * blk, blk)
        return wbuf.at[h, pl.ds(rows, blk)]

    def g_view(h, zz, xx, which):
        rows = pl.multiple_of((4 * zz + 2 * xx + which) * TOK_DEV, TOK_DEV)
        return gvbuf.at[h, pl.ds(rows, TOK_DEV)]

    up, down = lax.rem(me + 4, n), lax.rem(me - 4 + n, n)
    across = me + 2 - 4 * x

    def z_copy(view, sems, h, way, zz):
        block = view(h, zz, x, core)
        return remote(
            block,
            block,
            sems[0].at[h, way, zz],
            sems[1].at[h, zz],
            {"dp": up if way == 0 else down},
        )

    def x_copy(view, sems, h, zz, xx):
        block = view(h, zz, xx, core)
        return remote(block, block, sems[2].at[h, zz], sems[3].at[h, zz], {"dp": across})

    def s_copy(view, sems, h, zz, xx, which):
        block = view(h, zz, xx, which)
        return remote(
            block, block, sems[4].at[h, xx, zz], sems[5].at[h, xx, zz], {"dp": sibling}
        )

    def begin(view, sems, h):
        @pl.when(z < zs - 1)
        def _():
            z_copy(view, sems, h, 0, z).start()

        @pl.when(z > 0)
        def _():
            z_copy(view, sems, h, 1, z).start()

        x_copy(view, sems, h, z, x).start()
        s_copy(view, sems, h, z, x, core).start()

    def step(view, sems, h, k):
        if k < zs:

            @pl.when(z >= k)
            def _():
                zz = z - k
                z_copy(view, sems, h, 0, zz).wait_recv()

                @pl.when(z < zs - 1)
                def _():
                    z_copy(view, sems, h, 0, zz).start()

                x_copy(view, sems, h, zz, x).start()
                s_copy(view, sems, h, zz, x, core).start()

            @pl.when(z + k < zs)
            def _():
                zz = z + k
                z_copy(view, sems, h, 1, zz).wait_recv()

                @pl.when(z > 0)
                def _():
                    z_copy(view, sems, h, 1, zz).start()

                x_copy(view, sems, h, zz, x).start()
                s_copy(view, sems, h, zz, x, core).start()

        def from_across(zz):
            x_copy(view, sems, h, zz, 1 - x).wait_recv()
            s_copy(view, sems, h, zz, 1 - x, core).start()

        if k == 1:
            from_across(z)
        else:

            @pl.when(z >= k - 1)
            def _():
                from_across(z - k + 1)

            @pl.when(z + k - 1 < zs)
            def _():
                from_across(z + k - 1)

    def gathered(view, sems, h):
        def one(zz, carry):
            s_copy(view, sems, h, zz, x, 1 - core).wait_recv()
            s_copy(view, sems, h, zz, 1 - x, 1 - core).wait_recv()
            return carry

        lax.fori_loop(0, zs, one, 0)

    def drained(view, sems, h):
        def one(zz, carry):
            s_copy(view, sems, h, zz, x, core).wait_send()
            s_copy(view, sems, h, zz, 1 - x, core).wait_send()
            x_copy(view, sems, h, zz, x).wait_send()

            @pl.when((zz <= z) & (z < zs - 1))
            def _():
                z_copy(view, sems, h, 0, zz).wait_send()

            @pl.when((zz >= z) & (z > 0))
            def _():
                z_copy(view, sems, h, 1, zz).wait_send()

            return carry

        lax.fori_loop(0, zs, one, 0)

    w_sems = (wzs, wzr, wxs, wxr, wss, wsr)
    g_sems = (gzs, gzr, gxs, gxr, gss, gsr)
    early = zs // 2
    for load in loads:
        load.wait()
    for h in range(kh):
        begin(w_view, w_sems, h)

    def picked(table, row, target, slot):
        total = jnp.int32(0)
        for c in range(4):
            total = total + jnp.where(dest_shard[row, c] == target, table[row, c], 0)
        return total

    home_plan, dest_plan = [], []
    for stride in strides:
        target = lax.rem(me + stride, n)
        source = lax.rem(me - stride + n, n)
        home_plan.append(
            (picked(home_offset, me, target, 0), picked(seq_length, me, target, 0))
        )
        dest_plan.append(
            (picked(dest_offset, source, me, 0), picked(seq_length, source, me, 0))
        )

    def cut(plan, rows):
        w = lax.broadcasted_iota(jnp.int32, (MAXLEN, rows), 0)
        r = lax.broadcasted_iota(jnp.int32, (MAXLEN, rows), 1)
        return jnp.concatenate(
            [
                jnp.where((w < length) & (r == start + w), 1.0, 0.0)
                for start, length in plan
            ],
            0,
        ).astype(BF16)

    def uncut(plan, rows):
        place = lax.broadcasted_iota(jnp.int32, (rows, 4 * MAXLEN), 1)
        r = lax.broadcasted_iota(jnp.int32, (rows, 4 * MAXLEN), 0)
        total = jnp.zeros((rows, 4 * MAXLEN), F32)
        for e, (start, length) in enumerate(plan):
            w = place - e * MAXLEN
            total = jnp.where((w >= 0) & (w < length) & (r == start + w), 1.0, total)
        return total.astype(BF16)

    picks = cut(dest_plan, CAP)
    for i in range(tp):
        columns = slice(i * TILE, (i + 1) * TILE)
        cot_send[:, :, columns] = (
            mm(picks, cotangent[:, columns]).astype(BF16).reshape(4, MAXLEN, TILE)
        )
    cot_copies = [
        remote(
            cot_send.at[e],
            cot_recv.at[e],
            csend.at[e],
            crecv.at[e],
            {"dp": lax.rem(me - strides[e] + n, n)},
        )
        for e in range(4)
    ]
    for copy in cot_copies:
        copy.start()
    for k in range(1, early):
        step(w_view, w_sems, 0, k)

    for copy in tensor_copies:
        copy.wait_send()
    for j in range(1, nt):
        theirs = pl.ds(lax.rem(t - j + nt, nt) * tp, tp)
        peer = {"tensor": lax.rem(t + j, nt)}
        remote(hid.at[theirs], hid.at[theirs], hsend.at[j, 0], hrecv.at[j, 0], peer).wait_recv()
        remote(gbuf.at[theirs], gbuf.at[theirs], hsend.at[j, 1], hrecv.at[j, 1], peer).wait_recv()
    squares = jnp.zeros((TOK_DEV, 1), F32)
    for j in range(TILES):
        values = hid[j].astype(F32)
        squares = squares + jnp.sum(values * values, 1, keepdims=True)
    inverse_rms = lax.rsqrt(squares * (1.0 / D) + EPSILON)
    for j in range(TILES):
        rows = (hid[j].astype(F32) * inverse_rms * gbuf[j, 0:1, :]).astype(BF16)
        nrm[j] = rows
        for i in range(TILE // blk):
            nblk[j * (TILE // blk) + i] = rows[:, i * blk : (i + 1) * blk]
    my_tokens = pl.ds(pl.multiple_of(me * TOK_DEV, TOK_DEV), TOK_DEV)
    share = TOK_DEV // nt
    my_share = pl.ds(pl.multiple_of(t * share, share), share)

    def norm_copy(j, src, dst):
        return remote(
            nblk.at[src, my_share],
            ncol.at[dst, my_share],
            bsend.at[j],
            brecv.at[j],
            {"dp": lax.rem(me + j, n)},
        )

    def norm_start(j, carry):
        norm_copy(j, lax.rem(me + j, n), me).start()
        return carry

    lax.fori_loop(1, n, norm_start, 0)
    ncol[me, my_share, :] = nblk[me, my_share, :]

    def share_copy(j, shard):
        rows = pl.ds(pl.multiple_of(shard * share, share), share)
        block = ncol.at[:, rows]
        return remote(
            block, block, ysend.at[j], yrecv.at[j], {"tensor": lax.rem(t + j, nt)}
        )

    def share_rows():
        def norm_wait(j, carry):
            norm_copy(j, lax.rem(me + j, n), lax.rem(me - j + n, n)).wait_recv()
            norm_copy(j, lax.rem(me + j, n), me).wait_send()
            return carry

        lax.fori_loop(1, n, norm_wait, 0)
        for j in range(1, nt):
            share_copy(j, t).start()

    step(w_view, w_sems, 0, early)

    row = lax.broadcasted_iota(jnp.int32, (TOK_DEV, TOK_DEV), 0)
    col = lax.broadcasted_iota(jnp.int32, (TOK_DEV, TOK_DEV), 1)
    row_start = jnp.zeros((TOK_DEV, TOK_DEV), jnp.int32)
    col_start = jnp.zeros((TOK_DEV, TOK_DEV), jnp.int32)
    for start, length in home_plan:
        row_start = jnp.where((row >= start) & (row < start + length), start, row_start)
        col_start = jnp.where((col >= start) & (col < start + length), start, col_start)
    bias = jnp.where((row_start == col_start) & (col <= row), 0.0, -1e30).astype(F32)
    bias = jnp.concatenate([bias] * GROUP, 0)
    angles = (row - row_start).astype(F32) * freq[0:1, :]
    cosine = jnp.cos(angles)
    sine = jnp.sin(angles) * jnp.where(col < HEAD // 2, -1.0, 1.0)

    def rotate(values, sine_part):
        return values * cosine + pltpu.roll(values, HEAD // 2, 1) * sine_part

    for copy in cot_copies:
        copy.wait()
    picks = uncut(home_plan, TOK_DEV)
    for h in range(kh):
        arrived = cot_recv[:, :, h * TILE : (h + 1) * TILE].reshape(4 * MAXLEN, TILE)
        cot_home[h] = mm(picks, arrived).astype(BF16)

    for j in range(TILES):
        pacc[j] = jnp.zeros((TILE, TOK_DEV), F32)

    def out_copy(h, e):
        return remote(
            out_send.at[h, e],
            out_recv.at[h, e],
            osend.at[h, e],
            orecv.at[h, e],
            {"dp": lax.rem(me + strides[e], n)},
        )

    def project_head(h, first, last):
        def project(j, carry):
            rows = pl.ds(pl.multiple_of(j * TILE, TILE), TILE)
            acc[...] += mm(nrm[j], wbuf[h, rows, :])
            return carry

        lax.fori_loop(first, last, project, 0)

    def attend_head(h):
        query = jnp.concatenate(
            [rotate(acc[:, g * HEAD : (g + 1) * HEAD], sine) for g in range(GROUP)], 0
        ).astype(BF16)
        key = rotate(acc[:, GROUP * HEAD : (GROUP + 1) * HEAD], sine).astype(BF16)
        value = acc[:, (GROUP + 1) * HEAD :].astype(BF16)
        factor = HEAD**-0.5
        scores = mm(query, key, NT) * factor + bias
        exp_terms = jnp.exp(scores - jnp.max(scores, -1, keepdims=True))
        probs = exp_terms / jnp.sum(exp_terms, -1, keepdims=True)
        probs_low = probs.astype(BF16)
        mixed = mm(probs_low, value).astype(BF16)
        cot = cot_home[h]
        grad_out = jnp.concatenate(
            [cot[:, g * HEAD : (g + 1) * HEAD] for g in range(GROUP)], 0
        )
        grad_value = mm(probs_low, grad_out, TN)
        grad_probs = mm(grad_out, value, NT)
        centre = jnp.sum(grad_probs * probs, -1, keepdims=True)
        grad_scores = (probs * (grad_probs - centre) * factor).astype(BF16)
        grad_query = mm(grad_scores, key)
        grad_key = rotate(mm(grad_scores, query, TN), -sine)
        attn = jnp.concatenate(
            [mixed[g * TOK_DEV : (g + 1) * TOK_DEV] for g in range(GROUP)], 1
        )
        out_send[h] = (
            mm(cut(home_plan, TOK_DEV), attn).astype(BF16).reshape(4, MAXLEN, TILE)
        )
        for e in range(4):
            out_copy(h, e).start()
        gvbuf[h, my_tokens, :] = grad_value.astype(BF16)
        grads = jnp.concatenate(
            [
                rotate(grad_query[g * TOK_DEV : (g + 1) * TOK_DEV], -sine).T
                for g in range(GROUP)
            ]
            + [grad_key.T, grad_value.T],
            0,
        )
        grads_t[...] = grads.astype(BF16)
        begin(g_view, g_sems, h)

    def back_head(h):
        def back(j, carry):
            rows = pl.ds(pl.multiple_of(j * TILE, TILE), TILE)
            pacc[j] += mm(wbuf[h, rows, :], grads_t[...])
            return carry

        lax.fori_loop(0, TILES, back, 0)

    def round_of(h, carry):
        for k in range(1, early + 1):

            @pl.when(h < kh)
            def _():
                step(w_view, w_sems, h, early + k)

            @pl.when((h >= 2) & (h < kh))
            def _():
                step(g_view, g_sems, h - 2, 2 * k - 1)
                step(g_view, g_sems, h - 2, 2 * k)

            if k == 1:

                @pl.when(h >= 1)
                def _():
                    gathered(w_view, w_sems, h - 1)
                    acc[...] = jnp.zeros_like(acc)
                    project_head(h - 1, 0, TILES // 2)

            if k == 2:

                @pl.when(h >= 1)
                def _():
                    attend_head(h - 1)

            @pl.when(h + 1 < kh)
            def _():
                step(w_view, w_sems, h + 1, k)

            if k == 1:

                @pl.when(h >= 1)
                def _():
                    project_head(h - 1, TILES // 2, TILES)

            if k == 2:

                @pl.when(h >= 1)
                def _():
                    back_head(h - 1)

        @pl.when(h == 1)
        def _():
            share_rows()

        return carry

    lax.fori_loop(0, kh + 1, round_of, 0)

    last = range(max(kh - 2, 0), kh)
    dots = jnp.zeros((TOK_DEV, 1), F32)
    for j in range(TILES):
        low = pacc[j].T.astype(BF16)
        psend[j] = low
        dots = dots + jnp.sum(
            low.astype(F32) * gbuf[j, 0:1, :] * hid[j].astype(F32), 1, keepdims=True
        )
    rsend[...] = jnp.broadcast_to(dots, (TOK_DEV, HEAD))
    term_copies = []
    for j in range(1, nt):
        to = lax.rem(t + j, nt)
        peer = {"tensor": to}
        term_copies.append(
            remote(
                psend.at[pl.ds(to * tp, tp)], precv.at[j - 1], psems.at[j], prems.at[j], peer
            )
        )
        term_copies.append(remote(rsend, rrecv.at[j - 1], rsems.at[j], rrems.at[j], peer))
    for copy in term_copies:
        copy.start()
    def place_out(h):
        for e in range(4):
            out_copy(h, e).wait()
        arrived = out_recv[h].reshape(4 * MAXLEN, TILE)
        out_ref[:, h * TILE : (h + 1) * TILE] = mm(uncut(dest_plan, CAP), arrived).astype(BF16)

    for k in range(1, zs + 1):
        for h in last:
            step(g_view, g_sems, h, k)
        if k <= kh:
            place_out(k - 1)
    for copy in term_copies:
        copy.wait()
    row_dot = rsend[:, 0:1]
    for j in range(1, nt):
        row_dot = row_dot + rrecv[j - 1, :, 0:1]
    for i in range(tp):
        summed = psend[t * tp + i].astype(F32)
        for j in range(1, nt):
            summed = summed + precv[j - 1, i].astype(F32)
        weighted = summed * gbuf[t * tp + i, 0:1, :]
        gh_ref[:, i * TILE : (i + 1) * TILE] = (
            inverse_rms * weighted
            - hid[t * tp + i].astype(F32) * inverse_rms**3 * row_dot * (1.0 / D)
        ).astype(BF16)

    for j in range(1, nt):
        share_copy(j, t).wait_send()
        share_copy(j, lax.rem(t - j + nt, nt)).wait_recv()
    for h in range(kh):
        gathered(g_view, g_sems, h)
    gvw_acc[...] = jnp.zeros_like(gvw_acc)

    def weigh(c, carry):
        rows = pl.ds(pl.multiple_of(c * TILE, TILE), TILE)
        owners = pl.ds(c * (TILE // TOK_DEV), TILE // TOK_DEV)
        columns = ncol[owners].reshape(TILE, blk)
        values = jnp.concatenate([gvbuf[h, rows, :] for h in range(kh)], 1)
        gvw_acc[...] += mm(columns, values, TN)
        return carry

    lax.fori_loop(0, n * TOK_DEV // TILE, weigh, 0)
    gvw_ref[...] = gvw_acc[...]

    def finish(h, carry):
        drained(w_view, w_sems, h)
        drained(g_view, g_sems, h)
        return carry

    lax.fori_loop(0, kh, finish, 0)


def split_kernel(
    n,
    nt,
    seq_length,
    home_offset,
    dest_shard,
    dest_offset,
    hidden,
    gain,
    freq,
    cotangent,
    w_query,
    w_key,
    w_value,
    out_ref,
    gh_ref,
    gvw_ref,
    wbuf,
    hid,
    gbuf,
    cosines,
    sines,
    biases,
    cot_across,
    attn_out,
    attn_in,
    pxs,
    pxr,
    nblk,
    ncol,
    cot_send,
    cot_recv,
    cot_home,
    acc,
    grads_t,
    pacc,
    psend,
    precv,
    rsend,
    rrecv,
    gvbuf,
    out_send,
    out_recv,
    gvw_acc,
    load_sem,
    wzs,
    wzr,
    wxs,
    wxr,
    wss,
    wsr,
    gzs,
    gzr,
    gxs,
    gxr,
    gss,
    gsr,
    ysend,
    yrecv,
    ysends,
    yrecvs,
    qsend,
    qrecv,
    hsend,
    hrecv,
    bsend,
    brecv,
    csend,
    crecv,
    asend,
    arecv,
    osend,
    orecv,
    psems,
    prems,
    rsems,
    rrems,
):
    me = lax.axis_index("dp")
    t = lax.axis_index("tensor")
    kh = gvbuf.shape[0]
    hh = kh // 2
    blk = D // n
    tp = TILES // nt
    zs = n // 4
    core = lax.rem(me, 2)
    chip = lax.div(me, 2)
    z, x = lax.div(chip, 2), lax.rem(chip, 2)
    sibling = me + 1 - 2 * core
    across = me + 2 - 4 * x
    spot = 4 * z + 2 * core + x
    other_spot = spot + 1 - 2 * x
    strides = [n - 1, 1, n // 2, n // 2 + 1]

    barrier = pltpu.get_barrier_semaphore()

    def greet(j, carry):
        pl.semaphore_signal(
            barrier,
            inc=1,
            device_id={"dp": lax.rem(me + j, n)},
            device_id_type=pl.DeviceIdType.MESH,
        )
        return carry

    lax.fori_loop(1, n, greet, 0)
    for j in range(1, nt):
        pl.semaphore_signal(
            barrier,
            inc=1,
            device_id={"tensor": lax.rem(t + j, nt)},
            device_id_type=pl.DeviceIdType.MESH,
        )

    def remote(src, dst, ssem, rsem, where):
        return pltpu.make_async_remote_copy(
            src_ref=src,
            dst_ref=dst,
            send_sem=ssem,
            recv_sem=rsem,
            device_id=where,
            device_id_type=pl.DeviceIdType.MESH,
        )

    def shard_parts(h, which):
        head = which * hh + h
        for part, (src, first, width) in enumerate(
            (
                (w_query, 0, GROUP * HEAD),
                (w_key, GROUP * HEAD, HEAD),
                (w_value, (GROUP + 1) * HEAD, HEAD),
            )
        ):
            yield part, src.at[:, pl.ds(pl.multiple_of(head * width, width), width)], pl.ds(
                first, width
            )

    def rows_at(where):
        return pl.ds(pl.multiple_of(where * blk, blk), blk)

    def loads_of(h):
        return [
            pltpu.make_async_copy(src, wbuf.at[h, rows_at(spot), cols], load_sem.at[h, part])
            for part, src, cols in shard_parts(h, x)
        ]

    def swaps_of(h, where):
        return [
            remote(
                src,
                wbuf.at[h, rows_at(where), cols],
                wxs.at[h, part],
                wxr.at[h, part],
                {"dp": across},
            )
            for part, src, cols in shard_parts(h, 1 - x)
        ]

    for h in range(hh):
        for load in loads_of(h):
            load.start()

    for i in range(tp):
        hid[t * tp + i] = hidden[:, i * TILE : (i + 1) * TILE]
        gbuf[t * tp + i] = jnp.broadcast_to(gain[:, i * TILE : (i + 1) * TILE], (8, TILE))

    pl.semaphore_wait(barrier, n - 1 + nt - 1)

    for h in range(hh):
        for swap in swaps_of(h, spot):
            swap.start()

    own_tiles = pl.ds(t * tp, tp)
    tensor_copies = []
    for j in range(1, nt):
        peer = {"tensor": lax.rem(t + j, nt)}
        tensor_copies.append(
            remote(hid.at[own_tiles], hid.at[own_tiles], hsend.at[j, 0], hrecv.at[j, 0], peer)
        )
        tensor_copies.append(
            remote(gbuf.at[own_tiles], gbuf.at[own_tiles], hsend.at[j, 1], hrecv.at[j, 1], peer)
        )
    for copy in tensor_copies:
        copy.start()

    def w_view(h, zz, xx, which):
        rows = pl.multiple_of((4 * zz + 2 * which) * blk, 2 * blk)
        return wbuf.at[h, pl.ds(rows, 2 * blk)]

    def g_view(h, zz, xx, which):
        rows = pl.multiple_of((4 * zz + 2 * which) * TOK_DEV, 2 * TOK_DEV)
        return gvbuf.at[xx * hh + h, pl.ds(rows, 2 * TOK_DEV)]

    up, down = lax.rem(me + 4, n), lax.rem(me - 4 + n, n)

    def z_copy(view, sems, h, way, zz):
        block = view(h, zz, x, core)
        return remote(
            block,
            block,
            sems[0].at[h, way, zz],
            sems[1].at[h, zz],
            {"dp": up if way == 0 else down},
        )

    def x_copy(view, sems, h, zz, xx):
        block = view(h, zz, xx, core)
        return remote(block, block, sems[2].at[h, zz], sems[3].at[h, zz], {"dp": across})

    def s_copy(view, sems, h, zz, xx, which):
        block = view(h, zz, xx, which)
        return remote(
            block, block, sems[4].at[h, xx, zz], sems[5].at[h, xx, zz], {"dp": sibling}
        )

    def begin(view, sems, h):
        @pl.when(z < zs - 1)
        def _():
            z_copy(view, sems, h, 0, z).start()

        @pl.when(z > 0)
        def _():
            z_copy(view, sems, h, 1, z).start()

        if sems is g_sems:
            x_copy(view, sems, h, z, x).start()
        s_copy(view, sems, h, z, x, core).start()

    def step(view, sems, h, k):
        if k < zs:

            @pl.when(z >= k)
            def _():
                zz = z - k
                z_copy(view, sems, h, 0, zz).wait_recv()

                @pl.when(z < zs - 1)
                def _():
                    z_copy(view, sems, h, 0, zz).start()

                if sems is g_sems:
                    x_copy(view, sems, h, zz, x).start()
                s_copy(view, sems, h, zz, x, core).start()

            @pl.when(z + k < zs)
            def _():
                zz = z + k
                z_copy(view, sems, h, 1, zz).wait_recv()

                @pl.when(z > 0)
                def _():
                    z_copy(view, sems, h, 1, zz).start()

                if sems is g_sems:
                    x_copy(view, sems, h, zz, x).start()
                s_copy(view, sems, h, zz, x, core).start()

        if sems is w_sems:
            return

        def from_across(zz):
            x_copy(view, sems, h, zz, 1 - x).wait_recv()
            s_copy(view, sems, h, zz, 1 - x, core).start()

        if k == 1:
            from_across(z)
        else:

            @pl.when(z >= k - 1)
            def _():
                from_across(z - k + 1)

            @pl.when(z + k - 1 < zs)
            def _():
                from_across(z + k - 1)

    def gathered(view, sems, h):
        def one(zz, carry):
            s_copy(view, sems, h, zz, x, 1 - core).wait_recv()
            if sems is g_sems:
                s_copy(view, sems, h, zz, 1 - x, 1 - core).wait_recv()
            return carry

        lax.fori_loop(0, zs, one, 0)

    def drained(view, sems, h):
        def one(zz, carry):
            s_copy(view, sems, h, zz, x, core).wait_send()
            if sems is g_sems:
                s_copy(view, sems, h, zz, 1 - x, core).wait_send()
                x_copy(view, sems, h, zz, x).wait_send()

            @pl.when((zz <= z) & (z < zs - 1))
            def _():
                z_copy(view, sems, h, 0, zz).wait_send()

            @pl.when((zz >= z) & (z > 0))
            def _():
                z_copy(view, sems, h, 1, zz).wait_send()

            return carry

        lax.fori_loop(0, zs, one, 0)

    w_sems = (wzs, wzr, None, None, wss, wsr)
    g_sems = (gzs, gzr, gxs, gxr, gss, gsr)
    early = zs // 2
    def begin_weights(h):
        for load in loads_of(h):
            load.wait()
        for swap in swaps_of(h, other_spot):
            swap.wait_recv()
        begin(w_view, w_sems, h)

    begin_weights(0)

    def picked(table, row, target, slot):
        total = jnp.int32(0)
        for c in range(4):
            total = total + jnp.where(dest_shard[row, c] == target, table[row, c], 0)
        return total

    home_plan, dest_plan, across_plan = [], [], []
    for stride in strides:
        target = lax.rem(across + stride, n)
        across_plan.append(
            (
                picked(home_offset, across, target, 0),
                picked(seq_length, across, target, 0),
            )
        )
        target = lax.rem(me + stride, n)
        source = lax.rem(me - stride + n, n)
        home_plan.append(
            (picked(home_offset, me, target, 0), picked(seq_length, me, target, 0))
        )
        dest_plan.append(
            (picked(dest_offset, source, me, 0), picked(seq_length, source, me, 0))
        )

    def cut(plan, rows):
        w = lax.broadcasted_iota(jnp.int32, (MAXLEN, rows), 0)
        r = lax.broadcasted_iota(jnp.int32, (MAXLEN, rows), 1)
        return jnp.concatenate(
            [
                jnp.where((w < length) & (r == start + w), 1.0, 0.0)
                for start, length in plan
            ],
            0,
        ).astype(BF16)

    def uncut(plan, rows):
        place = lax.broadcasted_iota(jnp.int32, (rows, 4 * MAXLEN), 1)
        r = lax.broadcasted_iota(jnp.int32, (rows, 4 * MAXLEN), 0)
        total = jnp.zeros((rows, 4 * MAXLEN), F32)
        for e, (start, length) in enumerate(plan):
            w = place - e * MAXLEN
            total = jnp.where((w >= 0) & (w < length) & (r == start + w), 1.0, total)
        return total.astype(BF16)

    picks = cut(dest_plan, CAP)
    for i in range(tp):
        columns = slice(i * TILE, (i + 1) * TILE)
        cot_send[:, :, columns] = (
            mm(picks, cotangent[:, columns]).astype(BF16).reshape(4, MAXLEN, TILE)
        )
    cot_copies = [
        remote(
            cot_send.at[e],
            cot_recv.at[e],
            csend.at[e],
            crecv.at[e],
            {"dp": lax.rem(me - strides[e] + n, n)},
        )
        for e in range(4)
    ]
    for copy in cot_copies:
        copy.start()
    for h in range(1, hh):
        begin_weights(h)
    for k in range(1, early):
        step(w_view, w_sems, 0, k)

    for copy in tensor_copies:
        copy.wait_send()
    for j in range(1, nt):
        theirs = pl.ds(lax.rem(t - j + nt, nt) * tp, tp)
        peer = {"tensor": lax.rem(t + j, nt)}
        remote(hid.at[theirs], hid.at[theirs], hsend.at[j, 0], hrecv.at[j, 0], peer).wait_recv()
        remote(gbuf.at[theirs], gbuf.at[theirs], hsend.at[j, 1], hrecv.at[j, 1], peer).wait_recv()
    squares = jnp.zeros((TOK_DEV, 1), F32)
    for j in range(TILES):
        values = hid[j].astype(F32)
        squares = squares + jnp.sum(values * values, 1, keepdims=True)
    inverse_rms = lax.rsqrt(squares * (1.0 / D) + EPSILON)
    for j in range(TILES):
        rows = (hid[j].astype(F32) * inverse_rms * gbuf[j, 0:1, :]).astype(BF16)
        for i in range(TILE // blk):
            nblk[x, j * (TILE // blk) + i] = rows[:, i * blk : (i + 1) * blk]
    row_swap = remote(nblk.at[x], nblk.at[x], qsend.at[0], qrecv.at[0], {"dp": across})
    row_swap.start()
    share = TOK_DEV // nt
    my_share = pl.ds(pl.multiple_of(t * share, share), share)

    def norm_copy(j, src, dst):
        return remote(
            nblk.at[x, src, my_share],
            ncol.at[dst, my_share],
            bsend.at[j],
            brecv.at[j],
            {"dp": lax.rem(me + j, n)},
        )

    def norm_start(j, carry):
        norm_copy(j, lax.rem(me + j, n), spot).start()
        return carry

    lax.fori_loop(1, n, norm_start, 0)
    ncol[spot, my_share, :] = nblk[x, me, my_share, :]

    def share_copy(j, shard):
        rows = pl.ds(pl.multiple_of(shard * share, share), share)
        block = ncol.at[:, rows]
        return remote(
            block, block, ysend.at[j], yrecv.at[j], {"tensor": lax.rem(t + j, nt)}
        )

    def share_rows():
        def norm_wait(j, carry):
            sender = lax.rem(me - j + n, n)
            side = lax.rem(sender, 4)
            where = sender - side + 2 * lax.rem(side, 2) + lax.div(side, 2)
            norm_copy(j, lax.rem(me + j, n), where).wait_recv()
            norm_copy(j, lax.rem(me + j, n), spot).wait_send()
            return carry

        lax.fori_loop(1, n, norm_wait, 0)
        for j in range(1, nt):
            share_copy(j, t).start()

    step(w_view, w_sems, 0, early)

    row = lax.broadcasted_iota(jnp.int32, (TOK_DEV, TOK_DEV), 0)
    col = lax.broadcasted_iota(jnp.int32, (TOK_DEV, TOK_DEV), 1)

    def tables(plan):
        row_start = jnp.zeros((TOK_DEV, TOK_DEV), jnp.int32)
        col_start = jnp.zeros((TOK_DEV, TOK_DEV), jnp.int32)
        for start, length in plan:
            row_start = jnp.where((row >= start) & (row < start + length), start, row_start)
            col_start = jnp.where((col >= start) & (col < start + length), start, col_start)
        bias = jnp.where((row_start == col_start) & (col <= row), 0.0, -1e30).astype(F32)
        angles = (row - row_start).astype(F32) * freq[0:1, :]
        sine = jnp.sin(angles) * jnp.where(col < HEAD // 2, -1.0, 1.0)
        return jnp.cos(angles), sine, jnp.concatenate([bias] * GROUP, 0)

    for side, plan in enumerate((home_plan, across_plan)):
        cosines[side], sines[side], biases[side] = tables(plan)

    def rotate(values, cosine, sine_part):
        return values * cosine + pltpu.roll(values, HEAD // 2, 1) * sine_part

    for copy in cot_copies:
        copy.wait()
    picks = uncut(home_plan, TOK_DEV)
    for h in range(kh):
        arrived = cot_recv[:, :, h * TILE : (h + 1) * TILE].reshape(4 * MAXLEN, TILE)
        cot_home[h] = mm(picks, arrived).astype(BF16)

    cot_swap = remote(
        cot_home.at[pl.ds((1 - x) * hh, hh)], cot_across, qsend.at[1], qrecv.at[1], {"dp": across}
    )
    cot_swap.start()

    for j in range(n):
        pacc[j] = jnp.zeros((blk, 2 * TOK_DEV), F32)
    cot_swap.wait()
    row_swap.wait()

    def out_copy(h, e):
        return remote(
            out_send.at[h, e],
            out_recv.at[h, e],
            osend.at[h, e],
            orecv.at[h, e],
            {"dp": lax.rem(me + strides[e], n)},
        )

    def project_head(h, first, last):
        def project(j, carry):
            side = lax.rem(j, 4)
            shard = j - side + 2 * lax.rem(side, 2) + lax.div(side, 2)
            rows = pl.ds(pl.multiple_of(j * blk, blk), blk)
            both = jnp.concatenate([nblk[x, shard], nblk[1 - x, shard]], 0)
            acc[...] += mm(both, wbuf[h, rows, :])
            return carry

        lax.fori_loop(first, last, project, 0)

    def attn_copy(h):
        return remote(
            attn_out.at[h], attn_in.at[h], ysends.at[h], yrecvs.at[h], {"dp": across}
        )

    def send_out(head, attn):
        out_send[head] = (
            mm(cut(home_plan, TOK_DEV), attn).astype(BF16).reshape(4, MAXLEN, TILE)
        )
        for e in range(4):
            out_copy(head, e).start()

    def attend_side(h, side, where):
        first = side * TOK_DEV
        rows = slice(first, first + TOK_DEV)
        cosine, sine = cosines[side], sines[side]
        query = jnp.concatenate(
            [
                rotate(acc[rows, g * HEAD : (g + 1) * HEAD], cosine, sine)
                for g in range(GROUP)
            ],
            0,
        ).astype(BF16)
        key = rotate(acc[rows, GROUP * HEAD : (GROUP + 1) * HEAD], cosine, sine).astype(BF16)
        value = acc[rows, (GROUP + 1) * HEAD :].astype(BF16)
        factor = HEAD**-0.5
        scores = mm(query, key, NT) * factor + biases[side]
        exp_terms = jnp.exp(scores - jnp.max(scores, -1, keepdims=True))
        probs = exp_terms / jnp.sum(exp_terms, -1, keepdims=True)
        probs_low = probs.astype(BF16)
        mixed = mm(probs_low, value).astype(BF16)
        cot = cot_home[x * hh + h] if side == 0 else cot_across[h]
        grad_out = jnp.concatenate(
            [cot[:, g * HEAD : (g + 1) * HEAD] for g in range(GROUP)], 0
        )
        grad_value = mm(probs_low, grad_out, TN)
        grad_probs = mm(grad_out, value, NT)
        centre = jnp.sum(grad_probs * probs, -1, keepdims=True)
        grad_scores = (probs * (grad_probs - centre) * factor).astype(BF16)
        grad_query = mm(grad_scores, key)
        grad_key = rotate(mm(grad_scores, query, TN), cosine, -sine)
        attn = jnp.concatenate(
            [mixed[g * TOK_DEV : (g + 1) * TOK_DEV] for g in range(GROUP)], 1
        )
        if side == 0:
            send_out(x * hh + h, attn)
        else:
            attn_out[h] = attn
            attn_copy(h).start()
        tokens = pl.ds(pl.multiple_of(where * TOK_DEV, TOK_DEV), TOK_DEV)
        gvbuf[x * hh + h, tokens, :] = grad_value.astype(BF16)
        grads = jnp.concatenate(
            [
                rotate(grad_query[g * TOK_DEV : (g + 1) * TOK_DEV], cosine, -sine).T
                for g in range(GROUP)
            ]
            + [grad_key.T, grad_value.T],
            0,
        )
        grads_t[:, rows] = grads.astype(BF16)

    def attend_head(h):
        attend_side(h, 1, other_spot)
        attend_side(h, 0, spot)
        begin(g_view, g_sems, h)

    def from_other(h):
        attn_copy(h).wait()
        send_out((1 - x) * hh + h, attn_in[h])

    def back_head(h):
        def back(j, carry):
            rows = pl.ds(pl.multiple_of(j * blk, blk), blk)
            pacc[j] += mm(wbuf[h, rows, :], grads_t[...])
            return carry

        lax.fori_loop(0, n, back, 0)

    def round_of(h, carry):
        for k in range(1, early + 1):

            @pl.when(h < hh)
            def _():
                step(w_view, w_sems, h, early + k)

            @pl.when((h >= 2) & (h < hh))
            def _():
                step(g_view, g_sems, h - 2, 2 * k - 1)
                step(g_view, g_sems, h - 2, 2 * k)

            if k == 1:

                @pl.when(h >= 1)
                def _():
                    gathered(w_view, w_sems, h - 1)
                    acc[...] = jnp.zeros_like(acc)
                    project_head(h - 1, 0, n // 2)

            if k == 2:

                @pl.when(h >= 1)
                def _():
                    attend_head(h - 1)

            @pl.when(h + 1 < hh)
            def _():
                step(w_view, w_sems, h + 1, k)

            if k == 1:

                @pl.when(h >= 1)
                def _():
                    project_head(h - 1, n // 2, n)

            if k == 2:

                @pl.when(h >= 1)
                def _():
                    back_head(h - 1)

        @pl.when(h >= 2)
        def _():
            from_other(h - 2)

        @pl.when(h == 1)
        def _():
            share_rows()

        return carry

    lax.fori_loop(0, hh + 1, round_of, 0)

    last = range(max(hh - 2, 0), hh)
    for j in range(n):
        pxs[j] = pacc[j, :, TOK_DEV:].astype(BF16)
    half_swap = remote(pxs, pxr, qsend.at[2], qrecv.at[2], {"dp": across})
    half_swap.start()
    from_other(hh - 1)
    for h in last:
        step(g_view, g_sems, h, 1)
    half_swap.wait()
    for j in range(n):
        total = pacc[j, :, :TOK_DEV] + pxr[j].astype(F32)
        shard = j - j % 4 + 2 * (j % 2) + (j % 4) // 2
        first = shard * blk % TILE
        psend[shard * blk // TILE, :, first : first + blk] = total.T.astype(BF16)
    dots = jnp.zeros((TOK_DEV, 1), F32)
    for j in range(TILES):
        low = psend[j]
        dots = dots + jnp.sum(
            low.astype(F32) * gbuf[j, 0:1, :] * hid[j].astype(F32), 1, keepdims=True
        )
    rsend[...] = jnp.broadcast_to(dots, (TOK_DEV, HEAD))
    term_copies = []
    for j in range(1, nt):
        to = lax.rem(t + j, nt)
        peer = {"tensor": to}
        term_copies.append(
            remote(
                psend.at[pl.ds(to * tp, tp)], precv.at[j - 1], psems.at[j], prems.at[j], peer
            )
        )
        term_copies.append(remote(rsend, rrecv.at[j - 1], rsems.at[j], rrems.at[j], peer))
    for copy in term_copies:
        copy.start()
    def place_out(h):
        for e in range(4):
            out_copy(h, e).wait()
        arrived = out_recv[h].reshape(4 * MAXLEN, TILE)
        out_ref[:, h * TILE : (h + 1) * TILE] = mm(uncut(dest_plan, CAP), arrived).astype(BF16)

    for k in range(1, zs + 1):
        for h in last:
            if k > 1:
                step(g_view, g_sems, h, k)
        if k <= kh:
            place_out(k - 1)
    for copy in term_copies:
        copy.wait()
    row_dot = rsend[:, 0:1]
    for j in range(1, nt):
        row_dot = row_dot + rrecv[j - 1, :, 0:1]
    for i in range(tp):
        summed = psend[t * tp + i].astype(F32)
        for j in range(1, nt):
            summed = summed + precv[j - 1, i].astype(F32)
        weighted = summed * gbuf[t * tp + i, 0:1, :]
        gh_ref[:, i * TILE : (i + 1) * TILE] = (
            inverse_rms * weighted
            - hid[t * tp + i].astype(F32) * inverse_rms**3 * row_dot * (1.0 / D)
        ).astype(BF16)

    for j in range(1, nt):
        share_copy(j, t).wait_send()
        share_copy(j, lax.rem(t - j + nt, nt)).wait_recv()
    for h in range(hh):
        gathered(g_view, g_sems, h)
    gvw_acc[...] = jnp.zeros_like(gvw_acc)

    def weigh(c, carry):
        rows = pl.ds(pl.multiple_of(c * TILE, TILE), TILE)
        owners = pl.ds(c * (TILE // TOK_DEV), TILE // TOK_DEV)
        columns = ncol[owners].reshape(TILE, blk)
        values = jnp.concatenate([gvbuf[h, rows, :] for h in range(kh)], 1)
        gvw_acc[...] += mm(columns, values, TN)
        return carry

    lax.fori_loop(0, n * TOK_DEV // TILE, weigh, 0)
    gvw_ref[...] = gvw_acc[...]

    def finish(h, carry):
        drained(w_view, w_sems, h)
        drained(g_view, g_sems, h)
        return carry

    lax.fori_loop(0, hh, finish, 0)
    for h in range(hh):
        for swap in swaps_of(h, spot):
            swap.wait_send()


def on_device(
    hidden,
    gain,
    w_query,
    w_key,
    w_value,
    cotangent,
    seq_length,
    home_offset,
    dest_shard,
    dest_offset,
):
    n = lax.axis_size("dp")
    nt = lax.axis_size("tensor")
    kh = w_key.shape[1] // HEAD
    width = hidden.shape[1]
    blk = D // n
    tp = TILES // nt
    zs = n // 4
    half = HEAD // 2
    exponent = jnp.arange(half, dtype=F32) * (2.0 / HEAD)
    inverse = jnp.power(jnp.float32(ROPE_BASE), -exponent)
    freq = jnp.broadcast_to(jnp.concatenate([inverse, inverse])[None, :], (8, HEAD))
    dma = pltpu.SemaphoreType.DMA
    vmem = pl.BlockSpec(memory_space=pltpu.VMEM)
    smem = pl.BlockSpec(memory_space=pltpu.SMEM)
    anywhere = pl.BlockSpec(memory_space=pl.ANY)
    return pl.pallas_call(
        functools.partial(kernel, n, nt),
        out_shape=(
            jax.ShapeDtypeStruct((CAP, width), BF16),
            jax.ShapeDtypeStruct((TOK_DEV, width), BF16),
            jax.ShapeDtypeStruct((blk, kh * HEAD), F32),
        ),
        in_specs=[smem] * 4 + [vmem] * 4 + [anywhere] * 3,
        out_specs=(vmem, vmem, vmem),
        scratch_shapes=[
            pltpu.VMEM((kh, D, HEAD_COLS), BF16),
            pltpu.VMEM((TILES, TOK_DEV, TILE), BF16),
            pltpu.VMEM((TILES, 8, TILE), F32),
            pltpu.VMEM((TILES, TOK_DEV, TILE), BF16),
            pltpu.VMEM((n, TOK_DEV, blk), BF16),
            pltpu.VMEM((n, TOK_DEV, blk), BF16),
            pltpu.VMEM((4, MAXLEN, width), BF16),
            pltpu.VMEM((4, MAXLEN, width), BF16),
            pltpu.VMEM((kh, TOK_DEV, TILE), BF16),
            pltpu.VMEM((TOK_DEV, HEAD_COLS), F32),
            pltpu.VMEM((HEAD_COLS, TOK_DEV), BF16),
            pltpu.VMEM((TILES, TILE, TOK_DEV), F32),
            pltpu.VMEM((TILES, TOK_DEV, TILE), BF16),
            pltpu.VMEM((nt - 1, tp, TOK_DEV, TILE), BF16),
            pltpu.VMEM((TOK_DEV, HEAD), F32),
            pltpu.VMEM((nt - 1, TOK_DEV, HEAD), F32),
            pltpu.VMEM((kh, n * TOK_DEV, HEAD), BF16),
            pltpu.VMEM((kh, 4, MAXLEN, TILE), BF16),
            pltpu.VMEM((kh, 4, MAXLEN, TILE), BF16),
            pltpu.VMEM((blk, kh * HEAD), F32),
            dma((kh, 3)),
            dma((kh, 2, zs)),
            dma((kh, zs)),
            dma((kh, zs)),
            dma((kh, zs)),
            dma((kh, 2, zs)),
            dma((kh, 2, zs)),
            dma((kh, 2, zs)),
            dma((kh, zs)),
            dma((kh, zs)),
            dma((kh, zs)),
            dma((kh, 2, zs)),
            dma((kh, 2, zs)),
            dma((nt,)),
            dma((nt,)),
            dma((nt, 2)),
            dma((nt, 2)),
            dma((n,)),
            dma((n,)),
            dma((4,)),
            dma((4,)),
            dma((4,)),
            dma((4,)),
            dma((kh, 4)),
            dma((kh, 4)),
            dma((nt,)),
            dma((nt,)),
            dma((nt,)),
            dma((nt,)),
        ],
        compiler_params=pltpu.CompilerParams(
            collective_id=0, has_side_effects=True, vmem_limit_bytes=56 * 1024 * 1024
        ),
        cost_estimate=pl.CostEstimate(
            flops=8 * 10**9, bytes_accessed=8 * 10**6, transcendentals=10**6
        ),
    )(
        seq_length,
        home_offset,
        dest_shard,
        dest_offset,
        hidden,
        gain.astype(F32)[None, :],
        freq,
        cotangent,
        w_query,
        w_key,
        w_value,
    )


def on_split_device(
    hidden,
    gain,
    w_query,
    w_key,
    w_value,
    cotangent,
    seq_length,
    home_offset,
    dest_shard,
    dest_offset,
):
    n = lax.axis_size("dp")
    nt = lax.axis_size("tensor")
    kh = w_key.shape[1] // HEAD
    hh = kh // 2
    width = hidden.shape[1]
    blk = D // n
    tp = TILES // nt
    zs = n // 4
    half = HEAD // 2
    exponent = jnp.arange(half, dtype=F32) * (2.0 / HEAD)
    inverse = jnp.power(jnp.float32(ROPE_BASE), -exponent)
    freq = jnp.broadcast_to(jnp.concatenate([inverse, inverse])[None, :], (8, HEAD))
    dma = pltpu.SemaphoreType.DMA
    vmem = pl.BlockSpec(memory_space=pltpu.VMEM)
    smem = pl.BlockSpec(memory_space=pltpu.SMEM)
    anywhere = pl.BlockSpec(memory_space=pl.ANY)
    return pl.pallas_call(
        functools.partial(split_kernel, n, nt),
        out_shape=(
            jax.ShapeDtypeStruct((CAP, width), BF16),
            jax.ShapeDtypeStruct((TOK_DEV, width), BF16),
            jax.ShapeDtypeStruct((blk, kh * HEAD), F32),
        ),
        in_specs=[smem] * 4 + [vmem] * 4 + [anywhere] * 3,
        out_specs=(vmem, vmem, vmem),
        scratch_shapes=[
            pltpu.VMEM((hh, D, HEAD_COLS), BF16),
            pltpu.VMEM((TILES, TOK_DEV, TILE), BF16),
            pltpu.VMEM((TILES, 8, TILE), F32),
            pltpu.VMEM((2, TOK_DEV, HEAD), F32),
            pltpu.VMEM((2, TOK_DEV, HEAD), F32),
            pltpu.VMEM((2, GROUP * TOK_DEV, TOK_DEV), F32),
            pltpu.VMEM((hh, TOK_DEV, TILE), BF16),
            pltpu.VMEM((hh, TOK_DEV, TILE), BF16),
            pltpu.VMEM((hh, TOK_DEV, TILE), BF16),
            pltpu.VMEM((n, blk, TOK_DEV), BF16),
            pltpu.VMEM((n, blk, TOK_DEV), BF16),
            pltpu.VMEM((2, n, TOK_DEV, blk), BF16),
            pltpu.VMEM((n, TOK_DEV, blk), BF16),
            pltpu.VMEM((4, MAXLEN, width), BF16),
            pltpu.VMEM((4, MAXLEN, width), BF16),
            pltpu.VMEM((kh, TOK_DEV, TILE), BF16),
            pltpu.VMEM((2 * TOK_DEV, HEAD_COLS), F32),
            pltpu.VMEM((HEAD_COLS, 2 * TOK_DEV), BF16),
            pltpu.VMEM((n, blk, 2 * TOK_DEV), F32),
            pltpu.VMEM((TILES, TOK_DEV, TILE), BF16),
            pltpu.VMEM((nt - 1, tp, TOK_DEV, TILE), BF16),
            pltpu.VMEM((TOK_DEV, HEAD), F32),
            pltpu.VMEM((nt - 1, TOK_DEV, HEAD), F32),
            pltpu.VMEM((kh, n * TOK_DEV, HEAD), BF16),
            pltpu.VMEM((kh, 4, MAXLEN, TILE), BF16),
            pltpu.VMEM((kh, 4, MAXLEN, TILE), BF16),
            pltpu.VMEM((blk, kh * HEAD), F32),
            dma((kh, 3)),
            dma((kh, 2, zs)),
            dma((kh, zs)),
            dma((kh, max(zs, 3))),
            dma((kh, max(zs, 3))),
            dma((kh, 2, zs)),
            dma((kh, 2, zs)),
            dma((kh, 2, zs)),
            dma((kh, zs)),
            dma((kh, zs)),
            dma((kh, zs)),
            dma((kh, 2, zs)),
            dma((kh, 2, zs)),
            dma((nt,)),
            dma((nt,)),
            dma((hh,)),
            dma((hh,)),
            dma((3,)),
            dma((3,)),
            dma((nt, 2)),
            dma((nt, 2)),
            dma((n,)),
            dma((n,)),
            dma((4,)),
            dma((4,)),
            dma((4,)),
            dma((4,)),
            dma((kh, 4)),
            dma((kh, 4)),
            dma((nt,)),
            dma((nt,)),
            dma((nt,)),
            dma((nt,)),
        ],
        compiler_params=pltpu.CompilerParams(
            collective_id=1, has_side_effects=True, vmem_limit_bytes=56 * 1024 * 1024
        ),
        cost_estimate=pl.CostEstimate(
            flops=8 * 10**9, bytes_accessed=8 * 10**6, transcendentals=10**6
        ),
    )(
        seq_length,
        home_offset,
        dest_shard,
        dest_offset,
        hidden,
        gain.astype(F32)[None, :],
        freq,
        cotangent,
        w_query,
        w_key,
        w_value,
    )


def solution(mesh):
    def chosen(*arrays):
        heads = arrays[3].shape[1] // HEAD
        return (on_split_device if heads % 2 == 0 else on_device)(*arrays)

    return jax.shard_map(
        chosen,
        mesh=mesh,
        in_specs=(
            P("dp", "tensor"),
            P("tensor"),
            P("dp", "tensor"),
            P("dp", "tensor"),
            P("dp", "tensor"),
            P("dp", "tensor"),
            P(),
            P(),
            P(),
            P(),
        ),
        out_specs=(P("dp", "tensor"), P("dp", "tensor"), P("dp", "tensor")),
        check_vma=False,
    )
```

```python
import functools
import math

import jax
import jax.numpy as jnp
from jax import lax
from jax.experimental import pallas as pl
from jax.experimental.pallas import tpu as pltpu
from jax.sharding import PartitionSpec as P

D = 4096
HEAD = 128
GROUP = 4
TOK_DEV = 128
MAXLEN = 64
CAP = 256
TILE = 512
TILES = D // TILE
HEAD_COLS = (GROUP + 2) * HEAD
EPSILON = 1e-05
ROPE_BASE = 500000.0
BF16 = jnp.bfloat16
F32 = jnp.float32
NN = (((1,), (0,)), ((), ()))
NT = (((1,), (1,)), ((), ()))
TN = (((0,), (0,)), ((), ()))


def mm(a, b, dims=NN):
    return lax.dot_general(a, b, dims, preferred_element_type=F32)


def kernel(
    n,
    nt,
    seq_length,
    home_offset,
    dest_shard,
    dest_offset,
    hidden,
    gain,
    freq,
    cotangent,
    w_query,
    w_key,
    w_value,
    out_ref,
    gh_ref,
    gvw_ref,
    wbuf,
    hid,
    gbuf,
    nrm,
    nblk,
    ncol,
    cot_send,
    cot_recv,
    cot_home,
    acc,
    grads_t,
    pacc,
    psend,
    precv,
    rsend,
    rrecv,
    gvbuf,
    out_send,
    out_recv,
    gvw_acc,
    load_sem,
    wzs,
    wzr,
    wxs,
    wxr,
    wss,
    wsr,
    gzs,
    gzr,
    gxs,
    gxr,
    gss,
    gsr,
    ysend,
    yrecv,
    hsend,
    hrecv,
    bsend,
    brecv,
    csend,
    crecv,
    asend,
    arecv,
    osend,
    orecv,
    psems,
    prems,
    rsems,
    rrems,
):
    me = lax.axis_index("dp")
    t = lax.axis_index("tensor")
    kh = wbuf.shape[0]
    blk = D // n
    tp = TILES // nt
    zs = n // 4
    core = lax.rem(me, 2)
    chip = lax.div(me, 2)
    z, x = lax.div(chip, 2), lax.rem(chip, 2)
    sibling = me + 1 - 2 * core
    strides = [n - 1, 1, n // 2, n // 2 + 1]

    barrier = pltpu.get_barrier_semaphore()

    def greet(j, carry):
        pl.semaphore_signal(
            barrier,
            inc=1,
            device_id={"dp": lax.rem(me + j, n)},
            device_id_type=pl.DeviceIdType.MESH,
        )
        return carry

    lax.fori_loop(1, n, greet, 0)
    for j in range(1, nt):
        pl.semaphore_signal(
            barrier,
            inc=1,
            device_id={"tensor": lax.rem(t + j, nt)},
            device_id_type=pl.DeviceIdType.MESH,
        )

    def remote(src, dst, ssem, rsem, where):
        return pltpu.make_async_remote_copy(
            src_ref=src,
            dst_ref=dst,
            send_sem=ssem,
            recv_sem=rsem,
            device_id=where,
            device_id_type=pl.DeviceIdType.MESH,
        )

    loads = []
    own_rows = pl.ds(pl.multiple_of(me * blk, blk), blk)
    for h in range(kh):
        for part, (src, first, width) in enumerate(
            (
                (w_query, 0, GROUP * HEAD),
                (w_key, GROUP * HEAD, HEAD),
                (w_value, (GROUP + 1) * HEAD, HEAD),
            )
        ):
            loads.append(
                pltpu.make_async_copy(
                    src.at[:, pl.ds(h * width, width)],
                    wbuf.at[h, own_rows, pl.ds(first, width)],
                    load_sem.at[h, part],
                )
            )
    for load in loads:
        load.start()

    for i in range(tp):
        hid[t * tp + i] = hidden[:, i * TILE : (i + 1) * TILE]
        gbuf[t * tp + i] = jnp.broadcast_to(gain[:, i * TILE : (i + 1) * TILE], (8, TILE))

    pl.semaphore_wait(barrier, n - 1 + nt - 1)

    own_tiles = pl.ds(t * tp, tp)
    tensor_copies = []
    for j in range(1, nt):
        peer = {"tensor": lax.rem(t + j, nt)}
        tensor_copies.append(
            remote(hid.at[own_tiles], hid.at[own_tiles], hsend.at[j, 0], hrecv.at[j, 0], peer)
        )
        tensor_copies.append(
            remote(gbuf.at[own_tiles], gbuf.at[own_tiles], hsend.at[j, 1], hrecv.at[j, 1], peer)
        )
    for copy in tensor_copies:
        copy.start()

    def w_view(h, zz, xx, which):
        rows = pl.multiple_of((4 * zz + 2 * xx + which) * blk, blk)
        return wbuf.at[h, pl.ds(rows, blk)]

    def g_view(h, zz, xx, which):
        rows = pl.multiple_of((4 * zz + 2 * xx + which) * TOK_DEV, TOK_DEV)
        return gvbuf.at[h, pl.ds(rows, TOK_DEV)]

    up, down = lax.rem(me + 4, n), lax.rem(me - 4 + n, n)
    across = me + 2 - 4 * x

    def z_copy(view, sems, h, way, zz):
        block = view(h, zz, x, core)
        return remote(
            block,
            block,
            sems[0].at[h, way, zz],
            sems[1].at[h, zz],
            {"dp": up if way == 0 else down},
        )

    def x_copy(view, sems, h, zz, xx):
        block = view(h, zz, xx, core)
        return remote(block, block, sems[2].at[h, zz], sems[3].at[h, zz], {"dp": across})

    def s_copy(view, sems, h, zz, xx, which):
        block = view(h, zz, xx, which)
        return remote(
            block, block, sems[4].at[h, xx, zz], sems[5].at[h, xx, zz], {"dp": sibling}
        )

    def begin(view, sems, h):
        @pl.when(z < zs - 1)
        def _():
            z_copy(view, sems, h, 0, z).start()

        @pl.when(z > 0)
        def _():
            z_copy(view, sems, h, 1, z).start()

        x_copy(view, sems, h, z, x).start()
        s_copy(view, sems, h, z, x, core).start()

    def step(view, sems, h, k):
        if k < zs:

            @pl.when(z >= k)
            def _():
                zz = z - k
                z_copy(view, sems, h, 0, zz).wait_recv()

                @pl.when(z < zs - 1)
                def _():
                    z_copy(view, sems, h, 0, zz).start()

                x_copy(view, sems, h, zz, x).start()
                s_copy(view, sems, h, zz, x, core).start()

            @pl.when(z + k < zs)
            def _():
                zz = z + k
                z_copy(view, sems, h, 1, zz).wait_recv()

                @pl.when(z > 0)
                def _():
                    z_copy(view, sems, h, 1, zz).start()

                x_copy(view, sems, h, zz, x).start()
                s_copy(view, sems, h, zz, x, core).start()

        def from_across(zz):
            x_copy(view, sems, h, zz, 1 - x).wait_recv()
            s_copy(view, sems, h, zz, 1 - x, core).start()

        if k == 1:
            from_across(z)
        else:

            @pl.when(z >= k - 1)
            def _():
                from_across(z - k + 1)

            @pl.when(z + k - 1 < zs)
            def _():
                from_across(z + k - 1)

    def gathered(view, sems, h):
        def one(zz, carry):
            s_copy(view, sems, h, zz, x, 1 - core).wait_recv()
            s_copy(view, sems, h, zz, 1 - x, 1 - core).wait_recv()
            return carry

        lax.fori_loop(0, zs, one, 0)

    def drained(view, sems, h):
        def one(zz, carry):
            s_copy(view, sems, h, zz, x, core).wait_send()
            s_copy(view, sems, h, zz, 1 - x, core).wait_send()
            x_copy(view, sems, h, zz, x).wait_send()

            @pl.when((zz <= z) & (z < zs - 1))
            def _():
                z_copy(view, sems, h, 0, zz).wait_send()

            @pl.when((zz >= z) & (z > 0))
            def _():
                z_copy(view, sems, h, 1, zz).wait_send()

            return carry

        lax.fori_loop(0, zs, one, 0)

    w_sems = (wzs, wzr, wxs, wxr, wss, wsr)
    g_sems = (gzs, gzr, gxs, gxr, gss, gsr)
    early = zs // 2
    for load in loads:
        load.wait()
    for h in range(kh):
        begin(w_view, w_sems, h)

    def picked(table, row, target, slot):
        total = jnp.int32(0)
        for c in range(4):
            total = total + jnp.where(dest_shard[row, c] == target, table[row, c], 0)
        return total

    home_plan, dest_plan = [], []
    for stride in strides:
        target = lax.rem(me + stride, n)
        source = lax.rem(me - stride + n, n)
        home_plan.append(
            (picked(home_offset, me, target, 0), picked(seq_length, me, target, 0))
        )
        dest_plan.append(
            (picked(dest_offset, source, me, 0), picked(seq_length, source, me, 0))
        )

    def cut(plan, rows):
        w = lax.broadcasted_iota(jnp.int32, (MAXLEN, rows), 0)
        r = lax.broadcasted_iota(jnp.int32, (MAXLEN, rows), 1)
        return jnp.concatenate(
            [
                jnp.where((w < length) & (r == start + w), 1.0, 0.0)
                for start, length in plan
            ],
            0,
        ).astype(BF16)

    def uncut(plan, rows):
        place = lax.broadcasted_iota(jnp.int32, (rows, 4 * MAXLEN), 1)
        r = lax.broadcasted_iota(jnp.int32, (rows, 4 * MAXLEN), 0)
        total = jnp.zeros((rows, 4 * MAXLEN), F32)
        for e, (start, length) in enumerate(plan):
            w = place - e * MAXLEN
            total = jnp.where((w >= 0) & (w < length) & (r == start + w), 1.0, total)
        return total.astype(BF16)

    picks = cut(dest_plan, CAP)
    for i in range(tp):
        columns = slice(i * TILE, (i + 1) * TILE)
        cot_send[:, :, columns] = (
            mm(picks, cotangent[:, columns]).astype(BF16).reshape(4, MAXLEN, TILE)
        )
    cot_copies = [
        remote(
            cot_send.at[e],
            cot_recv.at[e],
            csend.at[e],
            crecv.at[e],
            {"dp": lax.rem(me - strides[e] + n, n)},
        )
        for e in range(4)
    ]
    for copy in cot_copies:
        copy.start()
    for k in range(1, early):
        step(w_view, w_sems, 0, k)

    for copy in tensor_copies:
        copy.wait_send()
    for j in range(1, nt):
        theirs = pl.ds(lax.rem(t - j + nt, nt) * tp, tp)
        peer = {"tensor": lax.rem(t + j, nt)}
        remote(hid.at[theirs], hid.at[theirs], hsend.at[j, 0], hrecv.at[j, 0], peer).wait_recv()
        remote(gbuf.at[theirs], gbuf.at[theirs], hsend.at[j, 1], hrecv.at[j, 1], peer).wait_recv()
    squares = jnp.zeros((TOK_DEV, 1), F32)
    for j in range(TILES):
        values = hid[j].astype(F32)
        squares = squares + jnp.sum(values * values, 1, keepdims=True)
    inverse_rms = lax.rsqrt(squares * (1.0 / D) + EPSILON)
    for j in range(TILES):
        rows = (hid[j].astype(F32) * inverse_rms * gbuf[j, 0:1, :]).astype(BF16)
        nrm[j] = rows
        for i in range(TILE // blk):
            nblk[j * (TILE // blk) + i] = rows[:, i * blk : (i + 1) * blk]
    my_tokens = pl.ds(pl.multiple_of(me * TOK_DEV, TOK_DEV), TOK_DEV)
    share = TOK_DEV // nt
    my_share = pl.ds(pl.multiple_of(t * share, share), share)

    def norm_copy(j, src, dst):
        return remote(
            nblk.at[src, my_share],
            ncol.at[dst, my_share],
            bsend.at[j],
            brecv.at[j],
            {"dp": lax.rem(me + j, n)},
        )

    def norm_start(j, carry):
        norm_copy(j, lax.rem(me + j, n), me).start()
        return carry

    lax.fori_loop(1, n, norm_start, 0)
    ncol[me, my_share, :] = nblk[me, my_share, :]

    def share_copy(j, shard):
        rows = pl.ds(pl.multiple_of(shard * share, share), share)
        block = ncol.at[:, rows]
        return remote(
            block, block, ysend.at[j], yrecv.at[j], {"tensor": lax.rem(t + j, nt)}
        )

    def share_rows():
        def norm_wait(j, carry):
            norm_copy(j, lax.rem(me + j, n), lax.rem(me - j + n, n)).wait_recv()
            norm_copy(j, lax.rem(me + j, n), me).wait_send()
            return carry

        lax.fori_loop(1, n, norm_wait, 0)
        for j in range(1, nt):
            share_copy(j, t).start()

    step(w_view, w_sems, 0, early)

    row = lax.broadcasted_iota(jnp.int32, (TOK_DEV, TOK_DEV), 0)
    col = lax.broadcasted_iota(jnp.int32, (TOK_DEV, TOK_DEV), 1)
    row_start = jnp.zeros((TOK_DEV, TOK_DEV), jnp.int32)
    col_start = jnp.zeros((TOK_DEV, TOK_DEV), jnp.int32)
    for start, length in home_plan:
        row_start = jnp.where((row >= start) & (row < start + length), start, row_start)
        col_start = jnp.where((col >= start) & (col < start + length), start, col_start)
    bias = jnp.where((row_start == col_start) & (col <= row), 0.0, -1e30).astype(F32)
    bias = jnp.concatenate([bias] * GROUP, 0)
    angles = (row - row_start).astype(F32) * freq[0:1, :]
    cosine = jnp.cos(angles)
    sine = jnp.sin(angles) * jnp.where(col < HEAD // 2, -1.0, 1.0)

    def rotate(values, sine_part):
        return values * cosine + pltpu.roll(values, HEAD // 2, 1) * sine_part

    for copy in cot_copies:
        copy.wait()
    picks = uncut(home_plan, TOK_DEV)
    for h in range(kh):
        arrived = cot_recv[:, :, h * TILE : (h + 1) * TILE].reshape(4 * MAXLEN, TILE)
        cot_home[h] = mm(picks, arrived).astype(BF16)

    for j in range(TILES):
        pacc[j] = jnp.zeros((TILE, TOK_DEV), F32)

    def out_copy(h, e):
        return remote(
            out_send.at[h, e],
            out_recv.at[h, e],
            osend.at[h, e],
            orecv.at[h, e],
            {"dp": lax.rem(me + strides[e], n)},
        )

    def project_head(h, first, last):
        def project(j, carry):
            rows = pl.ds(pl.multiple_of(j * TILE, TILE), TILE)
            acc[...] += mm(nrm[j], wbuf[h, rows, :])
            return carry

        lax.fori_loop(first, last, project, 0)

    def attend_head(h):
        query = jnp.concatenate(
            [rotate(acc[:, g * HEAD : (g + 1) * HEAD], sine) for g in range(GROUP)], 0
        ).astype(BF16)
        key = rotate(acc[:, GROUP * HEAD : (GROUP + 1) * HEAD], sine).astype(BF16)
        value = acc[:, (GROUP + 1) * HEAD :].astype(BF16)
        factor = HEAD**-0.5
        scores = mm(query, key, NT) * factor + bias
        exp_terms = jnp.exp(scores - jnp.max(scores, -1, keepdims=True))
        probs = exp_terms / jnp.sum(exp_terms, -1, keepdims=True)
        probs_low = probs.astype(BF16)
        mixed = mm(probs_low, value).astype(BF16)
        cot = cot_home[h]
        grad_out = jnp.concatenate(
            [cot[:, g * HEAD : (g + 1) * HEAD] for g in range(GROUP)], 0
        )
        grad_value = mm(probs_low, grad_out, TN)
        grad_probs = mm(grad_out, value, NT)
        centre = jnp.sum(grad_probs * probs, -1, keepdims=True)
        grad_scores = (probs * (grad_probs - centre) * factor).astype(BF16)
        grad_query = mm(grad_scores, key)
        grad_key = rotate(mm(grad_scores, query, TN), -sine)
        attn = jnp.concatenate(
            [mixed[g * TOK_DEV : (g + 1) * TOK_DEV] for g in range(GROUP)], 1
        )
        out_send[h] = (
            mm(cut(home_plan, TOK_DEV), attn).astype(BF16).reshape(4, MAXLEN, TILE)
        )
        for e in range(4):
            out_copy(h, e).start()
        gvbuf[h, my_tokens, :] = grad_value.astype(BF16)
        grads = jnp.concatenate(
            [
                rotate(grad_query[g * TOK_DEV : (g + 1) * TOK_DEV], -sine).T
                for g in range(GROUP)
            ]
            + [grad_key.T, grad_value.T],
            0,
        )
        grads_t[...] = grads.astype(BF16)
        begin(g_view, g_sems, h)

    def back_head(h):
        def back(j, carry):
            rows = pl.ds(pl.multiple_of(j * TILE, TILE), TILE)
            pacc[j] += mm(wbuf[h, rows, :], grads_t[...])
            return carry

        lax.fori_loop(0, TILES, back, 0)

    def round_of(h, carry):
        for k in range(1, early + 1):

            @pl.when(h < kh)
            def _():
                step(w_view, w_sems, h, early + k)

            @pl.when((h >= 2) & (h < kh))
            def _():
                step(g_view, g_sems, h - 2, 2 * k - 1)
                step(g_view, g_sems, h - 2, 2 * k)

            if k == 1:

                @pl.when(h >= 1)
                def _():
                    gathered(w_view, w_sems, h - 1)
                    acc[...] = jnp.zeros_like(acc)
                    project_head(h - 1, 0, TILES // 2)

            if k == 2:

                @pl.when(h >= 1)
                def _():
                    attend_head(h - 1)

            @pl.when(h + 1 < kh)
            def _():
                step(w_view, w_sems, h + 1, k)

            if k == 1:

                @pl.when(h >= 1)
                def _():
                    project_head(h - 1, TILES // 2, TILES)

            if k == 2:

                @pl.when(h >= 1)
                def _():
                    back_head(h - 1)

        @pl.when(h == 1)
        def _():
            share_rows()

        return carry

    lax.fori_loop(0, kh + 1, round_of, 0)

    last = range(max(kh - 2, 0), kh)
    dots = jnp.zeros((TOK_DEV, 1), F32)
    for j in range(TILES):
        low = pacc[j].T.astype(BF16)
        psend[j] = low
        dots = dots + jnp.sum(
            low.astype(F32) * gbuf[j, 0:1, :] * hid[j].astype(F32), 1, keepdims=True
        )
    rsend[...] = jnp.broadcast_to(dots, (TOK_DEV, HEAD))
    term_copies = []
    for j in range(1, nt):
        to = lax.rem(t + j, nt)
        peer = {"tensor": to}
        term_copies.append(
            remote(
                psend.at[pl.ds(to * tp, tp)], precv.at[j - 1], psems.at[j], prems.at[j], peer
            )
        )
        term_copies.append(remote(rsend, rrecv.at[j - 1], rsems.at[j], rrems.at[j], peer))
    for copy in term_copies:
        copy.start()
    def place_out(h):
        for e in range(4):
            out_copy(h, e).wait()
        arrived = out_recv[h].reshape(4 * MAXLEN, TILE)
        out_ref[:, h * TILE : (h + 1) * TILE] = mm(uncut(dest_plan, CAP), arrived).astype(BF16)

    for k in range(1, zs + 1):
        for h in last:
            step(g_view, g_sems, h, k)
        if k <= kh:
            place_out(k - 1)
    for copy in term_copies:
        copy.wait()
    row_dot = rsend[:, 0:1]
    for j in range(1, nt):
        row_dot = row_dot + rrecv[j - 1, :, 0:1]
    for i in range(tp):
        summed = psend[t * tp + i].astype(F32)
        for j in range(1, nt):
            summed = summed + precv[j - 1, i].astype(F32)
        weighted = summed * gbuf[t * tp + i, 0:1, :]
        gh_ref[:, i * TILE : (i + 1) * TILE] = (
            inverse_rms * weighted
            - hid[t * tp + i].astype(F32) * inverse_rms**3 * row_dot * (1.0 / D)
        ).astype(BF16)

    for j in range(1, nt):
        share_copy(j, t).wait_send()
        share_copy(j, lax.rem(t - j + nt, nt)).wait_recv()
    for h in range(kh):
        gathered(g_view, g_sems, h)
    gvw_acc[...] = jnp.zeros_like(gvw_acc)

    def weigh(c, carry):
        rows = pl.ds(pl.multiple_of(c * TILE, TILE), TILE)
        owners = pl.ds(c * (TILE // TOK_DEV), TILE // TOK_DEV)
        columns = ncol[owners].reshape(TILE, blk)
        values = jnp.concatenate([gvbuf[h, rows, :] for h in range(kh)], 1)
        gvw_acc[...] += mm(columns, values, TN)
        return carry

    lax.fori_loop(0, n * TOK_DEV // TILE, weigh, 0)
    gvw_ref[...] = gvw_acc[...]

    def finish(h, carry):
        drained(w_view, w_sems, h)
        drained(g_view, g_sems, h)
        return carry

    lax.fori_loop(0, kh, finish, 0)


def split_kernel(
    n,
    nt,
    seq_length,
    home_offset,
    dest_shard,
    dest_offset,
    hidden,
    gain,
    freq,
    cotangent,
    w_query,
    w_key,
    w_value,
    out_ref,
    gh_ref,
    gvw_ref,
    wbuf,
    hid,
    gbuf,
    cosines,
    sines,
    biases,
    cot_across,
    attn_out,
    attn_in,
    pxs,
    pxr,
    nblk,
    ncol,
    cot_send,
    cot_recv,
    cot_home,
    acc,
    grads_t,
    pacc,
    psend,
    precv,
    rsend,
    rrecv,
    gvbuf,
    out_send,
    out_recv,
    gvw_acc,
    load_sem,
    wzs,
    wzr,
    wxs,
    wxr,
    wss,
    wsr,
    gzs,
    gzr,
    gxs,
    gxr,
    gss,
    gsr,
    ysend,
    yrecv,
    ysends,
    yrecvs,
    qsend,
    qrecv,
    hsend,
    hrecv,
    bsend,
    brecv,
    csend,
    crecv,
    asend,
    arecv,
    osend,
    orecv,
    psems,
    prems,
    rsems,
    rrems,
):
    me = lax.axis_index("dp")
    t = lax.axis_index("tensor")
    kh = gvbuf.shape[0]
    hh = kh // 2
    blk = D // n
    tp = TILES // nt
    zs = n // 4
    core = lax.rem(me, 2)
    chip = lax.div(me, 2)
    z, x = lax.div(chip, 2), lax.rem(chip, 2)
    sibling = me + 1 - 2 * core
    across = me + 2 - 4 * x
    spot = 4 * z + 2 * core + x
    other_spot = spot + 1 - 2 * x
    strides = [n - 1, 1, n // 2, n // 2 + 1]

    barrier = pltpu.get_barrier_semaphore()

    def greet(j, carry):
        pl.semaphore_signal(
            barrier,
            inc=1,
            device_id={"dp": lax.rem(me + j, n)},
            device_id_type=pl.DeviceIdType.MESH,
        )
        return carry

    lax.fori_loop(1, n, greet, 0)
    for j in range(1, nt):
        pl.semaphore_signal(
            barrier,
            inc=1,
            device_id={"tensor": lax.rem(t + j, nt)},
            device_id_type=pl.DeviceIdType.MESH,
        )

    def remote(src, dst, ssem, rsem, where):
        return pltpu.make_async_remote_copy(
            src_ref=src,
            dst_ref=dst,
            send_sem=ssem,
            recv_sem=rsem,
            device_id=where,
            device_id_type=pl.DeviceIdType.MESH,
        )

    def shard_parts(h, which):
        head = which * hh + h
        for part, (src, first, width) in enumerate(
            (
                (w_query, 0, GROUP * HEAD),
                (w_key, GROUP * HEAD, HEAD),
                (w_value, (GROUP + 1) * HEAD, HEAD),
            )
        ):
            yield part, src.at[:, pl.ds(pl.multiple_of(head * width, width), width)], pl.ds(
                first, width
            )

    def rows_at(where):
        return pl.ds(pl.multiple_of(where * blk, blk), blk)

    def loads_of(h):
        return [
            pltpu.make_async_copy(src, wbuf.at[h, rows_at(spot), cols], load_sem.at[h, part])
            for part, src, cols in shard_parts(h, x)
        ]

    def swaps_of(h, where):
        return [
            remote(
                src,
                wbuf.at[h, rows_at(where), cols],
                wxs.at[h, part],
                wxr.at[h, part],
                {"dp": across},
            )
            for part, src, cols in shard_parts(h, 1 - x)
        ]

    for h in range(hh):
        for load in loads_of(h):
            load.start()

    for i in range(tp):
        hid[t * tp + i] = hidden[:, i * TILE : (i + 1) * TILE]
        gbuf[t * tp + i] = jnp.broadcast_to(gain[:, i * TILE : (i + 1) * TILE], (8, TILE))

    pl.semaphore_wait(barrier, n - 1 + nt - 1)

    for h in range(hh):
        for swap in swaps_of(h, spot):
            swap.start()

    own_tiles = pl.ds(t * tp, tp)
    tensor_copies = []
    for j in range(1, nt):
        peer = {"tensor": lax.rem(t + j, nt)}
        tensor_copies.append(
            remote(hid.at[own_tiles], hid.at[own_tiles], hsend.at[j, 0], hrecv.at[j, 0], peer)
        )
        tensor_copies.append(
            remote(gbuf.at[own_tiles], gbuf.at[own_tiles], hsend.at[j, 1], hrecv.at[j, 1], peer)
        )
    for copy in tensor_copies:
        copy.start()

    def w_view(h, zz, xx, which):
        rows = pl.multiple_of((4 * zz + 2 * which + lax.rem(h, 2)) * blk, blk)
        return wbuf.at[lax.div(h, 2), pl.ds(rows, blk)]

    def g_view(h, zz, xx, which):
        rows = pl.multiple_of((4 * zz + 2 * which) * TOK_DEV, 2 * TOK_DEV)
        return gvbuf.at[xx * hh + h, pl.ds(rows, 2 * TOK_DEV)]

    up, down = lax.rem(me + 4, n), lax.rem(me - 4 + n, n)

    def z_copy(view, sems, h, way, zz):
        block = view(h, zz, x, core)
        return remote(
            block,
            block,
            sems[0].at[h, way, zz],
            sems[1].at[h, zz],
            {"dp": up if way == 0 else down},
        )

    def x_copy(view, sems, h, zz, xx):
        block = view(h, zz, xx, core)
        return remote(block, block, sems[2].at[h, zz], sems[3].at[h, zz], {"dp": across})

    def s_copy(view, sems, h, zz, xx, which):
        block = view(h, zz, xx, which)
        return remote(
            block, block, sems[4].at[h, xx, zz], sems[5].at[h, xx, zz], {"dp": sibling}
        )

    def begin(view, sems, h):
        @pl.when(z < zs - 1)
        def _():
            z_copy(view, sems, h, 0, z).start()

        @pl.when(z > 0)
        def _():
            z_copy(view, sems, h, 1, z).start()

        if sems is g_sems:
            x_copy(view, sems, h, z, x).start()
        s_copy(view, sems, h, z, x, core).start()

    def step(view, sems, h, k):
        if k < zs:

            @pl.when(z >= k)
            def _():
                zz = z - k
                z_copy(view, sems, h, 0, zz).wait_recv()

                @pl.when(z < zs - 1)
                def _():
                    z_copy(view, sems, h, 0, zz).start()

                if sems is g_sems:
                    x_copy(view, sems, h, zz, x).start()
                s_copy(view, sems, h, zz, x, core).start()

            @pl.when(z + k < zs)
            def _():
                zz = z + k
                z_copy(view, sems, h, 1, zz).wait_recv()

                @pl.when(z > 0)
                def _():
                    z_copy(view, sems, h, 1, zz).start()

                if sems is g_sems:
                    x_copy(view, sems, h, zz, x).start()
                s_copy(view, sems, h, zz, x, core).start()

        if sems is w_sems:
            return

        def from_across(zz):
            x_copy(view, sems, h, zz, 1 - x).wait_recv()
            s_copy(view, sems, h, zz, 1 - x, core).start()

        if k == 1:
            from_across(z)
        else:

            @pl.when(z >= k - 1)
            def _():
                from_across(z - k + 1)

            @pl.when(z + k - 1 < zs)
            def _():
                from_across(z + k - 1)

    def gathered(view, sems, h):
        def one(zz, carry):
            s_copy(view, sems, h, zz, x, 1 - core).wait_recv()
            if sems is g_sems:
                s_copy(view, sems, h, zz, 1 - x, 1 - core).wait_recv()
            return carry

        lax.fori_loop(0, zs, one, 0)

    def drained(view, sems, h):
        def one(zz, carry):
            s_copy(view, sems, h, zz, x, core).wait_send()
            if sems is g_sems:
                s_copy(view, sems, h, zz, 1 - x, core).wait_send()
                x_copy(view, sems, h, zz, x).wait_send()

            @pl.when((zz <= z) & (z < zs - 1))
            def _():
                z_copy(view, sems, h, 0, zz).wait_send()

            @pl.when((zz >= z) & (z > 0))
            def _():
                z_copy(view, sems, h, 1, zz).wait_send()

            return carry

        lax.fori_loop(0, zs, one, 0)

    w_sems = (wzs, wzr, None, None, wss, wsr)
    g_sems = (gzs, gzr, gxs, gxr, gss, gsr)
    early = zs // 2
    def w_step(h, k):
        step(w_view, w_sems, 2 * h, k)
        step(w_view, w_sems, 2 * h + 1, k)

    def begin_weights(h):
        for load in loads_of(h):
            load.wait()
        for swap in swaps_of(h, other_spot):
            swap.wait_recv()
        begin(w_view, w_sems, 2 * h)
        begin(w_view, w_sems, 2 * h + 1)

    begin_weights(0)

    def picked(table, row, target, slot):
        total = jnp.int32(0)
        for c in range(4):
            total = total + jnp.where(dest_shard[row, c] == target, table[row, c], 0)
        return total

    home_plan, dest_plan, across_plan = [], [], []
    for stride in strides:
        target = lax.rem(across + stride, n)
        across_plan.append(
            (
                picked(home_offset, across, target, 0),
                picked(seq_length, across, target, 0),
            )
        )
        target = lax.rem(me + stride, n)
        source = lax.rem(me - stride + n, n)
        home_plan.append(
            (picked(home_offset, me, target, 0), picked(seq_length, me, target, 0))
        )
        dest_plan.append(
            (picked(dest_offset, source, me, 0), picked(seq_length, source, me, 0))
        )

    def cut(plan, rows):
        w = lax.broadcasted_iota(jnp.int32, (MAXLEN, rows), 0)
        r = lax.broadcasted_iota(jnp.int32, (MAXLEN, rows), 1)
        return jnp.concatenate(
            [
                jnp.where((w < length) & (r == start + w), 1.0, 0.0)
                for start, length in plan
            ],
            0,
        ).astype(BF16)

    def uncut(plan, rows):
        place = lax.broadcasted_iota(jnp.int32, (rows, 4 * MAXLEN), 1)
        r = lax.broadcasted_iota(jnp.int32, (rows, 4 * MAXLEN), 0)
        total = jnp.zeros((rows, 4 * MAXLEN), F32)
        for e, (start, length) in enumerate(plan):
            w = place - e * MAXLEN
            total = jnp.where((w >= 0) & (w < length) & (r == start + w), 1.0, total)
        return total.astype(BF16)

    picks = cut(dest_plan, CAP)
    for i in range(tp):
        columns = slice(i * TILE, (i + 1) * TILE)
        cot_send[:, :, columns] = (
            mm(picks, cotangent[:, columns]).astype(BF16).reshape(4, MAXLEN, TILE)
        )
    cot_copies = [
        remote(
            cot_send.at[e],
            cot_recv.at[e],
            csend.at[e],
            crecv.at[e],
            {"dp": lax.rem(me - strides[e] + n, n)},
        )
        for e in range(4)
    ]
    for copy in cot_copies:
        copy.start()
    for h in range(1, hh):
        begin_weights(h)
    for k in range(1, early):
        w_step(0, k)

    for copy in tensor_copies:
        copy.wait_send()
    for j in range(1, nt):
        theirs = pl.ds(lax.rem(t - j + nt, nt) * tp, tp)
        peer = {"tensor": lax.rem(t + j, nt)}
        remote(hid.at[theirs], hid.at[theirs], hsend.at[j, 0], hrecv.at[j, 0], peer).wait_recv()
        remote(gbuf.at[theirs], gbuf.at[theirs], hsend.at[j, 1], hrecv.at[j, 1], peer).wait_recv()
    squares = jnp.zeros((TOK_DEV, 1), F32)
    for j in range(TILES):
        values = hid[j].astype(F32)
        squares = squares + jnp.sum(values * values, 1, keepdims=True)
    inverse_rms = lax.rsqrt(squares * (1.0 / D) + EPSILON)
    for j in range(TILES):
        rows = (hid[j].astype(F32) * inverse_rms * gbuf[j, 0:1, :]).astype(BF16)
        for i in range(TILE // blk):
            nblk[x, j * (TILE // blk) + i] = rows[:, i * blk : (i + 1) * blk]
    row_swap = remote(nblk.at[x], nblk.at[x], qsend.at[0], qrecv.at[0], {"dp": across})
    row_swap.start()
    share = TOK_DEV // nt
    my_share = pl.ds(pl.multiple_of(t * share, share), share)

    def norm_copy(j, src, dst):
        return remote(
            nblk.at[x, src, my_share],
            ncol.at[dst, my_share],
            bsend.at[j],
            brecv.at[j],
            {"dp": lax.rem(me + j, n)},
        )

    def norm_start(j, carry):
        norm_copy(j, lax.rem(me + j, n), spot).start()
        return carry

    lax.fori_loop(1, n, norm_start, 0)
    ncol[spot, my_share, :] = nblk[x, me, my_share, :]

    def share_copy(j, shard):
        rows = pl.ds(pl.multiple_of(shard * share, share), share)
        block = ncol.at[:, rows]
        return remote(
            block, block, ysend.at[j], yrecv.at[j], {"tensor": lax.rem(t + j, nt)}
        )

    def share_rows():
        def norm_wait(j, carry):
            sender = lax.rem(me - j + n, n)
            side = lax.rem(sender, 4)
            where = sender - side + 2 * lax.rem(side, 2) + lax.div(side, 2)
            norm_copy(j, lax.rem(me + j, n), where).wait_recv()
            norm_copy(j, lax.rem(me + j, n), spot).wait_send()
            return carry

        lax.fori_loop(1, n, norm_wait, 0)
        for j in range(1, nt):
            share_copy(j, t).start()

    w_step(0, early)

    row = lax.broadcasted_iota(jnp.int32, (TOK_DEV, TOK_DEV), 0)
    col = lax.broadcasted_iota(jnp.int32, (TOK_DEV, TOK_DEV), 1)

    def tables(plan):
        row_start = jnp.zeros((TOK_DEV, TOK_DEV), jnp.int32)
        col_start = jnp.zeros((TOK_DEV, TOK_DEV), jnp.int32)
        for start, length in plan:
            row_start = jnp.where((row >= start) & (row < start + length), start, row_start)
            col_start = jnp.where((col >= start) & (col < start + length), start, col_start)
        bias = jnp.where((row_start == col_start) & (col <= row), 0.0, -1e30).astype(F32)
        angles = (row - row_start).astype(F32) * freq[0:1, :]
        sine = jnp.sin(angles) * jnp.where(col < HEAD // 2, -1.0, 1.0)
        return jnp.cos(angles), sine, jnp.concatenate([bias] * GROUP, 0)

    for side, plan in enumerate((home_plan, across_plan)):
        cosines[side], sines[side], biases[side] = tables(plan)

    def rotate(values, cosine, sine_part):
        return values * cosine + pltpu.roll(values, HEAD // 2, 1) * sine_part

    for copy in cot_copies:
        copy.wait()
    picks = uncut(home_plan, TOK_DEV)
    for h in range(kh):
        arrived = cot_recv[:, :, h * TILE : (h + 1) * TILE].reshape(4 * MAXLEN, TILE)
        cot_home[h] = mm(picks, arrived).astype(BF16)

    cot_swap = remote(
        cot_home.at[pl.ds((1 - x) * hh, hh)], cot_across, qsend.at[1], qrecv.at[1], {"dp": across}
    )
    cot_swap.start()

    for j in range(n):
        pacc[j] = jnp.zeros((blk, 2 * TOK_DEV), F32)
    cot_swap.wait()
    row_swap.wait()

    def out_copy(h, e):
        return remote(
            out_send.at[h, e],
            out_recv.at[h, e],
            osend.at[h, e],
            orecv.at[h, e],
            {"dp": lax.rem(me + strides[e], n)},
        )

    def project_head(h, first, last):
        def project(j, carry):
            side = lax.rem(j, 4)
            shard = j - side + 2 * lax.rem(side, 2) + lax.div(side, 2)
            rows = pl.ds(pl.multiple_of(j * blk, blk), blk)
            both = jnp.concatenate([nblk[x, shard], nblk[1 - x, shard]], 0)
            acc[...] += mm(both, wbuf[h, rows, :])
            return carry

        lax.fori_loop(first, last, project, 0)

    def attn_copy(h):
        return remote(
            attn_out.at[h], attn_in.at[h], ysends.at[h], yrecvs.at[h], {"dp": across}
        )

    def send_out(head, attn):
        out_send[head] = (
            mm(cut(home_plan, TOK_DEV), attn).astype(BF16).reshape(4, MAXLEN, TILE)
        )
        for e in range(4):
            out_copy(head, e).start()

    def attend_side(h, side, where):
        first = side * TOK_DEV
        rows = slice(first, first + TOK_DEV)
        cosine, sine = cosines[side], sines[side]
        query = jnp.concatenate(
            [
                rotate(acc[rows, g * HEAD : (g + 1) * HEAD], cosine, sine)
                for g in range(GROUP)
            ],
            0,
        ).astype(BF16)
        key = rotate(acc[rows, GROUP * HEAD : (GROUP + 1) * HEAD], cosine, sine).astype(BF16)
        value = acc[rows, (GROUP + 1) * HEAD :].astype(BF16)
        factor = HEAD**-0.5
        scores = mm(query, key, NT) * factor + biases[side]
        exp_terms = jnp.exp(scores - jnp.max(scores, -1, keepdims=True))
        probs = exp_terms / jnp.sum(exp_terms, -1, keepdims=True)
        probs_low = probs.astype(BF16)
        mixed = mm(probs_low, value).astype(BF16)
        cot = cot_home[x * hh + h] if side == 0 else cot_across[h]
        grad_out = jnp.concatenate(
            [cot[:, g * HEAD : (g + 1) * HEAD] for g in range(GROUP)], 0
        )
        grad_value = mm(probs_low, grad_out, TN)
        grad_probs = mm(grad_out, value, NT)
        centre = jnp.sum(grad_probs * probs, -1, keepdims=True)
        grad_scores = (probs * (grad_probs - centre) * factor).astype(BF16)
        grad_query = mm(grad_scores, key)
        grad_key = rotate(mm(grad_scores, query, TN), cosine, -sine)
        attn = jnp.concatenate(
            [mixed[g * TOK_DEV : (g + 1) * TOK_DEV] for g in range(GROUP)], 1
        )
        if side == 0:
            send_out(x * hh + h, attn)
        else:
            attn_out[h] = attn
            attn_copy(h).start()
        tokens = pl.ds(pl.multiple_of(where * TOK_DEV, TOK_DEV), TOK_DEV)
        gvbuf[x * hh + h, tokens, :] = grad_value.astype(BF16)
        grads = jnp.concatenate(
            [
                rotate(grad_query[g * TOK_DEV : (g + 1) * TOK_DEV], cosine, -sine).T
                for g in range(GROUP)
            ]
            + [grad_key.T, grad_value.T],
            0,
        )
        grads_t[:, rows] = grads.astype(BF16)

    def attend_head(h):
        attend_side(h, 1, other_spot)
        attend_side(h, 0, spot)
        begin(g_view, g_sems, h)

    def from_other(h):
        attn_copy(h).wait()
        send_out((1 - x) * hh + h, attn_in[h])

    def back_head(h):
        def back(j, carry):
            rows = pl.ds(pl.multiple_of(j * blk, blk), blk)
            pacc[j] += mm(wbuf[h, rows, :], grads_t[...])
            return carry

        lax.fori_loop(0, n, back, 0)

    def round_of(h, carry):
        for k in range(1, early + 1):

            @pl.when(h < hh)
            def _():
                w_step(h, early + k)

            if k == 1:

                @pl.when(h >= 1)
                def _():
                    gathered(w_view, w_sems, 2 * h - 2)
                    gathered(w_view, w_sems, 2 * h - 1)
                    acc[...] = jnp.zeros_like(acc)
                    project_head(h - 1, 0, n // 2)

            if k == 2:

                @pl.when(h >= 1)
                def _():
                    attend_head(h - 1)

            @pl.when(h >= 2)
            def _():
                step(g_view, g_sems, h - 2, 2 * k - 1)
                step(g_view, g_sems, h - 2, 2 * k)

            @pl.when(h + 1 < hh)
            def _():
                w_step(h + 1, k)

            if k == 1:

                @pl.when(h >= 1)
                def _():
                    project_head(h - 1, n // 2, n)

            if k == 2:

                @pl.when(h >= 1)
                def _():
                    back_head(h - 1)

        @pl.when(h >= 2)
        def _():
            from_other(h - 2)

        @pl.when(h == 1)
        def _():
            share_rows()

        return carry

    lax.fori_loop(0, hh + 1, round_of, 0)

    last = range(hh - 1, hh)
    for j in range(n):
        pxs[j] = pacc[j, :, TOK_DEV:].astype(BF16)
    half_swap = remote(pxs, pxr, qsend.at[2], qrecv.at[2], {"dp": across})
    half_swap.start()
    from_other(hh - 1)
    for h in last:
        step(g_view, g_sems, h, 1)
    half_swap.wait()
    for j in range(n):
        total = pacc[j, :, :TOK_DEV] + pxr[j].astype(F32)
        shard = j - j % 4 + 2 * (j % 2) + (j % 4) // 2
        first = shard * blk % TILE
        psend[shard * blk // TILE, :, first : first + blk] = total.T.astype(BF16)
    dots = jnp.zeros((TOK_DEV, 1), F32)
    for j in range(TILES):
        low = psend[j]
        dots = dots + jnp.sum(
            low.astype(F32) * gbuf[j, 0:1, :] * hid[j].astype(F32), 1, keepdims=True
        )
    rsend[...] = jnp.broadcast_to(dots, (TOK_DEV, HEAD))
    term_copies = []
    for j in range(1, nt):
        to = lax.rem(t + j, nt)
        peer = {"tensor": to}
        term_copies.append(
            remote(
                psend.at[pl.ds(to * tp, tp)], precv.at[j - 1], psems.at[j], prems.at[j], peer
            )
        )
        term_copies.append(remote(rsend, rrecv.at[j - 1], rsems.at[j], rrems.at[j], peer))
    for copy in term_copies:
        copy.start()
    def place_out(h):
        for e in range(4):
            out_copy(h, e).wait()
        arrived = out_recv[h].reshape(4 * MAXLEN, TILE)
        out_ref[:, h * TILE : (h + 1) * TILE] = mm(uncut(dest_plan, CAP), arrived).astype(BF16)

    for k in range(1, zs + 1):
        for h in last:
            if k > 1:
                step(g_view, g_sems, h, k)
        if k <= kh:
            place_out(k - 1)
    for copy in term_copies:
        copy.wait()
    row_dot = rsend[:, 0:1]
    for j in range(1, nt):
        row_dot = row_dot + rrecv[j - 1, :, 0:1]
    for i in range(tp):
        summed = psend[t * tp + i].astype(F32)
        for j in range(1, nt):
            summed = summed + precv[j - 1, i].astype(F32)
        weighted = summed * gbuf[t * tp + i, 0:1, :]
        gh_ref[:, i * TILE : (i + 1) * TILE] = (
            inverse_rms * weighted
            - hid[t * tp + i].astype(F32) * inverse_rms**3 * row_dot * (1.0 / D)
        ).astype(BF16)

    for j in range(1, nt):
        share_copy(j, t).wait_send()
        share_copy(j, lax.rem(t - j + nt, nt)).wait_recv()
    for h in range(hh):
        gathered(g_view, g_sems, h)
    gvw_acc[...] = jnp.zeros_like(gvw_acc)

    def weigh(c, carry):
        rows = pl.ds(pl.multiple_of(c * TILE, TILE), TILE)
        owners = pl.ds(c * (TILE // TOK_DEV), TILE // TOK_DEV)
        columns = ncol[owners].reshape(TILE, blk)
        values = jnp.concatenate([gvbuf[h, rows, :] for h in range(kh)], 1)
        gvw_acc[...] += mm(columns, values, TN)
        return carry

    lax.fori_loop(0, n * TOK_DEV // TILE, weigh, 0)
    gvw_ref[...] = gvw_acc[...]

    def finish(h, carry):
        drained(w_view, w_sems, 2 * h)
        drained(w_view, w_sems, 2 * h + 1)
        drained(g_view, g_sems, h)
        return carry

    lax.fori_loop(0, hh, finish, 0)
    for h in range(hh):
        for swap in swaps_of(h, spot):
            swap.wait_send()


def on_device(
    hidden,
    gain,
    w_query,
    w_key,
    w_value,
    cotangent,
    seq_length,
    home_offset,
    dest_shard,
    dest_offset,
):
    n = lax.axis_size("dp")
    nt = lax.axis_size("tensor")
    kh = w_key.shape[1] // HEAD
    width = hidden.shape[1]
    blk = D // n
    tp = TILES // nt
    zs = n // 4
    half = HEAD // 2
    exponent = jnp.arange(half, dtype=F32) * (2.0 / HEAD)
    inverse = jnp.power(jnp.float32(ROPE_BASE), -exponent)
    freq = jnp.broadcast_to(jnp.concatenate([inverse, inverse])[None, :], (8, HEAD))
    dma = pltpu.SemaphoreType.DMA
    vmem = pl.BlockSpec(memory_space=pltpu.VMEM)
    smem = pl.BlockSpec(memory_space=pltpu.SMEM)
    anywhere = pl.BlockSpec(memory_space=pl.ANY)
    return pl.pallas_call(
        functools.partial(kernel, n, nt),
        out_shape=(
            jax.ShapeDtypeStruct((CAP, width), BF16),
            jax.ShapeDtypeStruct((TOK_DEV, width), BF16),
            jax.ShapeDtypeStruct((blk, kh * HEAD), F32),
        ),
        in_specs=[smem] * 4 + [vmem] * 4 + [anywhere] * 3,
        out_specs=(vmem, vmem, vmem),
        scratch_shapes=[
            pltpu.VMEM((kh, D, HEAD_COLS), BF16),
            pltpu.VMEM((TILES, TOK_DEV, TILE), BF16),
            pltpu.VMEM((TILES, 8, TILE), F32),
            pltpu.VMEM((TILES, TOK_DEV, TILE), BF16),
            pltpu.VMEM((n, TOK_DEV, blk), BF16),
            pltpu.VMEM((n, TOK_DEV, blk), BF16),
            pltpu.VMEM((4, MAXLEN, width), BF16),
            pltpu.VMEM((4, MAXLEN, width), BF16),
            pltpu.VMEM((kh, TOK_DEV, TILE), BF16),
            pltpu.VMEM((TOK_DEV, HEAD_COLS), F32),
            pltpu.VMEM((HEAD_COLS, TOK_DEV), BF16),
            pltpu.VMEM((TILES, TILE, TOK_DEV), F32),
            pltpu.VMEM((TILES, TOK_DEV, TILE), BF16),
            pltpu.VMEM((nt - 1, tp, TOK_DEV, TILE), BF16),
            pltpu.VMEM((TOK_DEV, HEAD), F32),
            pltpu.VMEM((nt - 1, TOK_DEV, HEAD), F32),
            pltpu.VMEM((kh, n * TOK_DEV, HEAD), BF16),
            pltpu.VMEM((kh, 4, MAXLEN, TILE), BF16),
            pltpu.VMEM((kh, 4, MAXLEN, TILE), BF16),
            pltpu.VMEM((blk, kh * HEAD), F32),
            dma((kh, 3)),
            dma((kh, 2, zs)),
            dma((kh, zs)),
            dma((kh, zs)),
            dma((kh, zs)),
            dma((kh, 2, zs)),
            dma((kh, 2, zs)),
            dma((kh, 2, zs)),
            dma((kh, zs)),
            dma((kh, zs)),
            dma((kh, zs)),
            dma((kh, 2, zs)),
            dma((kh, 2, zs)),
            dma((nt,)),
            dma((nt,)),
            dma((nt, 2)),
            dma((nt, 2)),
            dma((n,)),
            dma((n,)),
            dma((4,)),
            dma((4,)),
            dma((4,)),
            dma((4,)),
            dma((kh, 4)),
            dma((kh, 4)),
            dma((nt,)),
            dma((nt,)),
            dma((nt,)),
            dma((nt,)),
        ],
        compiler_params=pltpu.CompilerParams(
            collective_id=0, has_side_effects=True, vmem_limit_bytes=56 * 1024 * 1024
        ),
        cost_estimate=pl.CostEstimate(
            flops=8 * 10**9, bytes_accessed=8 * 10**6, transcendentals=10**6
        ),
    )(
        seq_length,
        home_offset,
        dest_shard,
        dest_offset,
        hidden,
        gain.astype(F32)[None, :],
        freq,
        cotangent,
        w_query,
        w_key,
        w_value,
    )


def on_split_device(
    hidden,
    gain,
    w_query,
    w_key,
    w_value,
    cotangent,
    seq_length,
    home_offset,
    dest_shard,
    dest_offset,
):
    n = lax.axis_size("dp")
    nt = lax.axis_size("tensor")
    kh = w_key.shape[1] // HEAD
    hh = kh // 2
    width = hidden.shape[1]
    blk = D // n
    tp = TILES // nt
    zs = n // 4
    half = HEAD // 2
    exponent = jnp.arange(half, dtype=F32) * (2.0 / HEAD)
    inverse = jnp.power(jnp.float32(ROPE_BASE), -exponent)
    freq = jnp.broadcast_to(jnp.concatenate([inverse, inverse])[None, :], (8, HEAD))
    dma = pltpu.SemaphoreType.DMA
    vmem = pl.BlockSpec(memory_space=pltpu.VMEM)
    smem = pl.BlockSpec(memory_space=pltpu.SMEM)
    anywhere = pl.BlockSpec(memory_space=pl.ANY)
    return pl.pallas_call(
        functools.partial(split_kernel, n, nt),
        out_shape=(
            jax.ShapeDtypeStruct((CAP, width), BF16),
            jax.ShapeDtypeStruct((TOK_DEV, width), BF16),
            jax.ShapeDtypeStruct((blk, kh * HEAD), F32),
        ),
        in_specs=[smem] * 4 + [vmem] * 4 + [anywhere] * 3,
        out_specs=(vmem, vmem, vmem),
        scratch_shapes=[
            pltpu.VMEM((hh, D, HEAD_COLS), BF16),
            pltpu.VMEM((TILES, TOK_DEV, TILE), BF16),
            pltpu.VMEM((TILES, 8, TILE), F32),
            pltpu.VMEM((2, TOK_DEV, HEAD), F32),
            pltpu.VMEM((2, TOK_DEV, HEAD), F32),
            pltpu.VMEM((2, GROUP * TOK_DEV, TOK_DEV), F32),
            pltpu.VMEM((hh, TOK_DEV, TILE), BF16),
            pltpu.VMEM((hh, TOK_DEV, TILE), BF16),
            pltpu.VMEM((hh, TOK_DEV, TILE), BF16),
            pltpu.VMEM((n, blk, TOK_DEV), BF16),
            pltpu.VMEM((n, blk, TOK_DEV), BF16),
            pltpu.VMEM((2, n, TOK_DEV, blk), BF16),
            pltpu.VMEM((n, TOK_DEV, blk), BF16),
            pltpu.VMEM((4, MAXLEN, width), BF16),
            pltpu.VMEM((4, MAXLEN, width), BF16),
            pltpu.VMEM((kh, TOK_DEV, TILE), BF16),
            pltpu.VMEM((2 * TOK_DEV, HEAD_COLS), F32),
            pltpu.VMEM((HEAD_COLS, 2 * TOK_DEV), BF16),
            pltpu.VMEM((n, blk, 2 * TOK_DEV), F32),
            pltpu.VMEM((TILES, TOK_DEV, TILE), BF16),
            pltpu.VMEM((nt - 1, tp, TOK_DEV, TILE), BF16),
            pltpu.VMEM((TOK_DEV, HEAD), F32),
            pltpu.VMEM((nt - 1, TOK_DEV, HEAD), F32),
            pltpu.VMEM((kh, n * TOK_DEV, HEAD), BF16),
            pltpu.VMEM((kh, 4, MAXLEN, TILE), BF16),
            pltpu.VMEM((kh, 4, MAXLEN, TILE), BF16),
            pltpu.VMEM((blk, kh * HEAD), F32),
            dma((kh, 3)),
            dma((kh, 2, zs)),
            dma((kh, zs)),
            dma((kh, max(zs, 3))),
            dma((kh, max(zs, 3))),
            dma((kh, 2, zs)),
            dma((kh, 2, zs)),
            dma((kh, 2, zs)),
            dma((kh, zs)),
            dma((kh, zs)),
            dma((kh, zs)),
            dma((kh, 2, zs)),
            dma((kh, 2, zs)),
            dma((nt,)),
            dma((nt,)),
            dma((hh,)),
            dma((hh,)),
            dma((3,)),
            dma((3,)),
            dma((nt, 2)),
            dma((nt, 2)),
            dma((n,)),
            dma((n,)),
            dma((4,)),
            dma((4,)),
            dma((4,)),
            dma((4,)),
            dma((kh, 4)),
            dma((kh, 4)),
            dma((nt,)),
            dma((nt,)),
            dma((nt,)),
            dma((nt,)),
        ],
        compiler_params=pltpu.CompilerParams(
            collective_id=1, has_side_effects=True, vmem_limit_bytes=56 * 1024 * 1024
        ),
        cost_estimate=pl.CostEstimate(
            flops=8 * 10**9, bytes_accessed=8 * 10**6, transcendentals=10**6
        ),
    )(
        seq_length,
        home_offset,
        dest_shard,
        dest_offset,
        hidden,
        gain.astype(F32)[None, :],
        freq,
        cotangent,
        w_query,
        w_key,
        w_value,
    )


def solution(mesh):
    def chosen(*arrays):
        heads = arrays[3].shape[1] // HEAD
        return (on_split_device if heads % 2 == 0 else on_device)(*arrays)

    return jax.shard_map(
        chosen,
        mesh=mesh,
        in_specs=(
            P("dp", "tensor"),
            P("tensor"),
            P("dp", "tensor"),
            P("dp", "tensor"),
            P("dp", "tensor"),
            P("dp", "tensor"),
            P(),
            P(),
            P(),
            P(),
        ),
        out_specs=(P("dp", "tensor"), P("dp", "tensor"), P("dp", "tensor")),
        check_vma=False,
    )
```

```python
import functools
import math

import jax
import jax.numpy as jnp
from jax import lax
from jax.experimental import pallas as pl
from jax.experimental.pallas import tpu as pltpu
from jax.sharding import PartitionSpec as P

D = 4096
HEAD = 128
GROUP = 4
TOK_DEV = 128
MAXLEN = 64
CAP = 256
TILE = 512
TILES = D // TILE
HEAD_COLS = (GROUP + 2) * HEAD
EPSILON = 1e-05
ROPE_BASE = 500000.0
BF16 = jnp.bfloat16
F32 = jnp.float32
NN = (((1,), (0,)), ((), ()))
NT = (((1,), (1,)), ((), ()))
TN = (((0,), (0,)), ((), ()))


def mm(a, b, dims=NN):
    return lax.dot_general(a, b, dims, preferred_element_type=F32)


def kernel(
    n,
    nt,
    seq_length,
    home_offset,
    dest_shard,
    dest_offset,
    hidden,
    gain,
    freq,
    cotangent,
    w_query,
    w_key,
    w_value,
    out_ref,
    gh_ref,
    gvw_ref,
    wbuf,
    hid,
    gbuf,
    nrm,
    nblk,
    ncol,
    cot_send,
    cot_recv,
    cot_home,
    acc,
    grads_t,
    pacc,
    psend,
    precv,
    rsend,
    rrecv,
    gvbuf,
    out_send,
    out_recv,
    gvw_acc,
    load_sem,
    wzs,
    wzr,
    wxs,
    wxr,
    wss,
    wsr,
    gzs,
    gzr,
    gxs,
    gxr,
    gss,
    gsr,
    ysend,
    yrecv,
    hsend,
    hrecv,
    bsend,
    brecv,
    csend,
    crecv,
    asend,
    arecv,
    osend,
    orecv,
    psems,
    prems,
    rsems,
    rrems,
):
    me = lax.axis_index("dp")
    t = lax.axis_index("tensor")
    kh = wbuf.shape[0]
    blk = D // n
    tp = TILES // nt
    zs = n // 4
    core = lax.rem(me, 2)
    chip = lax.div(me, 2)
    z, x = lax.div(chip, 2), lax.rem(chip, 2)
    sibling = me + 1 - 2 * core
    strides = [n - 1, 1, n // 2, n // 2 + 1]

    barrier = pltpu.get_barrier_semaphore()

    def greet(j, carry):
        pl.semaphore_signal(
            barrier,
            inc=1,
            device_id={"dp": lax.rem(me + j, n)},
            device_id_type=pl.DeviceIdType.MESH,
        )
        return carry

    lax.fori_loop(1, n, greet, 0)
    for j in range(1, nt):
        pl.semaphore_signal(
            barrier,
            inc=1,
            device_id={"tensor": lax.rem(t + j, nt)},
            device_id_type=pl.DeviceIdType.MESH,
        )

    def remote(src, dst, ssem, rsem, where):
        return pltpu.make_async_remote_copy(
            src_ref=src,
            dst_ref=dst,
            send_sem=ssem,
            recv_sem=rsem,
            device_id=where,
            device_id_type=pl.DeviceIdType.MESH,
        )

    loads = []
    own_rows = pl.ds(pl.multiple_of(me * blk, blk), blk)
    for h in range(kh):
        for part, (src, first, width) in enumerate(
            (
                (w_query, 0, GROUP * HEAD),
                (w_key, GROUP * HEAD, HEAD),
                (w_value, (GROUP + 1) * HEAD, HEAD),
            )
        ):
            loads.append(
                pltpu.make_async_copy(
                    src.at[:, pl.ds(h * width, width)],
                    wbuf.at[h, own_rows, pl.ds(first, width)],
                    load_sem.at[h, part],
                )
            )
    for load in loads:
        load.start()

    for i in range(tp):
        hid[t * tp + i] = hidden[:, i * TILE : (i + 1) * TILE]
        gbuf[t * tp + i] = jnp.broadcast_to(gain[:, i * TILE : (i + 1) * TILE], (8, TILE))

    pl.semaphore_wait(barrier, n - 1 + nt - 1)

    own_tiles = pl.ds(t * tp, tp)
    tensor_copies = []
    for j in range(1, nt):
        peer = {"tensor": lax.rem(t + j, nt)}
        tensor_copies.append(
            remote(hid.at[own_tiles], hid.at[own_tiles], hsend.at[j, 0], hrecv.at[j, 0], peer)
        )
        tensor_copies.append(
            remote(gbuf.at[own_tiles], gbuf.at[own_tiles], hsend.at[j, 1], hrecv.at[j, 1], peer)
        )
    for copy in tensor_copies:
        copy.start()

    def w_view(h, zz, xx, which):
        rows = pl.multiple_of((4 * zz + 2 * xx + which) * blk, blk)
        return wbuf.at[h, pl.ds(rows, blk)]

    def g_view(h, zz, xx, which):
        rows = pl.multiple_of((4 * zz + 2 * xx + which) * TOK_DEV, TOK_DEV)
        return gvbuf.at[h, pl.ds(rows, TOK_DEV)]

    up, down = lax.rem(me + 4, n), lax.rem(me - 4 + n, n)
    across = me + 2 - 4 * x

    def z_copy(view, sems, h, way, zz):
        block = view(h, zz, x, core)
        return remote(
            block,
            block,
            sems[0].at[h, way, zz],
            sems[1].at[h, zz],
            {"dp": up if way == 0 else down},
        )

    def x_copy(view, sems, h, zz, xx):
        block = view(h, zz, xx, core)
        return remote(block, block, sems[2].at[h, zz], sems[3].at[h, zz], {"dp": across})

    def s_copy(view, sems, h, zz, xx, which):
        block = view(h, zz, xx, which)
        return remote(
            block, block, sems[4].at[h, xx, zz], sems[5].at[h, xx, zz], {"dp": sibling}
        )

    def begin(view, sems, h):
        @pl.when(z < zs - 1)
        def _():
            z_copy(view, sems, h, 0, z).start()

        @pl.when(z > 0)
        def _():
            z_copy(view, sems, h, 1, z).start()

        x_copy(view, sems, h, z, x).start()
        s_copy(view, sems, h, z, x, core).start()

    def step(view, sems, h, k):
        if k < zs:

            @pl.when(z >= k)
            def _():
                zz = z - k
                z_copy(view, sems, h, 0, zz).wait_recv()

                @pl.when(z < zs - 1)
                def _():
                    z_copy(view, sems, h, 0, zz).start()

                x_copy(view, sems, h, zz, x).start()
                s_copy(view, sems, h, zz, x, core).start()

            @pl.when(z + k < zs)
            def _():
                zz = z + k
                z_copy(view, sems, h, 1, zz).wait_recv()

                @pl.when(z > 0)
                def _():
                    z_copy(view, sems, h, 1, zz).start()

                x_copy(view, sems, h, zz, x).start()
                s_copy(view, sems, h, zz, x, core).start()

        def from_across(zz):
            x_copy(view, sems, h, zz, 1 - x).wait_recv()
            s_copy(view, sems, h, zz, 1 - x, core).start()

        if k == 1:
            from_across(z)
        else:

            @pl.when(z >= k - 1)
            def _():
                from_across(z - k + 1)

            @pl.when(z + k - 1 < zs)
            def _():
                from_across(z + k - 1)

    def gathered(view, sems, h):
        def one(zz, carry):
            s_copy(view, sems, h, zz, x, 1 - core).wait_recv()
            s_copy(view, sems, h, zz, 1 - x, 1 - core).wait_recv()
            return carry

        lax.fori_loop(0, zs, one, 0)

    def drained(view, sems, h):
        def one(zz, carry):
            s_copy(view, sems, h, zz, x, core).wait_send()
            s_copy(view, sems, h, zz, 1 - x, core).wait_send()
            x_copy(view, sems, h, zz, x).wait_send()

            @pl.when((zz <= z) & (z < zs - 1))
            def _():
                z_copy(view, sems, h, 0, zz).wait_send()

            @pl.when((zz >= z) & (z > 0))
            def _():
                z_copy(view, sems, h, 1, zz).wait_send()

            return carry

        lax.fori_loop(0, zs, one, 0)

    w_sems = (wzs, wzr, wxs, wxr, wss, wsr)
    g_sems = (gzs, gzr, gxs, gxr, gss, gsr)
    early = zs // 2
    for load in loads:
        load.wait()
    for h in range(kh):
        begin(w_view, w_sems, h)

    def picked(table, row, target, slot):
        total = jnp.int32(0)
        for c in range(4):
            total = total + jnp.where(dest_shard[row, c] == target, table[row, c], 0)
        return total

    home_plan, dest_plan = [], []
    for stride in strides:
        target = lax.rem(me + stride, n)
        source = lax.rem(me - stride + n, n)
        home_plan.append(
            (picked(home_offset, me, target, 0), picked(seq_length, me, target, 0))
        )
        dest_plan.append(
            (picked(dest_offset, source, me, 0), picked(seq_length, source, me, 0))
        )

    def cut(plan, rows):
        w = lax.broadcasted_iota(jnp.int32, (MAXLEN, rows), 0)
        r = lax.broadcasted_iota(jnp.int32, (MAXLEN, rows), 1)
        return jnp.concatenate(
            [
                jnp.where((w < length) & (r == start + w), 1.0, 0.0)
                for start, length in plan
            ],
            0,
        ).astype(BF16)

    def uncut(plan, rows):
        place = lax.broadcasted_iota(jnp.int32, (rows, 4 * MAXLEN), 1)
        r = lax.broadcasted_iota(jnp.int32, (rows, 4 * MAXLEN), 0)
        total = jnp.zeros((rows, 4 * MAXLEN), F32)
        for e, (start, length) in enumerate(plan):
            w = place - e * MAXLEN
            total = jnp.where((w >= 0) & (w < length) & (r == start + w), 1.0, total)
        return total.astype(BF16)

    picks = cut(dest_plan, CAP)
    for i in range(tp):
        columns = slice(i * TILE, (i + 1) * TILE)
        cot_send[:, :, columns] = (
            mm(picks, cotangent[:, columns]).astype(BF16).reshape(4, MAXLEN, TILE)
        )
    cot_copies = [
        remote(
            cot_send.at[e],
            cot_recv.at[e],
            csend.at[e],
            crecv.at[e],
            {"dp": lax.rem(me - strides[e] + n, n)},
        )
        for e in range(4)
    ]
    for copy in cot_copies:
        copy.start()
    for k in range(1, early):
        step(w_view, w_sems, 0, k)

    for copy in tensor_copies:
        copy.wait_send()
    for j in range(1, nt):
        theirs = pl.ds(lax.rem(t - j + nt, nt) * tp, tp)
        peer = {"tensor": lax.rem(t + j, nt)}
        remote(hid.at[theirs], hid.at[theirs], hsend.at[j, 0], hrecv.at[j, 0], peer).wait_recv()
        remote(gbuf.at[theirs], gbuf.at[theirs], hsend.at[j, 1], hrecv.at[j, 1], peer).wait_recv()
    squares = jnp.zeros((TOK_DEV, 1), F32)
    for j in range(TILES):
        values = hid[j].astype(F32)
        squares = squares + jnp.sum(values * values, 1, keepdims=True)
    inverse_rms = lax.rsqrt(squares * (1.0 / D) + EPSILON)
    for j in range(TILES):
        rows = (hid[j].astype(F32) * inverse_rms * gbuf[j, 0:1, :]).astype(BF16)
        nrm[j] = rows
        for i in range(TILE // blk):
            nblk[j * (TILE // blk) + i] = rows[:, i * blk : (i + 1) * blk]
    my_tokens = pl.ds(pl.multiple_of(me * TOK_DEV, TOK_DEV), TOK_DEV)
    share = TOK_DEV // nt
    my_share = pl.ds(pl.multiple_of(t * share, share), share)

    def norm_copy(j, src, dst):
        return remote(
            nblk.at[src, my_share],
            ncol.at[dst, my_share],
            bsend.at[j],
            brecv.at[j],
            {"dp": lax.rem(me + j, n)},
        )

    def norm_start(j, carry):
        norm_copy(j, lax.rem(me + j, n), me).start()
        return carry

    lax.fori_loop(1, n, norm_start, 0)
    ncol[me, my_share, :] = nblk[me, my_share, :]

    def share_copy(j, shard):
        rows = pl.ds(pl.multiple_of(shard * share, share), share)
        block = ncol.at[:, rows]
        return remote(
            block, block, ysend.at[j], yrecv.at[j], {"tensor": lax.rem(t + j, nt)}
        )

    def share_rows():
        def norm_wait(j, carry):
            norm_copy(j, lax.rem(me + j, n), lax.rem(me - j + n, n)).wait_recv()
            norm_copy(j, lax.rem(me + j, n), me).wait_send()
            return carry

        lax.fori_loop(1, n, norm_wait, 0)
        for j in range(1, nt):
            share_copy(j, t).start()

    step(w_view, w_sems, 0, early)

    row = lax.broadcasted_iota(jnp.int32, (TOK_DEV, TOK_DEV), 0)
    col = lax.broadcasted_iota(jnp.int32, (TOK_DEV, TOK_DEV), 1)
    row_start = jnp.zeros((TOK_DEV, TOK_DEV), jnp.int32)
    col_start = jnp.zeros((TOK_DEV, TOK_DEV), jnp.int32)
    for start, length in home_plan:
        row_start = jnp.where((row >= start) & (row < start + length), start, row_start)
        col_start = jnp.where((col >= start) & (col < start + length), start, col_start)
    bias = jnp.where((row_start == col_start) & (col <= row), 0.0, -1e30).astype(F32)
    bias = jnp.concatenate([bias] * GROUP, 0)
    angles = (row - row_start).astype(F32) * freq[0:1, :]
    cosine = jnp.cos(angles)
    sine = jnp.sin(angles) * jnp.where(col < HEAD // 2, -1.0, 1.0)

    def rotate(values, sine_part):
        return values * cosine + pltpu.roll(values, HEAD // 2, 1) * sine_part

    for copy in cot_copies:
        copy.wait()
    picks = uncut(home_plan, TOK_DEV)
    for h in range(kh):
        arrived = cot_recv[:, :, h * TILE : (h + 1) * TILE].reshape(4 * MAXLEN, TILE)
        cot_home[h] = mm(picks, arrived).astype(BF16)

    for j in range(TILES):
        pacc[j] = jnp.zeros((TILE, TOK_DEV), F32)

    def out_copy(h, e):
        return remote(
            out_send.at[h, e],
            out_recv.at[h, e],
            osend.at[h, e],
            orecv.at[h, e],
            {"dp": lax.rem(me + strides[e], n)},
        )

    def project_head(h, first, last):
        def project(j, carry):
            rows = pl.ds(pl.multiple_of(j * TILE, TILE), TILE)
            acc[...] += mm(nrm[j], wbuf[h, rows, :])
            return carry

        lax.fori_loop(first, last, project, 0)

    def attend_head(h):
        query = jnp.concatenate(
            [rotate(acc[:, g * HEAD : (g + 1) * HEAD], sine) for g in range(GROUP)], 0
        ).astype(BF16)
        key = rotate(acc[:, GROUP * HEAD : (GROUP + 1) * HEAD], sine).astype(BF16)
        value = acc[:, (GROUP + 1) * HEAD :].astype(BF16)
        factor = HEAD**-0.5
        scores = mm(query, key, NT) * factor + bias
        exp_terms = jnp.exp(scores - jnp.max(scores, -1, keepdims=True))
        probs = exp_terms / jnp.sum(exp_terms, -1, keepdims=True)
        probs_low = probs.astype(BF16)
        mixed = mm(probs_low, value).astype(BF16)
        cot = cot_home[h]
        grad_out = jnp.concatenate(
            [cot[:, g * HEAD : (g + 1) * HEAD] for g in range(GROUP)], 0
        )
        grad_value = mm(probs_low, grad_out, TN)
        grad_probs = mm(grad_out, value, NT)
        centre = jnp.sum(grad_probs * probs, -1, keepdims=True)
        grad_scores = (probs * (grad_probs - centre) * factor).astype(BF16)
        grad_query = mm(grad_scores, key)
        grad_key = rotate(mm(grad_scores, query, TN), -sine)
        attn = jnp.concatenate(
            [mixed[g * TOK_DEV : (g + 1) * TOK_DEV] for g in range(GROUP)], 1
        )
        out_send[h] = (
            mm(cut(home_plan, TOK_DEV), attn).astype(BF16).reshape(4, MAXLEN, TILE)
        )
        for e in range(4):
            out_copy(h, e).start()
        gvbuf[h, my_tokens, :] = grad_value.astype(BF16)
        grads = jnp.concatenate(
            [
                rotate(grad_query[g * TOK_DEV : (g + 1) * TOK_DEV], -sine).T
                for g in range(GROUP)
            ]
            + [grad_key.T, grad_value.T],
            0,
        )
        grads_t[...] = grads.astype(BF16)
        begin(g_view, g_sems, h)

    def back_head(h):
        def back(j, carry):
            rows = pl.ds(pl.multiple_of(j * TILE, TILE), TILE)
            pacc[j] += mm(wbuf[h, rows, :], grads_t[...])
            return carry

        lax.fori_loop(0, TILES, back, 0)

    def round_of(h, carry):
        for k in range(1, early + 1):

            @pl.when(h < kh)
            def _():
                step(w_view, w_sems, h, early + k)

            @pl.when((h >= 2) & (h < kh))
            def _():
                step(g_view, g_sems, h - 2, 2 * k - 1)
                step(g_view, g_sems, h - 2, 2 * k)

            if k == 1:

                @pl.when(h >= 1)
                def _():
                    gathered(w_view, w_sems, h - 1)
                    acc[...] = jnp.zeros_like(acc)
                    project_head(h - 1, 0, TILES // 2)

            if k == 2:

                @pl.when(h >= 1)
                def _():
                    attend_head(h - 1)

            @pl.when(h + 1 < kh)
            def _():
                step(w_view, w_sems, h + 1, k)

            if k == 1:

                @pl.when(h >= 1)
                def _():
                    project_head(h - 1, TILES // 2, TILES)

            if k == 2:

                @pl.when(h >= 1)
                def _():
                    back_head(h - 1)

        @pl.when(h == 1)
        def _():
            share_rows()

        return carry

    lax.fori_loop(0, kh + 1, round_of, 0)

    last = range(max(kh - 2, 0), kh)
    dots = jnp.zeros((TOK_DEV, 1), F32)
    for j in range(TILES):
        low = pacc[j].T.astype(BF16)
        psend[j] = low
        dots = dots + jnp.sum(
            low.astype(F32) * gbuf[j, 0:1, :] * hid[j].astype(F32), 1, keepdims=True
        )
    rsend[...] = jnp.broadcast_to(dots, (TOK_DEV, HEAD))
    term_copies = []
    for j in range(1, nt):
        to = lax.rem(t + j, nt)
        peer = {"tensor": to}
        term_copies.append(
            remote(
                psend.at[pl.ds(to * tp, tp)], precv.at[j - 1], psems.at[j], prems.at[j], peer
            )
        )
        term_copies.append(remote(rsend, rrecv.at[j - 1], rsems.at[j], rrems.at[j], peer))
    for copy in term_copies:
        copy.start()
    def place_out(h):
        for e in range(4):
            out_copy(h, e).wait()
        arrived = out_recv[h].reshape(4 * MAXLEN, TILE)
        out_ref[:, h * TILE : (h + 1) * TILE] = mm(uncut(dest_plan, CAP), arrived).astype(BF16)

    for k in range(1, zs + 1):
        for h in last:
            step(g_view, g_sems, h, k)
        if k <= kh:
            place_out(k - 1)
    for copy in term_copies:
        copy.wait()
    row_dot = rsend[:, 0:1]
    for j in range(1, nt):
        row_dot = row_dot + rrecv[j - 1, :, 0:1]
    for i in range(tp):
        summed = psend[t * tp + i].astype(F32)
        for j in range(1, nt):
            summed = summed + precv[j - 1, i].astype(F32)
        weighted = summed * gbuf[t * tp + i, 0:1, :]
        gh_ref[:, i * TILE : (i + 1) * TILE] = (
            inverse_rms * weighted
            - hid[t * tp + i].astype(F32) * inverse_rms**3 * row_dot * (1.0 / D)
        ).astype(BF16)

    for j in range(1, nt):
        share_copy(j, t).wait_send()
        share_copy(j, lax.rem(t - j + nt, nt)).wait_recv()
    for h in range(kh):
        gathered(g_view, g_sems, h)
    gvw_acc[...] = jnp.zeros_like(gvw_acc)

    def weigh(c, carry):
        rows = pl.ds(pl.multiple_of(c * TILE, TILE), TILE)
        owners = pl.ds(c * (TILE // TOK_DEV), TILE // TOK_DEV)
        columns = ncol[owners].reshape(TILE, blk)
        values = jnp.concatenate([gvbuf[h, rows, :] for h in range(kh)], 1)
        gvw_acc[...] += mm(columns, values, TN)
        return carry

    lax.fori_loop(0, n * TOK_DEV // TILE, weigh, 0)
    gvw_ref[...] = gvw_acc[...]

    def finish(h, carry):
        drained(w_view, w_sems, h)
        drained(g_view, g_sems, h)
        return carry

    lax.fori_loop(0, kh, finish, 0)


def split_kernel(
    n,
    nt,
    seq_length,
    home_offset,
    dest_shard,
    dest_offset,
    hidden,
    gain,
    freq,
    cotangent,
    w_query,
    w_key,
    w_value,
    out_ref,
    gh_ref,
    gvw_ref,
    wbuf,
    hid,
    gbuf,
    cosines,
    sines,
    biases,
    cot_across,
    attn_out,
    attn_in,
    pxs,
    pxr,
    nblk,
    ncol,
    cot_send,
    cot_recv,
    cot_home,
    acc,
    grads_t,
    pacc,
    psend,
    precv,
    rsend,
    rrecv,
    gvbuf,
    out_send,
    out_recv,
    gvw_acc,
    load_sem,
    wzs,
    wzr,
    wxs,
    wxr,
    wss,
    wsr,
    gzs,
    gzr,
    gxs,
    gxr,
    gss,
    gsr,
    ysend,
    yrecv,
    ysends,
    yrecvs,
    qsend,
    qrecv,
    hsend,
    hrecv,
    bsend,
    brecv,
    csend,
    crecv,
    asend,
    arecv,
    osend,
    orecv,
    psems,
    prems,
    rsems,
    rrems,
):
    me = lax.axis_index("dp")
    t = lax.axis_index("tensor")
    kh = gvbuf.shape[0]
    hh = kh // 2
    blk = D // n
    tp = TILES // nt
    zs = n // 4
    core = lax.rem(me, 2)
    chip = lax.div(me, 2)
    z, x = lax.div(chip, 2), lax.rem(chip, 2)
    sibling = me + 1 - 2 * core
    across = me + 2 - 4 * x
    spot = 4 * z + 2 * core + x
    other_spot = spot + 1 - 2 * x
    strides = [n - 1, 1, n // 2, n // 2 + 1]

    barrier = pltpu.get_barrier_semaphore()

    def greet(j, carry):
        pl.semaphore_signal(
            barrier,
            inc=1,
            device_id={"dp": lax.rem(me + j, n)},
            device_id_type=pl.DeviceIdType.MESH,
        )
        return carry

    lax.fori_loop(1, n, greet, 0)
    for j in range(1, nt):
        pl.semaphore_signal(
            barrier,
            inc=1,
            device_id={"tensor": lax.rem(t + j, nt)},
            device_id_type=pl.DeviceIdType.MESH,
        )

    def remote(src, dst, ssem, rsem, where):
        return pltpu.make_async_remote_copy(
            src_ref=src,
            dst_ref=dst,
            send_sem=ssem,
            recv_sem=rsem,
            device_id=where,
            device_id_type=pl.DeviceIdType.MESH,
        )

    def shard_parts(h, which):
        head = which * hh + h
        for part, (src, first, width) in enumerate(
            (
                (w_query, 0, GROUP * HEAD),
                (w_key, GROUP * HEAD, HEAD),
                (w_value, (GROUP + 1) * HEAD, HEAD),
            )
        ):
            yield part, src.at[:, pl.ds(pl.multiple_of(head * width, width), width)], pl.ds(
                first, width
            )

    def rows_at(where):
        return pl.ds(pl.multiple_of(where * blk, blk), blk)

    def loads_of(h):
        return [
            pltpu.make_async_copy(src, wbuf.at[h, rows_at(spot), cols], load_sem.at[h, part])
            for part, src, cols in shard_parts(h, x)
        ]

    def swaps_of(h, where):
        return [
            remote(
                src,
                wbuf.at[h, rows_at(where), cols],
                wxs.at[h, part],
                wxr.at[h, part],
                {"dp": across},
            )
            for part, src, cols in shard_parts(h, 1 - x)
        ]

    for h in range(hh):
        for load in loads_of(h):
            load.start()

    for i in range(tp):
        hid[t * tp + i] = hidden[:, i * TILE : (i + 1) * TILE]
        gbuf[t * tp + i] = jnp.broadcast_to(gain[:, i * TILE : (i + 1) * TILE], (8, TILE))

    pl.semaphore_wait(barrier, n - 1 + nt - 1)

    for h in range(hh):
        for swap in swaps_of(h, spot):
            swap.start()

    own_tiles = pl.ds(t * tp, tp)
    tensor_copies = []
    for j in range(1, nt):
        peer = {"tensor": lax.rem(t + j, nt)}
        tensor_copies.append(
            remote(hid.at[own_tiles], hid.at[own_tiles], hsend.at[j, 0], hrecv.at[j, 0], peer)
        )
        tensor_copies.append(
            remote(gbuf.at[own_tiles], gbuf.at[own_tiles], hsend.at[j, 1], hrecv.at[j, 1], peer)
        )
    for copy in tensor_copies:
        copy.start()

    def w_view(h, zz, xx, which):
        rows = pl.multiple_of((4 * zz + 2 * which + lax.rem(h, 2)) * blk, blk)
        return wbuf.at[lax.div(h, 2), pl.ds(rows, blk)]

    def g_view(h, zz, xx, which):
        rows = pl.multiple_of((4 * zz + 2 * which) * TOK_DEV, 2 * TOK_DEV)
        return gvbuf.at[xx * hh + h, pl.ds(rows, 2 * TOK_DEV)]

    up, down = lax.rem(me + 4, n), lax.rem(me - 4 + n, n)

    def z_copy(view, sems, h, way, zz):
        block = view(h, zz, x, core)
        return remote(
            block,
            block,
            sems[0].at[h, way, zz],
            sems[1].at[h, zz],
            {"dp": up if way == 0 else down},
        )

    def x_copy(view, sems, h, zz, xx):
        block = view(h, zz, xx, core)
        return remote(block, block, sems[2].at[h, zz], sems[3].at[h, zz], {"dp": across})

    def s_copy(view, sems, h, zz, xx, which):
        block = view(h, zz, xx, which)
        return remote(
            block, block, sems[4].at[h, xx, zz], sems[5].at[h, xx, zz], {"dp": sibling}
        )

    def begin(view, sems, h):
        @pl.when(z < zs - 1)
        def _():
            z_copy(view, sems, h, 0, z).start()

        @pl.when(z > 0)
        def _():
            z_copy(view, sems, h, 1, z).start()

        if sems is g_sems:
            x_copy(view, sems, h, z, x).start()
        s_copy(view, sems, h, z, x, core).start()

    def step(view, sems, h, k):
        if k < zs:

            @pl.when(z >= k)
            def _():
                zz = z - k
                z_copy(view, sems, h, 0, zz).wait_recv()

                @pl.when(z < zs - 1)
                def _():
                    z_copy(view, sems, h, 0, zz).start()

                if sems is g_sems:
                    x_copy(view, sems, h, zz, x).start()
                s_copy(view, sems, h, zz, x, core).start()

            @pl.when(z + k < zs)
            def _():
                zz = z + k
                z_copy(view, sems, h, 1, zz).wait_recv()

                @pl.when(z > 0)
                def _():
                    z_copy(view, sems, h, 1, zz).start()

                if sems is g_sems:
                    x_copy(view, sems, h, zz, x).start()
                s_copy(view, sems, h, zz, x, core).start()

        if sems is w_sems:
            return

        def from_across(zz):
            x_copy(view, sems, h, zz, 1 - x).wait_recv()
            s_copy(view, sems, h, zz, 1 - x, core).start()

        if k == 1:
            from_across(z)
        else:

            @pl.when(z >= k - 1)
            def _():
                from_across(z - k + 1)

            @pl.when(z + k - 1 < zs)
            def _():
                from_across(z + k - 1)

    def gathered(view, sems, h):
        def one(zz, carry):
            s_copy(view, sems, h, zz, x, 1 - core).wait_recv()
            if sems is g_sems:
                s_copy(view, sems, h, zz, 1 - x, 1 - core).wait_recv()
            return carry

        lax.fori_loop(0, zs, one, 0)

    def drained(view, sems, h):
        def one(zz, carry):
            s_copy(view, sems, h, zz, x, core).wait_send()
            if sems is g_sems:
                s_copy(view, sems, h, zz, 1 - x, core).wait_send()
                x_copy(view, sems, h, zz, x).wait_send()

            @pl.when((zz <= z) & (z < zs - 1))
            def _():
                z_copy(view, sems, h, 0, zz).wait_send()

            @pl.when((zz >= z) & (z > 0))
            def _():
                z_copy(view, sems, h, 1, zz).wait_send()

            return carry

        lax.fori_loop(0, zs, one, 0)

    w_sems = (wzs, wzr, None, None, wss, wsr)
    g_sems = (gzs, gzr, gxs, gxr, gss, gsr)
    early = zs // 2
    def w_step(h, k):
        step(w_view, w_sems, 2 * h, k)
        step(w_view, w_sems, 2 * h + 1, k)

    def begin_weights(h):
        for load in loads_of(h):
            load.wait()
        for swap in swaps_of(h, other_spot):
            swap.wait_recv()
        begin(w_view, w_sems, 2 * h)
        begin(w_view, w_sems, 2 * h + 1)

    begin_weights(0)

    def picked(table, row, target, slot):
        total = jnp.int32(0)
        for c in range(4):
            total = total + jnp.where(dest_shard[row, c] == target, table[row, c], 0)
        return total

    home_plan, dest_plan, across_plan = [], [], []
    for stride in strides:
        target = lax.rem(across + stride, n)
        across_plan.append(
            (
                picked(home_offset, across, target, 0),
                picked(seq_length, across, target, 0),
            )
        )
        target = lax.rem(me + stride, n)
        source = lax.rem(me - stride + n, n)
        home_plan.append(
            (picked(home_offset, me, target, 0), picked(seq_length, me, target, 0))
        )
        dest_plan.append(
            (picked(dest_offset, source, me, 0), picked(seq_length, source, me, 0))
        )

    def cut(plan, rows):
        w = lax.broadcasted_iota(jnp.int32, (MAXLEN, rows), 0)
        r = lax.broadcasted_iota(jnp.int32, (MAXLEN, rows), 1)
        return jnp.concatenate(
            [
                jnp.where((w < length) & (r == start + w), 1.0, 0.0)
                for start, length in plan
            ],
            0,
        ).astype(BF16)

    def uncut(plan, rows):
        place = lax.broadcasted_iota(jnp.int32, (rows, 4 * MAXLEN), 1)
        r = lax.broadcasted_iota(jnp.int32, (rows, 4 * MAXLEN), 0)
        total = jnp.zeros((rows, 4 * MAXLEN), F32)
        for e, (start, length) in enumerate(plan):
            w = place - e * MAXLEN
            total = jnp.where((w >= 0) & (w < length) & (r == start + w), 1.0, total)
        return total.astype(BF16)

    picks = cut(dest_plan, CAP)
    for i in range(tp):
        columns = slice(i * TILE, (i + 1) * TILE)
        cot_send[:, :, columns] = (
            mm(picks, cotangent[:, columns]).astype(BF16).reshape(4, MAXLEN, TILE)
        )
    cot_copies = [
        remote(
            cot_send.at[e],
            cot_recv.at[e],
            csend.at[e],
            crecv.at[e],
            {"dp": lax.rem(me - strides[e] + n, n)},
        )
        for e in range(4)
    ]
    for copy in cot_copies:
        copy.start()
    for h in range(1, hh):
        begin_weights(h)
    for k in range(1, early):
        w_step(0, k)

    for copy in tensor_copies:
        copy.wait_send()
    for j in range(1, nt):
        theirs = pl.ds(lax.rem(t - j + nt, nt) * tp, tp)
        peer = {"tensor": lax.rem(t + j, nt)}
        remote(hid.at[theirs], hid.at[theirs], hsend.at[j, 0], hrecv.at[j, 0], peer).wait_recv()
        remote(gbuf.at[theirs], gbuf.at[theirs], hsend.at[j, 1], hrecv.at[j, 1], peer).wait_recv()
    squares = jnp.zeros((TOK_DEV, 1), F32)
    for j in range(TILES):
        values = hid[j].astype(F32)
        squares = squares + jnp.sum(values * values, 1, keepdims=True)
    inverse_rms = lax.rsqrt(squares * (1.0 / D) + EPSILON)
    for j in range(TILES):
        rows = (hid[j].astype(F32) * inverse_rms * gbuf[j, 0:1, :]).astype(BF16)
        for i in range(TILE // blk):
            nblk[x, j * (TILE // blk) + i] = rows[:, i * blk : (i + 1) * blk]
    row_swap = remote(nblk.at[x], nblk.at[x], qsend.at[0], qrecv.at[0], {"dp": across})
    row_swap.start()
    share = TOK_DEV // nt
    my_share = pl.ds(pl.multiple_of(t * share, share), share)

    def norm_copy(j, src, dst):
        return remote(
            nblk.at[x, src, my_share],
            ncol.at[dst, my_share],
            bsend.at[j],
            brecv.at[j],
            {"dp": lax.rem(me + j, n)},
        )

    def norm_start(j, carry):
        norm_copy(j, lax.rem(me + j, n), spot).start()
        return carry

    lax.fori_loop(1, n, norm_start, 0)
    ncol[spot, my_share, :] = nblk[x, me, my_share, :]

    def share_copy(j, shard):
        rows = pl.ds(pl.multiple_of(shard * share, share), share)
        block = ncol.at[:, rows]
        return remote(
            block, block, ysend.at[j], yrecv.at[j], {"tensor": lax.rem(t + j, nt)}
        )

    def share_rows():
        def norm_wait(j, carry):
            sender = lax.rem(me - j + n, n)
            side = lax.rem(sender, 4)
            where = sender - side + 2 * lax.rem(side, 2) + lax.div(side, 2)
            norm_copy(j, lax.rem(me + j, n), where).wait_recv()
            norm_copy(j, lax.rem(me + j, n), spot).wait_send()
            return carry

        lax.fori_loop(1, n, norm_wait, 0)
        for j in range(1, nt):
            share_copy(j, t).start()

    w_step(0, early)

    row = lax.broadcasted_iota(jnp.int32, (TOK_DEV, TOK_DEV), 0)
    col = lax.broadcasted_iota(jnp.int32, (TOK_DEV, TOK_DEV), 1)

    def tables(plan):
        row_start = jnp.zeros((TOK_DEV, TOK_DEV), jnp.int32)
        col_start = jnp.zeros((TOK_DEV, TOK_DEV), jnp.int32)
        for start, length in plan:
            row_start = jnp.where((row >= start) & (row < start + length), start, row_start)
            col_start = jnp.where((col >= start) & (col < start + length), start, col_start)
        bias = jnp.where((row_start == col_start) & (col <= row), 0.0, -1e30).astype(F32)
        angles = (row - row_start).astype(F32) * freq[0:1, :]
        sine = jnp.sin(angles) * jnp.where(col < HEAD // 2, -1.0, 1.0)
        return jnp.cos(angles), sine, jnp.concatenate([bias] * GROUP, 0)

    for side, plan in enumerate((home_plan, across_plan)):
        cosines[side], sines[side], biases[side] = tables(plan)

    def rotate(values, cosine, sine_part):
        return values * cosine + pltpu.roll(values, HEAD // 2, 1) * sine_part

    for copy in cot_copies:
        copy.wait()
    picks = uncut(home_plan, TOK_DEV)
    for h in range(kh):
        arrived = cot_recv[:, :, h * TILE : (h + 1) * TILE].reshape(4 * MAXLEN, TILE)
        cot_home[h] = mm(picks, arrived).astype(BF16)

    cot_swap = remote(
        cot_home.at[pl.ds((1 - x) * hh, hh)], cot_across, qsend.at[1], qrecv.at[1], {"dp": across}
    )
    cot_swap.start()

    for j in range(n):
        pacc[j] = jnp.zeros((blk, 2 * TOK_DEV), F32)
    cot_swap.wait()
    row_swap.wait()

    def out_copy(h, e):
        return remote(
            out_send.at[h, e],
            out_recv.at[h, e],
            osend.at[h, e],
            orecv.at[h, e],
            {"dp": lax.rem(me + strides[e], n)},
        )

    def project_head(h, first, last):
        def project(j, carry):
            side = lax.rem(j, 4)
            shard = j - side + 2 * lax.rem(side, 2) + lax.div(side, 2)
            rows = pl.ds(pl.multiple_of(j * blk, blk), blk)
            both = jnp.concatenate([nblk[x, shard], nblk[1 - x, shard]], 0)
            acc[...] += mm(both, wbuf[h, rows, :])
            return carry

        lax.fori_loop(first, last, project, 0)

    def attn_copy(h):
        return remote(
            attn_out.at[h], attn_in.at[h], ysends.at[h], yrecvs.at[h], {"dp": across}
        )

    def send_out(head, attn):
        out_send[head] = (
            mm(cut(home_plan, TOK_DEV), attn).astype(BF16).reshape(4, MAXLEN, TILE)
        )
        for e in range(4):
            out_copy(head, e).start()

    def attend_side(h, side, where):
        first = side * TOK_DEV
        rows = slice(first, first + TOK_DEV)
        cosine, sine = cosines[side], sines[side]
        query = jnp.concatenate(
            [
                rotate(acc[rows, g * HEAD : (g + 1) * HEAD], cosine, sine)
                for g in range(GROUP)
            ],
            0,
        ).astype(BF16)
        key = rotate(acc[rows, GROUP * HEAD : (GROUP + 1) * HEAD], cosine, sine).astype(BF16)
        value = acc[rows, (GROUP + 1) * HEAD :].astype(BF16)
        factor = HEAD**-0.5
        scores = mm(query, key, NT) * factor + biases[side]
        exp_terms = jnp.exp(scores - jnp.max(scores, -1, keepdims=True))
        probs = exp_terms / jnp.sum(exp_terms, -1, keepdims=True)
        probs_low = probs.astype(BF16)
        mixed = mm(probs_low, value).astype(BF16)
        cot = cot_home[x * hh + h] if side == 0 else cot_across[h]
        grad_out = jnp.concatenate(
            [cot[:, g * HEAD : (g + 1) * HEAD] for g in range(GROUP)], 0
        )
        grad_value = mm(probs_low, grad_out, TN)
        grad_probs = mm(grad_out, value, NT)
        centre = jnp.sum(grad_probs * probs, -1, keepdims=True)
        grad_scores = (probs * (grad_probs - centre) * factor).astype(BF16)
        grad_query = mm(grad_scores, key)
        grad_key = rotate(mm(grad_scores, query, TN), cosine, -sine)
        attn = jnp.concatenate(
            [mixed[g * TOK_DEV : (g + 1) * TOK_DEV] for g in range(GROUP)], 1
        )
        if side == 0:
            send_out(x * hh + h, attn)
        else:
            attn_out[h] = attn
            attn_copy(h).start()
        tokens = pl.ds(pl.multiple_of(where * TOK_DEV, TOK_DEV), TOK_DEV)
        gvbuf[x * hh + h, tokens, :] = grad_value.astype(BF16)
        grads = jnp.concatenate(
            [
                rotate(grad_query[g * TOK_DEV : (g + 1) * TOK_DEV], cosine, -sine).T
                for g in range(GROUP)
            ]
            + [grad_key.T, grad_value.T],
            0,
        )
        grads_t[:, rows] = grads.astype(BF16)

    def attend_head(h):
        attend_side(h, 1, other_spot)
        attend_side(h, 0, spot)
        begin(g_view, g_sems, h)

    def from_other(h):
        attn_copy(h).wait()
        send_out((1 - x) * hh + h, attn_in[h])

    def back_head(h):
        def back(j, carry):
            rows = pl.ds(pl.multiple_of(j * blk, blk), blk)
            pacc[j] += mm(wbuf[h, rows, :], grads_t[...])
            return carry

        lax.fori_loop(0, n, back, 0)

    def round_of(h, carry):
        for k in range(1, early + 1):

            @pl.when(h < hh)
            def _():
                w_step(h, early + k)

            if k == 1:

                @pl.when(h >= 1)
                def _():
                    gathered(w_view, w_sems, 2 * h - 2)
                    gathered(w_view, w_sems, 2 * h - 1)
                    acc[...] = jnp.zeros_like(acc)
                    project_head(h - 1, 0, n // 2)

            if k == 2:

                @pl.when(h >= 1)
                def _():
                    attend_head(h - 1)

            @pl.when(h >= 2)
            def _():
                step(g_view, g_sems, h - 2, 2 * k - 1)
                step(g_view, g_sems, h - 2, 2 * k)

            @pl.when(h + 1 < hh)
            def _():
                w_step(h + 1, k)

            if k == 1:

                @pl.when(h >= 1)
                def _():
                    project_head(h - 1, n // 2, n)

            if k == 2:

                @pl.when(h >= 1)
                def _():
                    back_head(h - 1)

        @pl.when(h >= 2)
        def _():
            from_other(h - 2)

        @pl.when(h == 1)
        def _():
            share_rows()

        return carry

    lax.fori_loop(0, hh + 1, round_of, 0)

    last = range(hh - 1, hh)
    half_swaps = []
    for j in range(n):
        pxs[j] = pacc[j, :, TOK_DEV:].astype(BF16)
        if j % 4 == 3:
            piece = pl.ds(j - 3, 4)
            half_swaps.append(
                remote(
                    pxs.at[piece],
                    pxr.at[piece],
                    qsend.at[2 + j // 4],
                    qrecv.at[2 + j // 4],
                    {"dp": across},
                )
            )
            half_swaps[-1].start()
    from_other(hh - 1)
    for h in last:
        step(g_view, g_sems, h, 1)
    for j in range(n):
        if j % 4 == 0:
            half_swaps[j // 4].wait()
        total = pacc[j, :, :TOK_DEV] + pxr[j].astype(F32)
        shard = j - j % 4 + 2 * (j % 2) + (j % 4) // 2
        first = shard * blk % TILE
        psend[shard * blk // TILE, :, first : first + blk] = total.T.astype(BF16)
    dots = jnp.zeros((TOK_DEV, 1), F32)
    for j in range(TILES):
        low = psend[j]
        dots = dots + jnp.sum(
            low.astype(F32) * gbuf[j, 0:1, :] * hid[j].astype(F32), 1, keepdims=True
        )
    rsend[...] = jnp.broadcast_to(dots, (TOK_DEV, HEAD))
    term_copies = []
    for j in range(1, nt):
        to = lax.rem(t + j, nt)
        peer = {"tensor": to}
        term_copies.append(
            remote(
                psend.at[pl.ds(to * tp, tp)], precv.at[j - 1], psems.at[j], prems.at[j], peer
            )
        )
        term_copies.append(remote(rsend, rrecv.at[j - 1], rsems.at[j], rrems.at[j], peer))
    for copy in term_copies:
        copy.start()
    def place_out(h):
        for e in range(4):
            out_copy(h, e).wait()
        arrived = out_recv[h].reshape(4 * MAXLEN, TILE)
        out_ref[:, h * TILE : (h + 1) * TILE] = mm(uncut(dest_plan, CAP), arrived).astype(BF16)

    for k in range(1, zs + 1):
        for h in last:
            if k > 1:
                step(g_view, g_sems, h, k)
        if k <= kh:
            place_out(k - 1)
    for copy in term_copies:
        copy.wait()
    row_dot = rsend[:, 0:1]
    for j in range(1, nt):
        row_dot = row_dot + rrecv[j - 1, :, 0:1]
    for i in range(tp):
        summed = psend[t * tp + i].astype(F32)
        for j in range(1, nt):
            summed = summed + precv[j - 1, i].astype(F32)
        weighted = summed * gbuf[t * tp + i, 0:1, :]
        gh_ref[:, i * TILE : (i + 1) * TILE] = (
            inverse_rms * weighted
            - hid[t * tp + i].astype(F32) * inverse_rms**3 * row_dot * (1.0 / D)
        ).astype(BF16)

    for j in range(1, nt):
        share_copy(j, t).wait_send()
        share_copy(j, lax.rem(t - j + nt, nt)).wait_recv()
    for h in range(hh):
        gathered(g_view, g_sems, h)
    gvw_acc[...] = jnp.zeros_like(gvw_acc)

    def weigh(c, carry):
        rows = pl.ds(pl.multiple_of(c * TILE, TILE), TILE)
        owners = pl.ds(c * (TILE // TOK_DEV), TILE // TOK_DEV)
        columns = ncol[owners].reshape(TILE, blk)
        values = jnp.concatenate([gvbuf[h, rows, :] for h in range(kh)], 1)
        gvw_acc[...] += mm(columns, values, TN)
        return carry

    lax.fori_loop(0, n * TOK_DEV // TILE, weigh, 0)
    gvw_ref[...] = gvw_acc[...]

    def finish(h, carry):
        drained(w_view, w_sems, 2 * h)
        drained(w_view, w_sems, 2 * h + 1)
        drained(g_view, g_sems, h)
        return carry

    lax.fori_loop(0, hh, finish, 0)
    for h in range(hh):
        for swap in swaps_of(h, spot):
            swap.wait_send()


def on_device(
    hidden,
    gain,
    w_query,
    w_key,
    w_value,
    cotangent,
    seq_length,
    home_offset,
    dest_shard,
    dest_offset,
):
    n = lax.axis_size("dp")
    nt = lax.axis_size("tensor")
    kh = w_key.shape[1] // HEAD
    width = hidden.shape[1]
    blk = D // n
    tp = TILES // nt
    zs = n // 4
    half = HEAD // 2
    exponent = jnp.arange(half, dtype=F32) * (2.0 / HEAD)
    inverse = jnp.power(jnp.float32(ROPE_BASE), -exponent)
    freq = jnp.broadcast_to(jnp.concatenate([inverse, inverse])[None, :], (8, HEAD))
    dma = pltpu.SemaphoreType.DMA
    vmem = pl.BlockSpec(memory_space=pltpu.VMEM)
    smem = pl.BlockSpec(memory_space=pltpu.SMEM)
    anywhere = pl.BlockSpec(memory_space=pl.ANY)
    return pl.pallas_call(
        functools.partial(kernel, n, nt),
        out_shape=(
            jax.ShapeDtypeStruct((CAP, width), BF16),
            jax.ShapeDtypeStruct((TOK_DEV, width), BF16),
            jax.ShapeDtypeStruct((blk, kh * HEAD), F32),
        ),
        in_specs=[smem] * 4 + [vmem] * 4 + [anywhere] * 3,
        out_specs=(vmem, vmem, vmem),
        scratch_shapes=[
            pltpu.VMEM((kh, D, HEAD_COLS), BF16),
            pltpu.VMEM((TILES, TOK_DEV, TILE), BF16),
            pltpu.VMEM((TILES, 8, TILE), F32),
            pltpu.VMEM((TILES, TOK_DEV, TILE), BF16),
            pltpu.VMEM((n, TOK_DEV, blk), BF16),
            pltpu.VMEM((n, TOK_DEV, blk), BF16),
            pltpu.VMEM((4, MAXLEN, width), BF16),
            pltpu.VMEM((4, MAXLEN, width), BF16),
            pltpu.VMEM((kh, TOK_DEV, TILE), BF16),
            pltpu.VMEM((TOK_DEV, HEAD_COLS), F32),
            pltpu.VMEM((HEAD_COLS, TOK_DEV), BF16),
            pltpu.VMEM((TILES, TILE, TOK_DEV), F32),
            pltpu.VMEM((TILES, TOK_DEV, TILE), BF16),
            pltpu.VMEM((nt - 1, tp, TOK_DEV, TILE), BF16),
            pltpu.VMEM((TOK_DEV, HEAD), F32),
            pltpu.VMEM((nt - 1, TOK_DEV, HEAD), F32),
            pltpu.VMEM((kh, n * TOK_DEV, HEAD), BF16),
            pltpu.VMEM((kh, 4, MAXLEN, TILE), BF16),
            pltpu.VMEM((kh, 4, MAXLEN, TILE), BF16),
            pltpu.VMEM((blk, kh * HEAD), F32),
            dma((kh, 3)),
            dma((kh, 2, zs)),
            dma((kh, zs)),
            dma((kh, zs)),
            dma((kh, zs)),
            dma((kh, 2, zs)),
            dma((kh, 2, zs)),
            dma((kh, 2, zs)),
            dma((kh, zs)),
            dma((kh, zs)),
            dma((kh, zs)),
            dma((kh, 2, zs)),
            dma((kh, 2, zs)),
            dma((nt,)),
            dma((nt,)),
            dma((nt, 2)),
            dma((nt, 2)),
            dma((n,)),
            dma((n,)),
            dma((4,)),
            dma((4,)),
            dma((4,)),
            dma((4,)),
            dma((kh, 4)),
            dma((kh, 4)),
            dma((nt,)),
            dma((nt,)),
            dma((nt,)),
            dma((nt,)),
        ],
        compiler_params=pltpu.CompilerParams(
            collective_id=0, has_side_effects=True, vmem_limit_bytes=56 * 1024 * 1024
        ),
        cost_estimate=pl.CostEstimate(
            flops=8 * 10**9, bytes_accessed=8 * 10**6, transcendentals=10**6
        ),
    )(
        seq_length,
        home_offset,
        dest_shard,
        dest_offset,
        hidden,
        gain.astype(F32)[None, :],
        freq,
        cotangent,
        w_query,
        w_key,
        w_value,
    )


def on_split_device(
    hidden,
    gain,
    w_query,
    w_key,
    w_value,
    cotangent,
    seq_length,
    home_offset,
    dest_shard,
    dest_offset,
):
    n = lax.axis_size("dp")
    nt = lax.axis_size("tensor")
    kh = w_key.shape[1] // HEAD
    hh = kh // 2
    width = hidden.shape[1]
    blk = D // n
    tp = TILES // nt
    zs = n // 4
    half = HEAD // 2
    exponent = jnp.arange(half, dtype=F32) * (2.0 / HEAD)
    inverse = jnp.power(jnp.float32(ROPE_BASE), -exponent)
    freq = jnp.broadcast_to(jnp.concatenate([inverse, inverse])[None, :], (8, HEAD))
    dma = pltpu.SemaphoreType.DMA
    vmem = pl.BlockSpec(memory_space=pltpu.VMEM)
    smem = pl.BlockSpec(memory_space=pltpu.SMEM)
    anywhere = pl.BlockSpec(memory_space=pl.ANY)
    return pl.pallas_call(
        functools.partial(split_kernel, n, nt),
        out_shape=(
            jax.ShapeDtypeStruct((CAP, width), BF16),
            jax.ShapeDtypeStruct((TOK_DEV, width), BF16),
            jax.ShapeDtypeStruct((blk, kh * HEAD), F32),
        ),
        in_specs=[smem] * 4 + [vmem] * 4 + [anywhere] * 3,
        out_specs=(vmem, vmem, vmem),
        scratch_shapes=[
            pltpu.VMEM((hh, D, HEAD_COLS), BF16),
            pltpu.VMEM((TILES, TOK_DEV, TILE), BF16),
            pltpu.VMEM((TILES, 8, TILE), F32),
            pltpu.VMEM((2, TOK_DEV, HEAD), F32),
            pltpu.VMEM((2, TOK_DEV, HEAD), F32),
            pltpu.VMEM((2, GROUP * TOK_DEV, TOK_DEV), F32),
            pltpu.VMEM((hh, TOK_DEV, TILE), BF16),
            pltpu.VMEM((hh, TOK_DEV, TILE), BF16),
            pltpu.VMEM((hh, TOK_DEV, TILE), BF16),
            pltpu.VMEM((n, blk, TOK_DEV), BF16),
            pltpu.VMEM((n, blk, TOK_DEV), BF16),
            pltpu.VMEM((2, n, TOK_DEV, blk), BF16),
            pltpu.VMEM((n, TOK_DEV, blk), BF16),
            pltpu.VMEM((4, MAXLEN, width), BF16),
            pltpu.VMEM((4, MAXLEN, width), BF16),
            pltpu.VMEM((kh, TOK_DEV, TILE), BF16),
            pltpu.VMEM((2 * TOK_DEV, HEAD_COLS), F32),
            pltpu.VMEM((HEAD_COLS, 2 * TOK_DEV), BF16),
            pltpu.VMEM((n, blk, 2 * TOK_DEV), F32),
            pltpu.VMEM((TILES, TOK_DEV, TILE), BF16),
            pltpu.VMEM((nt - 1, tp, TOK_DEV, TILE), BF16),
            pltpu.VMEM((TOK_DEV, HEAD), F32),
            pltpu.VMEM((nt - 1, TOK_DEV, HEAD), F32),
            pltpu.VMEM((kh, n * TOK_DEV, HEAD), BF16),
            pltpu.VMEM((kh, 4, MAXLEN, TILE), BF16),
            pltpu.VMEM((kh, 4, MAXLEN, TILE), BF16),
            pltpu.VMEM((blk, kh * HEAD), F32),
            dma((kh, 3)),
            dma((kh, 2, zs)),
            dma((kh, zs)),
            dma((kh, max(zs, 3))),
            dma((kh, max(zs, 3))),
            dma((kh, 2, zs)),
            dma((kh, 2, zs)),
            dma((kh, 2, zs)),
            dma((kh, zs)),
            dma((kh, zs)),
            dma((kh, zs)),
            dma((kh, 2, zs)),
            dma((kh, 2, zs)),
            dma((nt,)),
            dma((nt,)),
            dma((hh,)),
            dma((hh,)),
            dma((2 + n // 4,)),
            dma((2 + n // 4,)),
            dma((nt, 2)),
            dma((nt, 2)),
            dma((n,)),
            dma((n,)),
            dma((4,)),
            dma((4,)),
            dma((4,)),
            dma((4,)),
            dma((kh, 4)),
            dma((kh, 4)),
            dma((nt,)),
            dma((nt,)),
            dma((nt,)),
            dma((nt,)),
        ],
        compiler_params=pltpu.CompilerParams(
            collective_id=1, has_side_effects=True, vmem_limit_bytes=56 * 1024 * 1024
        ),
        cost_estimate=pl.CostEstimate(
            flops=8 * 10**9, bytes_accessed=8 * 10**6, transcendentals=10**6
        ),
    )(
        seq_length,
        home_offset,
        dest_shard,
        dest_offset,
        hidden,
        gain.astype(F32)[None, :],
        freq,
        cotangent,
        w_query,
        w_key,
        w_value,
    )


def solution(mesh):
    def chosen(*arrays):
        heads = arrays[3].shape[1] // HEAD
        return (on_split_device if heads % 2 == 0 else on_device)(*arrays)

    return jax.shard_map(
        chosen,
        mesh=mesh,
        in_specs=(
            P("dp", "tensor"),
            P("tensor"),
            P("dp", "tensor"),
            P("dp", "tensor"),
            P("dp", "tensor"),
            P("dp", "tensor"),
            P(),
            P(),
            P(),
            P(),
        ),
        out_specs=(P("dp", "tensor"), P("dp", "tensor"), P("dp", "tensor")),
        check_vma=False,
    )
```
